128 devices in a mesh: dp: 8 (over y, z_lo), seq: 16 (over x, z_hi, core).
Axes of the slice: x: 4, y: 4, z: 4 (z_hi: 2, z_lo: 2; z = z_hi * 2 + z_lo), core: 2. Of those that a mesh axis runs over, the one named last changes fastest.
Arguments:
- query_space: bfloat16 [8, 4096, 1536], P('dp', 'seq'), may hold values from -40 to 40
- key_space: bfloat16 [8, 4096, 1536], P('dp', 'seq'), may hold values from -40 to 40
- value_space: bfloat16 [8, 4096, 1536], P('dp', 'seq'), may hold values from -6 to 6
- query_time: bfloat16 [8, 4096, 1536], P('dp', 'seq'), may hold values from -40 to 40
- key_time: bfloat16 [8, 4096, 1536], P('dp', 'seq'), may hold values from -40 to 40
- upstream: bfloat16 [8, 4096, 3072], P('dp', 'seq'), may hold values from -6 to 6
- out_weight: bfloat16 [1536, 3072], replicated, may hold values from -0.15625 to 0.15625
- tile_mask: int32 [16, 16], replicated, may hold values from 0 to 1, as said below
Outputs:
- query_space_grad: bfloat16 [8, 4096, 1536], P('dp', 'seq')
- key_space_grad: bfloat16 [8, 4096, 1536], P('dp', 'seq')
- value_space_grad: bfloat16 [8, 4096, 1536], P('dp', 'seq')
- query_time_grad: bfloat16 [8, 4096, 1536], P('dp', 'seq')
- key_time_grad: bfloat16 [8, 4096, 1536], P('dp', 'seq')
- weight_grad: float32 [1536, 3072], P('seq')
The draws below stay inside these ranges and needn't reach their ends.
Inputs may be any that keep to these rules, and one draw needn't show every extreme that they name: `tile_mask`: entry (i, i) is 1 for every tile i.
All inputs are finite; a program needn't handle non-finite values.
Results may differ from the reference program's by a relative error of at most 0.023.
Values may be sent and summed in bfloat16 or wider, within the bound.
A program may use at most 192 MiB of HBM per device.

```python
import math
import jax
import jax.numpy as jnp
from jax import lax

D = 3072
HEADS = 12
HD = 128
P_SIZE = 512
TILE = 32
HH = 1536
NT = 16
TOKENS = 4096
FRAMES = 8
VIDEOS = 8


def query_draw(key, stamp):
    key = jax.random.fold_in(key, stamp + 1)
    values = jnp.clip(jax.random.normal(key, (VIDEOS, TOKENS, HH), jnp.float32), -6.0, 6.0)
    return values.astype(jnp.bfloat16)


def key_draw(key, stamp):
    key = jax.random.fold_in(key, stamp + 2)
    values = jnp.clip(jax.random.normal(key, (VIDEOS, TOKENS, HH), jnp.float32), -6.0, 6.0)
    return values.astype(jnp.bfloat16)


def draw_query_space(key, part):
    return query_draw(key, 100)


def draw_key_space(key, part):
    return key_draw(key, 100)


def draw_query_time(key, part):
    return query_draw(key, 200)


def draw_key_time(key, part):
    return key_draw(key, 200)


def draw_tile_mask(key, part):
    key = jax.random.fold_in(key, 5)
    random_bits = jax.random.randint(key, (NT, NT), 0, 2)
    diagonal = jnp.arange(NT)[:, None] == jnp.arange(NT)[None, :]
    return jnp.where(diagonal, 1, random_bits).astype(jnp.int32)


def shard_levels(stream_key, shape, pieces, low, largest):
    loudness = 1.0
    for position, parts in pieces:
        heights = jax.random.uniform(jax.random.fold_in(jax.random.fold_in(stream_key, 6), position), (parts,), jnp.float32, low / len(pieces), largest / len(pieces))
        loudness = loudness * jnp.repeat(jnp.exp(heights), shape[position] // parts).reshape((-1,) + (1,) * (len(shape) - 1 - position))
    return loudness


def normal_values(rng, shape, deviation, most, shards=(), held_as=jnp.bfloat16):
    drawn = jax.random.normal(rng, shape, jnp.float32) * deviation
    if len(shards) > 0:
        drawn = shard_levels(rng, shape, shards, -0.22, 0.18) * drawn
    return jnp.clip(drawn, min=-most, max=most).astype(held_as)


def setup_inputs(seed: int = 0) -> dict:
    streams_of = jax.random.split(jax.random.key(seed), 9)
    return {
        "query_space": draw_query_space(jax.random.fold_in(streams_of[8], 71), 0),
        "key_space": draw_key_space(jax.random.fold_in(streams_of[8], 71), 0),
        "value_space": normal_values(streams_of[2], (VIDEOS, TOKENS, HH), 1.0, 6.0, ((0, 8), (1, 16))),
        "query_time": draw_query_time(jax.random.fold_in(streams_of[8], 71), 0),
        "key_time": draw_key_time(jax.random.fold_in(streams_of[8], 71), 0),
        "upstream": normal_values(streams_of[5], (VIDEOS, TOKENS, D), 1.0, 6.0, ((0, 8), (1, 16))),
        "out_weight": normal_values(streams_of[6], (HH, D), HH ** -0.5, 0.15625),
        "tile_mask": draw_tile_mask(jax.random.fold_in(streams_of[8], 71), 0),
    }


def masked_softmax(scores, allowed):
    highest = lax.optimization_barrier(jnp.max(jnp.where(allowed, scores, -jnp.inf), axis=-1, keepdims=True))
    powers = jnp.where(allowed, jnp.exp(scores - highest), 0.0)
    return powers / lax.optimization_barrier(jnp.sum(powers, axis=-1, keepdims=True))

def plain_softmax(scores):
    highest = lax.optimization_barrier(jnp.max(scores, axis=-1, keepdims=True))
    powers = jnp.exp(scores - highest)
    return powers / lax.optimization_barrier(jnp.sum(powers, axis=-1, keepdims=True))

def reference(query_space, key_space, value_space, query_time, key_time, upstream, out_weight, tile_mask):
    scale = 1.0 / math.sqrt(HD)
    dims = (FRAMES, P_SIZE, HEADS, HD)
    tiles = jnp.arange(P_SIZE) // TILE
    allowed = tile_mask[tiles][:, tiles] == 1
    f32 = jnp.float32
    b16 = jnp.bfloat16

    def one_video(carry, inputs):
        space_q, space_k, space_v, time_q, time_k, cot_up = inputs
        sq = space_q.reshape(dims).astype(f32)
        sk = space_k.reshape(dims).astype(f32)
        sv = space_v.reshape(dims).astype(f32)
        scores = jnp.einsum('fphd,fqhd->fhpq', sq, sk) * scale
        weights = masked_softmax(scores, allowed[None, None])
        weights_low = weights.astype(b16)
        space_out = jnp.einsum('fhpq,fqhd->fphd', weights_low.astype(f32), sv).astype(b16)
        tq = time_q.reshape(dims).astype(f32)
        tk = time_k.reshape(dims).astype(f32)
        time_scores = jnp.einsum('fphd,gphd->phfg', tq, tk) * scale
        time_weights = plain_softmax(time_scores)
        time_low = time_weights.astype(b16)
        time_out = jnp.einsum('phfg,gphd->fphd', time_low.astype(f32), space_out.astype(f32)).astype(b16)
        flat_out = time_out.reshape(TOKENS, HH)
        out_cot = lax.dot_general(cot_up, out_weight, (((1,), (1,)), ((), ())), preferred_element_type=f32).astype(b16)
        carry = carry + lax.dot_general(flat_out, cot_up, (((0,), (0,)), ((), ())), preferred_element_type=f32)
        tcot = out_cot.reshape(dims).astype(f32)
        prob_grad = jnp.einsum('fphd,gphd->phfg', tcot, space_out.astype(f32))
        centre = lax.optimization_barrier(jnp.sum(time_weights * prob_grad, axis=-1, keepdims=True))
        score_grad = (time_weights * (prob_grad - centre)).astype(b16).astype(f32)
        tq_grad = (jnp.einsum('phfg,gphd->fphd', score_grad, tk) * scale).astype(b16)
        tk_grad = (jnp.einsum('phfg,fphd->gphd', score_grad, tq) * scale).astype(b16)
        space_cot = jnp.einsum('phfg,fphd->gphd', time_low.astype(f32), tcot).astype(b16).astype(f32)
        prob_space = jnp.einsum('fphd,fqhd->fhpq', space_cot, sv)
        centre_space = lax.optimization_barrier(jnp.sum(weights * prob_space, axis=-1, keepdims=True))
        space_grad = (weights * (prob_space - centre_space)).astype(b16).astype(f32)
        sq_grad = (jnp.einsum('fhpq,fqhd->fphd', space_grad, sk) * scale).astype(b16)
        sk_grad = (jnp.einsum('fhpq,fphd->fqhd', space_grad, sq) * scale).astype(b16)
        sv_grad = jnp.einsum('fhpq,fphd->fqhd', weights_low.astype(f32), space_cot).astype(b16)
        shaped = tuple((item.reshape(TOKENS, HH) for item in (sq_grad, sk_grad, sv_grad, tq_grad, tk_grad)))
        return (carry, shaped)
    start = jnp.zeros((HH, D), jnp.float32)
    weight_grad, grads = lax.scan(one_video, start, (query_space, key_space, value_space, query_time, key_time, upstream))
    return (grads[0], grads[1], grads[2], grads[3], grads[4], weight_grad)
```

```python
import math

import jax
import jax.numpy as jnp
from jax import lax
from jax.experimental import pallas as pl
from jax.experimental.pallas import tpu as pltpu
from jax.sharding import PartitionSpec as P

HEADS = 12
HD = 128
HH = HEADS * HD
D = 3072
ROWS = 256
P_SIZE = 512
TILE = 32
NT = 16
FRAMES = 8
PIX = ROWS // FRAMES
HALF = PIX // 2
YS = 4
BLOCK = HH // YS
COLS = D // 8
OUT_ROWS = 96
GROUPS = 4
GH = HEADS // GROUPS
GC = GH * HD
WCH = 6
WROWS = HH // WCH
SCALE = 1.0 / math.sqrt(HD)
NEG = -1e30
MESH = pl.DeviceIdType.MESH
F32 = jnp.float32
B16 = jnp.bfloat16


def mm(a, b, ca, cb):
    return lax.dot_general(a, b, (((ca,), (cb,)), ((), ())), preferred_element_type=F32)


def kernel(
    qs, ks, vs, qt, kt, up, w, mask,
    sqg_o, skg_o, svg_o, tqg_o, tkg_o, wg_o,
    q_s, k_s, v_s, w_s, u_s, tq_r, tk_r, so_r, oc_r, sc_r, t_r,
    a_b, b_b, c_b, d_b, pw, tw, bias, tbias, tt, wgf, csend, crecv, rsend, rrecv, red,
    dk_f, dv_f, dk_x, dv_x, dk_r, dv_r, hop, t_f,
    ld, kv_ss, kv_rs, y_ss, y_rs, a2a_ss, a2a_rs, so_rs, sc_rs, t_rs, hop_ss, hop_rs,
    c_ss, c_rs, r_ss, r_rs, g_ss, g_rs, x_ss, x_rs, out_s,
):
    dp = lax.axis_index("dp")
    seq = lax.axis_index("seq")
    y, zl = dp // 2, dp % 2
    x, zh, core = seq // 4, (seq // 2) % 2, seq % 2
    frame = x * 2 + zh

    def dev(x_, y_, zh_, zl_, c_):
        return {"dp": y_ * 2 + zl_, "seq": x_ * 4 + zh_ * 2 + c_}

    def send(src, dst, ss, rs, to):
        pltpu.make_async_remote_copy(
            src_ref=src, dst_ref=dst, send_sem=ss, recv_sem=rs, device_id=to, device_id_type=MESH
        ).start()

    def await_bytes(ref, sem):
        pltpu.make_async_copy(ref, ref, sem).wait()

    def local(src, dst, sem):
        pltpu.make_async_copy(src, dst, sem).start()

    def rows(start, size):
        return pl.ds(pl.multiple_of(start, size), size)

    def spread(src, cols, put, unit, part):
        for zd in range(2):
            for side in range(2):
                far = ((x + 2) % 4 * 2 + zd) * PIX + side * HALF
                send(
                    src.at[rows(far, HALF), cols],
                    hop.at[unit, rows(side * PIX + zh * HALF, HALF), cols],
                    a2a_ss.at[unit], hop_rs.at[unit, part],
                    dev((x + 1 + 2 * side) % 4, y, zd, 1 - zl, core),
                )
        for step in (1, 3, 0):
            xd = (x + step) % 4
            for zd in range(2):
                put(
                    src, rows((xd * 2 + zd) * PIX, PIX), frame * PIX, PIX, a2a_ss.at[unit],
                    xd, zd, 1 - zl,
                )

    def forward(cols, put, unit, part):
        await_bytes(hop.at[unit, :, cols], hop_rs.at[unit, part])
        for side in range(2):
            came = (x + 3 + 2 * side) % 4
            for zs in range(2):
                put(
                    hop.at[unit], pl.ds(side * PIX + zs * HALF, HALF),
                    (came * 2 + zs) * PIX + side * HALF, HALF, hop_ss.at[unit],
                    (x + 1 + 2 * side) % 4, zh, zl,
                )

    def putter(dst, cols, rs):
        def put(src, src_rows, start, size, ss, xd, zd, zld):
            send(
                src.at[src_rows, cols], dst.at[rows(start, size), cols], ss, rs,
                dev(xd, y, zd, zld, core),
            )

        return put

    whole = pl.ds(0, HH)
    group_cols = [pl.ds(g * GC, GC) for g in range(GROUPS)]
    put_tq = putter(tq_r, whole, a2a_rs.at[0])
    put_tk = putter(tk_r, whole, a2a_rs.at[1])
    put_oc = putter(oc_r, whole, a2a_rs.at[2])
    put_so = [putter(so_r, group_cols[g], so_rs.at[g]) for g in range(GROUPS)]
    put_sc = [putter(sc_r, group_cols[g], sc_rs.at[g]) for g in range(GROUPS)]
    put_tqg = putter(tqg_o.at[0], whole, a2a_rs.at[5])
    put_tkg = putter(tkg_o.at[0], whole, a2a_rs.at[6])

    def put_out(src, src_rows, start, size, ss, xd, zd, zld):
        for k in range(YS):
            yd = (y + k) % YS
            send(
                src.at[src_rows, rows(yd * BLOCK, BLOCK)], t_r.at[rows(y * ROWS + start, size)],
                ss, t_rs, dev(xd, yd, zd, zld, core),
            )

    other = dev(x, y, zh, zl, 1 - core)
    y_up = dev(x, (y + 1) % YS, zh, zl, core)
    y_dn = dev(x, (y + 3) % YS, zh, zl, core)

    send(ks.at[0], k_s.at[pl.ds(ROWS, ROWS)], kv_ss.at[0], kv_rs.at[0], other)
    send(vs.at[0], v_s.at[pl.ds(ROWS, ROWS)], kv_ss.at[1], kv_rs.at[1], other)
    local(up.at[0], u_s.at[pl.ds(pl.multiple_of(y * ROWS, ROWS), ROWS)], ld.at[0])
    for i in range(WCH):
        local(w.at[pl.ds(i * WROWS, WROWS)], w_s.at[pl.ds(i * WROWS, WROWS)], ld.at[4 + i])
    local(qs.at[0], q_s, ld.at[1])
    local(ks.at[0], k_s.at[pl.ds(0, ROWS)], ld.at[2])
    local(vs.at[0], v_s.at[pl.ds(0, ROWS)], ld.at[3])
    half = ROWS // 2

    def u_half(owner, part):
        return u_s.at[pl.ds(pl.multiple_of(owner * ROWS + part * half, half), half)]

    send(up.at[0, pl.ds(0, half)], u_half(y, 0), y_ss.at[0], y_rs.at[0], y_up)
    send(up.at[0, pl.ds(half, half)], u_half(y, 1), y_ss.at[1], y_rs.at[1], y_dn)

    spread(qt.at[0], whole, put_tq, 0, 0)
    spread(kt.at[0], whole, put_tk, 1, 0)
    send(up.at[0, pl.ds(0, half)], u_half(y, 0), y_ss.at[2], y_rs.at[2], y_dn)
    send(up.at[0, pl.ds(half, half)], u_half(y, 1), y_ss.at[3], y_rs.at[3], y_up)

    key_row = lax.broadcasted_iota(jnp.int32, (P_SIZE, NT), 0)
    key_tile = jnp.where(
        key_row < ROWS, core * (NT // 2) + key_row // TILE,
        (1 - core) * (NT // 2) + (key_row - ROWS) // TILE,
    )
    key_hot = (key_tile == lax.broadcasted_iota(jnp.int32, (P_SIZE, NT), 1)).astype(F32)
    query_tile = core * (NT // 2) + lax.broadcasted_iota(jnp.int32, (ROWS, NT), 0) // TILE
    query_hot = (query_tile == lax.broadcasted_iota(jnp.int32, (ROWS, NT), 1)).astype(F32)
    rows_mask = mm(query_hot, mask[...].astype(F32), 1, 0)
    bias[...] = jnp.where(mm(key_hot, rows_mask, 1, 1) > 0.5, 0.0, NEG)
    same = (
        lax.broadcasted_iota(jnp.int32, (ROWS, ROWS), 0) % PIX
        == lax.broadcasted_iota(jnp.int32, (ROWS, ROWS), 1) % PIX
    )
    tbias[...] = jnp.where(same, 0.0, NEG)

    own_u = pl.ds(pl.multiple_of(y * ROWS, ROWS), ROWS)
    await_bytes(up.at[0], ld.at[0])

    for i in range(WCH):
        await_bytes(w_s.at[pl.ds(i * WROWS, WROWS)], ld.at[4 + i])
        c_b[:, pl.ds(i * WROWS, WROWS)] = mm(
            u_s[own_u, :], w_s[pl.ds(i * WROWS, WROWS), :], 1, 1
        ).astype(B16)

    forward(whole, put_tq, 0, 0)
    forward(whole, put_tk, 1, 0)

    await_bytes(q_s, ld.at[1])
    await_bytes(k_s.at[pl.ds(0, ROWS)], ld.at[2])
    await_bytes(v_s.at[pl.ds(0, ROWS)], ld.at[3])
    await_bytes(k_s.at[pl.ds(ROWS, ROWS)], kv_rs.at[0])
    await_bytes(v_s.at[pl.ds(ROWS, ROWS)], kv_rs.at[1])

    def space_forward(h, carry):
        hs = pl.ds(pl.multiple_of(h * HD, HD), HD)
        scores = mm(k_s[:, hs], q_s[:, hs], 1, 1) * SCALE + bias[...]
        powers = jnp.exp(scores - jnp.max(scores, axis=0, keepdims=True))
        weights = powers / jnp.sum(powers, axis=0, keepdims=True)
        pw[h] = weights
        a_b[:, hs] = mm(weights.astype(B16), v_s[:, hs], 0, 0).astype(B16)
        return carry

    for g in range(GROUPS):
        lax.fori_loop(g * GH, (g + 1) * GH, space_forward, 0)

        spread(a_b, group_cols[g], put_so[g], 3, g)

    spread(c_b, whole, put_oc, 2, 0)

    await_bytes(tq_r, a2a_rs.at[0])
    await_bytes(tk_r, a2a_rs.at[1])

    def time_forward(h, carry):
        hs = pl.ds(pl.multiple_of(h * HD, HD), HD)
        scores = mm(tk_r[:, hs], tq_r[:, hs], 1, 1) * SCALE + tbias[...]
        powers = jnp.exp(scores - jnp.max(scores, axis=0, keepdims=True))
        weights = powers / jnp.sum(powers, axis=0, keepdims=True)
        tw[h] = weights
        return carry

    lax.fori_loop(0, HEADS, time_forward, 0)
    for g in range(GROUPS):
        forward(group_cols[g], put_so[g], 3, g)

    y_m, y_p = (y + 3) % YS, (y + 1) % YS
    await_bytes(u_half(y_m, 0), y_rs.at[0])
    send(u_half(y_m, 0), u_half(y_m, 0), y_ss.at[4], y_rs.at[4], y_up)
    await_bytes(u_half(y_p, 1), y_rs.at[1])
    send(u_half(y_p, 1), u_half(y_p, 1), y_ss.at[5], y_rs.at[5], y_dn)

    for g in range(GROUPS):
        await_bytes(so_r.at[:, group_cols[g]], so_rs.at[g])
        heads = [
            mm(tw[h].astype(B16), so_r[:, h * HD:(h + 1) * HD], 0, 0)
            for h in range(g * GH, (g + 1) * GH)
        ]
        t_f[g] = jnp.concatenate(heads, axis=1)
    for k in range(YS):
        block = [t_f[g, :, k * OUT_ROWS:(k + 1) * OUT_ROWS] for g in range(GROUPS)]
        b_b[:, k * BLOCK:(k + 1) * BLOCK] = jnp.concatenate(block, axis=1).astype(B16)

    spread(b_b, whole, put_out, 7, 0)
    forward(whole, put_oc, 2, 0)

    await_bytes(oc_r, a2a_rs.at[2])
    await_bytes(c_b, a2a_ss.at[2])
    await_bytes(a_b, a2a_ss.at[3])

    def time_backward(h, carry):
        hs = pl.ds(pl.multiple_of(h * HD, HD), HD)
        weights = tw[h]
        cot = oc_r[:, hs]
        c_b[:, hs] = mm(weights.astype(B16), cot, 1, 0).astype(B16)
        prob = mm(so_r[:, hs], cot, 1, 1)
        centre = jnp.sum(weights * prob, axis=0, keepdims=True)
        grad = (weights * (prob - centre)).astype(B16)
        a_b[:, hs] = (mm(grad, tk_r[:, hs], 0, 0) * SCALE).astype(B16)
        d_b[:, hs] = (mm(grad, tq_r[:, hs], 1, 0) * SCALE).astype(B16)
        return carry

    for g in range(GROUPS):
        lax.fori_loop(g * GH, (g + 1) * GH, time_backward, 0)

        spread(c_b, group_cols[g], put_sc[g], 4, g)
        if g == 0:
            forward(whole, put_out, 7, 0)
        else:
            forward(group_cols[g - 1], put_sc[g - 1], 4, g - 1)

    forward(group_cols[GROUPS - 1], put_sc[GROUPS - 1], 4, GROUPS - 1)

    await_bytes(t_r, t_rs)
    tt[...] = t_r[...].T
    await_bytes(u_half(y_m, 1), y_rs.at[3])
    await_bytes(u_half(y_p, 0), y_rs.at[2])
    y_f = (y + 2) % YS
    await_bytes(u_half(y_f, 0), y_rs.at[4])
    await_bytes(u_half(y_f, 1), y_rs.at[5])

    def weight_part(chunk):
        return mm(tt[...], u_s[:, rows(chunk * COLS, COLS)], 1, 0)

    def pair_sum(i):
        await_bytes(crecv.at[i], c_rs.at[i])
        rsend[i] = (wgf[i] + crecv[i].astype(F32)).astype(B16)
        slot = rrecv.at[x * 4 + zh * 2 + zl]
        for k in range(4):
            xd = (x + k) % 4
            piece = rsend.at[i, rows(xd * OUT_ROWS, OUT_ROWS)]
            if k > 0:
                send(piece, slot, r_ss.at[k], r_rs, dev(xd, y, i // 2, i % 2, core))
            else:
                mine = zh * 2 + zl == i

                @pl.when(mine)
                def _():
                    local(piece, slot, r_rs)

                @pl.when(jnp.logical_not(mine))
                def _():
                    send(piece, slot, r_ss.at[0], r_rs, dev(xd, y, i // 2, i % 2, core))

    for i in range(4):
        csend[i] = weight_part(2 * i + 1 - core).astype(B16)
        send(csend.at[i], crecv.at[i], c_ss, c_rs.at[i], other)
        wgf[i] = weight_part(2 * i + core)
        if i > 0:
            pair_sum(i - 1)
    pair_sum(3)
    spread(a_b, whole, put_tqg, 5, 0)
    spread(d_b, whole, put_tkg, 6, 0)
    await_bytes(b_b, a2a_ss.at[7])

    def space_backward(h, carry):
        hs = pl.ds(pl.multiple_of(h * HD, HD), HD)
        weights = pw[h]
        cot = sc_r[:, hs]
        key = k_s[:, hs]
        prob = mm(v_s[:, hs], cot, 1, 1)
        centre = jnp.sum(weights * prob, axis=0, keepdims=True)
        grad = (weights * (prob - centre)).astype(B16)
        b_b[:, hs] = (mm(grad, key, 0, 0) * SCALE).astype(B16)
        dk = mm(grad, q_s[:, hs], 1, 0) * SCALE
        dv = mm(weights.astype(B16), cot, 1, 0)
        dk_f[:, hs] = dk[:ROWS]
        dv_f[:, hs] = dv[:ROWS]
        dk_x[:, hs] = dk[ROWS:].astype(B16)
        dv_x[:, hs] = dv[ROWS:].astype(B16)
        return carry

    def backward_group(g):
        cols = pl.ds(g * GC, GC)
        await_bytes(sc_r.at[:, cols], sc_rs.at[g])
        lax.fori_loop(g * GH, (g + 1) * GH, space_backward, 0)
        send(dk_x.at[:, cols], dk_r.at[:, cols], x_ss, x_rs.at[0, g], other)
        send(dv_x.at[:, cols], dv_r.at[:, cols], x_ss, x_rs.at[1, g], other)

    for g in range(GROUPS):
        backward_group(g)
        if g == 0:
            forward(whole, put_tqg, 5, 0)
            forward(whole, put_tkg, 6, 0)

    await_bytes(rrecv, r_rs)
    total = rrecv[0].astype(F32)
    for k in range(1, 16):
        total = total + rrecv[k].astype(F32)
    red[...] = total.astype(B16)
    out_cols = rows(((zh * 2 + zl) * 2 + core) * COLS, COLS)
    zh_own, core_own = y // 2, y % 2
    for k in range(8):
        yd, zld = (y + k // 2) % YS, (zl + k) % 2
        mine = (yd == y) & (zh_own == zh) & (zld == zl) & (core_own == core)

        @pl.when(mine)
        def _():
            local(red, wg_o.at[:, out_cols], g_rs)

        @pl.when(jnp.logical_not(mine))
        def _():
            send(red, wg_o.at[:, out_cols], g_ss.at[k], g_rs, dev(x, yd, zh_own, zld, core_own))

    local(b_b, sqg_o.at[0], out_s.at[0])
    for g in range(GROUPS):
        cols = pl.ds(g * GC, GC)
        await_bytes(dk_r.at[:, cols], x_rs.at[0, g])
        await_bytes(dv_r.at[:, cols], x_rs.at[1, g])
    await_bytes(dk_x, x_ss)
    await_bytes(dv_x, x_ss)
    dk_x[...] = (dk_f[...] + dk_r[...].astype(F32)).astype(B16)
    local(dk_x, skg_o.at[0], out_s.at[1])
    dv_x[...] = (dv_f[...] + dv_r[...].astype(F32)).astype(B16)
    local(dv_x, svg_o.at[0], out_s.at[2])

    await_bytes(ks.at[0], kv_ss.at[0])
    await_bytes(vs.at[0], kv_ss.at[1])
    for i in range(6):
        await_bytes(u_half(0, 0), y_ss.at[i])
    await_bytes(qt.at[0], a2a_ss.at[0])
    await_bytes(kt.at[0], a2a_ss.at[1])
    await_bytes(c_b, a2a_ss.at[4])
    await_bytes(a_b, a2a_ss.at[5])
    await_bytes(d_b, a2a_ss.at[6])
    for unit in range(8):
        await_bytes(hop.at[unit], hop_ss.at[unit])
    await_bytes(csend, c_ss)
    for k in range(1, 4):
        await_bytes(rsend.at[0], r_ss.at[k])
    await_bytes(rsend.at[0, pl.ds(0, 3 * OUT_ROWS)], r_ss.at[0])
    for k in range(8):
        yd, zld = (y + k // 2) % YS, (zl + k) % 2
        mine = (yd == y) & (zh_own == zh) & (zld == zl) & (core_own == core)

        @pl.when(jnp.logical_not(mine))
        def _():
            await_bytes(red, g_ss.at[k])

    await_bytes(tqg_o.at[0], a2a_rs.at[5])
    await_bytes(tkg_o.at[0], a2a_rs.at[6])
    await_bytes(wg_o, g_rs)
    await_bytes(b_b, out_s.at[0])
    await_bytes(dk_x, out_s.at[1])
    await_bytes(dv_x, out_s.at[2])


def local(qs, ks, vs, qt, kt, up, w, mask):
    hbm = pl.BlockSpec(memory_space=pl.ANY)
    vm = pltpu.VMEM
    dma = pltpu.SemaphoreType.DMA
    unit = jax.ShapeDtypeStruct((1, ROWS, HH), B16)
    own = vm((ROWS, HH), B16)
    outs = pl.pallas_call(
        kernel,
        out_shape=(unit,) * 5 + (jax.ShapeDtypeStruct((OUT_ROWS, D), B16),),
        in_specs=[hbm] * 7 + [pl.BlockSpec(memory_space=pltpu.VMEM)],
        out_specs=(hbm,) * 6,
        scratch_shapes=[
            own, vm((P_SIZE, HH), B16), vm((P_SIZE, HH), B16), vm((HH, D), B16),
            vm((YS * ROWS, D), B16), own, own, own, own, own, vm((YS * ROWS, BLOCK), B16),
            own, own, own, own,
            vm((HEADS, P_SIZE, ROWS), F32), vm((HEADS, ROWS, ROWS), F32),
            vm((P_SIZE, ROWS), F32), vm((ROWS, ROWS), F32),
            vm((BLOCK, YS * ROWS), B16), vm((4, BLOCK, COLS), F32),
            vm((4, BLOCK, COLS), B16), vm((4, BLOCK, COLS), B16),
            vm((4, BLOCK, COLS), B16), vm((16, OUT_ROWS, COLS), B16), vm((OUT_ROWS, COLS), B16),
            vm((ROWS, HH), F32), vm((ROWS, HH), F32), own, own, own, own,
            vm((8, 2 * PIX, HH), B16), vm((GROUPS, ROWS, GC), F32),
            dma((4 + WCH,)), dma((2,)), dma((2,)), dma((6,)), dma((6,)), dma((8,)), dma((7,)),
            dma((GROUPS,)), dma((GROUPS,)), dma, dma((8,)), dma((8, GROUPS)), dma, dma((4,)), dma((4,)), dma,
            dma((8,)), dma, dma, dma((2, GROUPS)), dma((3,)),
        ],
        compiler_params=pltpu.CompilerParams(
            has_side_effects=True, vmem_limit_bytes=62 * 1024 * 1024
        ),
        cost_estimate=pl.CostEstimate(
            flops=8 * 10**9, bytes_accessed=20 * 10**6, transcendentals=3 * 10**6
        ),
    )(qs, ks, vs, qt, kt, up, w, mask)
    return outs[:5] + (outs[5].astype(F32),)


def solution(mesh):
    tokens = P("dp", "seq", None)
    return jax.shard_map(
        local,
        mesh=mesh,
        in_specs=(tokens,) * 6 + (P(), P()),
        out_specs=(tokens,) * 5 + (P("seq", None),),
        check_vma=False,
    )
```

```python
import math

import jax
import jax.numpy as jnp
from jax import lax
from jax.experimental import pallas as pl
from jax.experimental.pallas import tpu as pltpu
from jax.sharding import PartitionSpec as P

HEADS = 12
HD = 128
HH = HEADS * HD
D = 3072
ROWS = 256
P_SIZE = 512
TILE = 32
NT = 16
FRAMES = 8
PIX = ROWS // FRAMES
HALF = PIX // 2
YS = 4
BLOCK = HH // YS
COLS = D // 8
OUT_ROWS = 96
GROUPS = 4
GH = HEADS // GROUPS
GC = GH * HD
WCH = 6
WROWS = HH // WCH
SCALE = 1.0 / math.sqrt(HD)
NEG = -1e30
MESH = pl.DeviceIdType.MESH
F32 = jnp.float32
B16 = jnp.bfloat16


def mm(a, b, ca, cb):
    return lax.dot_general(a, b, (((ca,), (cb,)), ((), ())), preferred_element_type=F32)


def kernel(
    qs, ks, vs, qt, kt, up, w, mask,
    sqg_o, skg_o, svg_o, tqg_o, tkg_o, wg_o,
    q_s, k_s, v_s, w_s, u_s, tq_r, tk_r, so_r, oc_r, sc_r, t_r,
    a_b, b_b, c_b, d_b, pw, tw, bias, tbias, tt, wgf, csend, crecv, rsend, rrecv, red,
    dk_f, dv_f, dk_x, dv_x, dk_r, dv_r, hop, t_f, tqg_r, tkg_r, g_r,
    ld, kv_ss, kv_rs, y_ss, y_rs, a2a_ss, a2a_rs, so_rs, sc_rs, t_rs, hop_ss, hop_rs,
    c_ss, c_rs, r_ss, r_rs, g_ss, g_rs, x_ss, x_rs, out_s,
):
    dp = lax.axis_index("dp")
    seq = lax.axis_index("seq")
    y, zl = dp // 2, dp % 2
    x, zh, core = seq // 4, (seq // 2) % 2, seq % 2
    frame = x * 2 + zh

    def dev(x_, y_, zh_, zl_, c_):
        return {"dp": y_ * 2 + zl_, "seq": x_ * 4 + zh_ * 2 + c_}

    def send(src, dst, ss, rs, to):
        pltpu.make_async_remote_copy(
            src_ref=src, dst_ref=dst, send_sem=ss, recv_sem=rs, device_id=to, device_id_type=MESH
        ).start()

    def await_bytes(ref, sem):
        pltpu.make_async_copy(ref, ref, sem).wait()

    def local(src, dst, sem):
        pltpu.make_async_copy(src, dst, sem).start()

    def rows(start, size):
        return pl.ds(pl.multiple_of(start, size), size)

    def spread(src, cols, put, unit, part):
        for zd in range(2):
            for side in range(2):
                far = ((x + 2) % 4 * 2 + zd) * PIX + side * HALF
                send(
                    src.at[rows(far, HALF), cols],
                    hop.at[unit, rows(side * PIX + zh * HALF, HALF), cols],
                    a2a_ss.at[unit], hop_rs.at[unit, part],
                    dev((x + 1 + 2 * side) % 4, y, zd, 1 - zl, core),
                )
        for step in (1, 3, 0):
            xd = (x + step) % 4
            for zd in range(2):
                put(
                    src, rows((xd * 2 + zd) * PIX, PIX), frame * PIX, PIX, a2a_ss.at[unit],
                    xd, zd, 1 - zl,
                )

    def forward(cols, put, unit, part):
        await_bytes(hop.at[unit, :, cols], hop_rs.at[unit, part])
        for side in range(2):
            came = (x + 3 + 2 * side) % 4
            for zs in range(2):
                put(
                    hop.at[unit], pl.ds(side * PIX + zs * HALF, HALF),
                    (came * 2 + zs) * PIX + side * HALF, HALF, hop_ss.at[unit],
                    (x + 1 + 2 * side) % 4, zh, zl,
                )

    def putter(dst, cols, rs):
        def put(src, src_rows, start, size, ss, xd, zd, zld):
            send(
                src.at[src_rows, cols], dst.at[rows(start, size), cols], ss, rs,
                dev(xd, y, zd, zld, core),
            )

        return put

    whole = pl.ds(0, HH)
    group_cols = [pl.ds(g * GC, GC) for g in range(GROUPS)]
    put_tq = putter(tq_r, whole, a2a_rs.at[0])
    put_tk = putter(tk_r, whole, a2a_rs.at[1])
    put_oc = putter(oc_r, whole, a2a_rs.at[2])
    put_so = [putter(so_r, group_cols[g], so_rs.at[g]) for g in range(GROUPS)]
    put_sc = [putter(sc_r, group_cols[g], sc_rs.at[g]) for g in range(GROUPS)]
    put_tqg = putter(tqg_r, whole, a2a_rs.at[5])
    put_tkg = putter(tkg_r, whole, a2a_rs.at[6])

    def put_out(src, src_rows, start, size, ss, xd, zd, zld):
        for k in range(YS):
            yd = (y + k) % YS
            send(
                src.at[src_rows, rows(yd * BLOCK, BLOCK)], t_r.at[rows(y * ROWS + start, size)],
                ss, t_rs, dev(xd, yd, zd, zld, core),
            )

    other = dev(x, y, zh, zl, 1 - core)
    y_up = dev(x, (y + 1) % YS, zh, zl, core)
    y_dn = dev(x, (y + 3) % YS, zh, zl, core)

    half = ROWS // 2
    own_k, far_k = pl.ds(0, ROWS), pl.ds(ROWS, ROWS)
    own_u = pl.ds(pl.multiple_of(y * ROWS, ROWS), ROWS)

    def u_half(owner, part):
        return u_s.at[pl.ds(pl.multiple_of(owner * ROWS + part * half, half), half)]

    loads = (
        (ks.at[0], k_s.at[own_k]), (vs.at[0], v_s.at[own_k]), (qt.at[0], b_b), (kt.at[0], d_b),
        (up.at[0], u_s.at[own_u]), (qs.at[0], q_s),
    )
    for i, (src, dst) in enumerate(loads):
        local(src, dst, ld.at[i])
    for i in range(WCH):
        local(w.at[pl.ds(i * WROWS, WROWS)], w_s.at[pl.ds(i * WROWS, WROWS)], ld.at[6 + i])

    await_bytes(k_s.at[own_k], ld.at[0])
    send(k_s.at[own_k], k_s.at[far_k], kv_ss.at[0], kv_rs.at[0], other)
    await_bytes(v_s.at[own_k], ld.at[1])
    send(v_s.at[own_k], v_s.at[far_k], kv_ss.at[1], kv_rs.at[1], other)
    await_bytes(b_b, ld.at[2])
    spread(b_b, whole, put_tq, 0, 0)
    await_bytes(u_s.at[own_u], ld.at[4])
    send(u_half(y, 0), u_half(y, 0), y_ss.at[0], y_rs.at[0], y_up)
    send(u_half(y, 1), u_half(y, 1), y_ss.at[1], y_rs.at[1], y_dn)
    await_bytes(d_b, ld.at[3])
    spread(d_b, whole, put_tk, 1, 0)
    send(u_half(y, 0), u_half(y, 0), y_ss.at[2], y_rs.at[2], y_dn)
    send(u_half(y, 1), u_half(y, 1), y_ss.at[3], y_rs.at[3], y_up)

    key_row = lax.broadcasted_iota(jnp.int32, (P_SIZE, NT), 0)
    key_tile = jnp.where(
        key_row < ROWS, core * (NT // 2) + key_row // TILE,
        (1 - core) * (NT // 2) + (key_row - ROWS) // TILE,
    )
    key_hot = (key_tile == lax.broadcasted_iota(jnp.int32, (P_SIZE, NT), 1)).astype(F32)
    query_tile = core * (NT // 2) + lax.broadcasted_iota(jnp.int32, (ROWS, NT), 0) // TILE
    query_hot = (query_tile == lax.broadcasted_iota(jnp.int32, (ROWS, NT), 1)).astype(F32)
    rows_mask = mm(query_hot, mask[...].astype(F32), 1, 0)
    bias[...] = jnp.where(mm(key_hot, rows_mask, 1, 1) > 0.5, 0.0, NEG)
    same = (
        lax.broadcasted_iota(jnp.int32, (ROWS, ROWS), 0) % PIX
        == lax.broadcasted_iota(jnp.int32, (ROWS, ROWS), 1) % PIX
    )
    tbias[...] = jnp.where(same, 0.0, NEG)

    for i in range(WCH):
        await_bytes(w_s.at[pl.ds(i * WROWS, WROWS)], ld.at[6 + i])
        c_b[:, pl.ds(i * WROWS, WROWS)] = mm(
            u_s[own_u, :], w_s[pl.ds(i * WROWS, WROWS), :], 1, 1
        ).astype(B16)

    await_bytes(q_s, ld.at[5])
    await_bytes(k_s.at[far_k], kv_rs.at[0])
    await_bytes(v_s.at[far_k], kv_rs.at[1])

    def space_forward(h):
        hs = pl.ds(h * HD, HD)
        scores = mm(k_s[:, hs], q_s[:, hs], 1, 1) * SCALE + bias[...]
        powers = jnp.exp(scores - jnp.max(scores, axis=0, keepdims=True))
        weights = powers * (1.0 / jnp.sum(powers, axis=0, keepdims=True))
        pw[h] = weights
        a_b[:, hs] = mm(weights.astype(B16), v_s[:, hs], 0, 0).astype(B16)

    for g in range(GROUPS):
        for h in range(g * GH, (g + 1) * GH):
            space_forward(h)
        spread(a_b, group_cols[g], put_so[g], 3, g)
        if g == 1:
            forward(whole, put_tq, 0, 0)
        if g == 3:
            forward(whole, put_tk, 1, 0)

    spread(c_b, whole, put_oc, 2, 0)

    await_bytes(tq_r, a2a_rs.at[0])
    await_bytes(tk_r, a2a_rs.at[1])

    def time_forward(h):
        hs = pl.ds(h * HD, HD)
        scores = mm(tk_r[:, hs], tq_r[:, hs], 1, 1) * SCALE + tbias[...]
        powers = jnp.exp(scores - jnp.max(scores, axis=0, keepdims=True))
        weights = powers * (1.0 / jnp.sum(powers, axis=0, keepdims=True))
        tw[h] = weights

    for h in range(HEADS):
        time_forward(h)
    for g in range(GROUPS):
        forward(group_cols[g], put_so[g], 3, g)

    y_m, y_p = (y + 3) % YS, (y + 1) % YS
    await_bytes(u_half(y_m, 0), y_rs.at[0])
    send(u_half(y_m, 0), u_half(y_m, 0), y_ss.at[4], y_rs.at[4], y_up)
    await_bytes(u_half(y_p, 1), y_rs.at[1])
    send(u_half(y_p, 1), u_half(y_p, 1), y_ss.at[5], y_rs.at[5], y_dn)

    await_bytes(b_b, a2a_ss.at[0])
    for g in range(GROUPS):
        await_bytes(so_r.at[:, group_cols[g]], so_rs.at[g])
        heads = [
            mm(tw[h].astype(B16), so_r[:, h * HD:(h + 1) * HD], 0, 0)
            for h in range(g * GH, (g + 1) * GH)
        ]
        t_f[g] = jnp.concatenate(heads, axis=1)
    for k in range(YS):
        block = [t_f[g, :, k * OUT_ROWS:(k + 1) * OUT_ROWS] for g in range(GROUPS)]
        b_b[:, k * BLOCK:(k + 1) * BLOCK] = jnp.concatenate(block, axis=1).astype(B16)

    spread(b_b, whole, put_out, 7, 0)
    forward(whole, put_oc, 2, 0)

    await_bytes(oc_r, a2a_rs.at[2])
    await_bytes(c_b, a2a_ss.at[2])
    await_bytes(a_b, a2a_ss.at[3])
    await_bytes(d_b, a2a_ss.at[1])

    def time_backward(h):
        hs = pl.ds(h * HD, HD)
        weights = tw[h]
        cot = oc_r[:, hs]
        c_b[:, hs] = mm(weights.astype(B16), cot, 1, 0).astype(B16)
        prob = mm(so_r[:, hs], cot, 1, 1)
        centre = jnp.sum(weights * prob, axis=0, keepdims=True)
        grad = (weights * (prob - centre)).astype(B16)
        a_b[:, hs] = (mm(grad, tk_r[:, hs], 0, 0) * SCALE).astype(B16)
        d_b[:, hs] = (mm(grad, tq_r[:, hs], 1, 0) * SCALE).astype(B16)

    for g in range(GROUPS):
        for h in range(g * GH, (g + 1) * GH):
            time_backward(h)
        spread(c_b, group_cols[g], put_sc[g], 4, g)
        if g == 0:
            forward(whole, put_out, 7, 0)
        else:
            forward(group_cols[g - 1], put_sc[g - 1], 4, g - 1)

    spread(a_b, whole, put_tqg, 5, 0)
    spread(d_b, whole, put_tkg, 6, 0)
    forward(group_cols[GROUPS - 1], put_sc[GROUPS - 1], 4, GROUPS - 1)

    await_bytes(b_b, a2a_ss.at[7])

    def space_backward(h):
        hs = pl.ds(h * HD, HD)
        weights = pw[h]
        cot = sc_r[:, hs]
        key = k_s[:, hs]
        prob = mm(v_s[:, hs], cot, 1, 1)
        centre = jnp.sum(weights * prob, axis=0, keepdims=True)
        grad = (weights * (prob - centre)).astype(B16)
        b_b[:, hs] = (mm(grad, key, 0, 0) * SCALE).astype(B16)
        dk = mm(grad, q_s[:, hs], 1, 0) * SCALE
        dv = mm(weights.astype(B16), cot, 1, 0)
        dk_f[:, hs] = dk[:ROWS]
        dv_f[:, hs] = dv[:ROWS]
        dk_x[:, hs] = dk[ROWS:].astype(B16)
        dv_x[:, hs] = dv[ROWS:].astype(B16)

    def backward_group(g):
        cols = pl.ds(g * GC, GC)
        await_bytes(sc_r.at[:, cols], sc_rs.at[g])
        for h in range(g * GH, (g + 1) * GH):
            space_backward(h)
        send(dk_x.at[:, cols], dk_r.at[:, cols], x_ss, x_rs.at[0, g], other)
        send(dv_x.at[:, cols], dv_r.at[:, cols], x_ss, x_rs.at[1, g], other)

    for g in range(GROUPS):
        backward_group(g)
        if g == 1:
            forward(whole, put_tqg, 5, 0)
        if g == 3:
            forward(whole, put_tkg, 6, 0)

    await_bytes(t_r, t_rs)
    tt[...] = t_r[...].T
    await_bytes(u_half(y_m, 1), y_rs.at[3])
    await_bytes(u_half(y_p, 0), y_rs.at[2])
    y_f = (y + 2) % YS
    await_bytes(u_half(y_f, 0), y_rs.at[4])
    await_bytes(u_half(y_f, 1), y_rs.at[5])

    def weight_part(chunk):
        return mm(tt[...], u_s[:, rows(chunk * COLS, COLS)], 1, 0)

    def pair_sum(i):
        await_bytes(crecv.at[i], c_rs.at[i])
        rsend[i] = (wgf[i] + crecv[i].astype(F32)).astype(B16)
        slot = rrecv.at[x * 4 + zh * 2 + zl]
        for k in range(4):
            xd = (x + k) % 4
            piece = rsend.at[i, rows(xd * OUT_ROWS, OUT_ROWS)]
            if k > 0:
                send(piece, slot, r_ss.at[k], r_rs, dev(xd, y, i // 2, i % 2, core))
            else:
                mine = zh * 2 + zl == i

                @pl.when(mine)
                def _():
                    local(piece, slot, r_rs)

                @pl.when(jnp.logical_not(mine))
                def _():
                    send(piece, slot, r_ss.at[0], r_rs, dev(xd, y, i // 2, i % 2, core))

    for i in range(4):
        csend[i] = weight_part(2 * i + 1 - core).astype(B16)
        send(csend.at[i], crecv.at[i], c_ss, c_rs.at[i], other)
        wgf[i] = weight_part(2 * i + core)
        if i > 0:
            pair_sum(i - 1)
    pair_sum(3)

    await_bytes(rrecv, r_rs)
    total = rrecv[0].astype(F32)
    for k in range(1, 16):
        total = total + rrecv[k].astype(F32)
    red[...] = total.astype(B16)
    out_cols = rows(((zh * 2 + zl) * 2 + core) * COLS, COLS)
    zh_own, core_own = y // 2, y % 2
    for k in range(8):
        yd, zld = (y + k // 2) % YS, (zl + k) % 2
        mine = (yd == y) & (zh_own == zh) & (zld == zl) & (core_own == core)

        @pl.when(mine)
        def _():
            local(red, g_r.at[:, out_cols], g_rs)

        @pl.when(jnp.logical_not(mine))
        def _():
            send(red, g_r.at[:, out_cols], g_ss.at[k], g_rs, dev(x, yd, zh_own, zld, core_own))

    local(b_b, sqg_o.at[0], out_s.at[0])
    for g in range(GROUPS):
        cols = pl.ds(g * GC, GC)
        await_bytes(dk_r.at[:, cols], x_rs.at[0, g])
        await_bytes(dv_r.at[:, cols], x_rs.at[1, g])
    await_bytes(dk_x, x_ss)
    await_bytes(dv_x, x_ss)
    dk_x[...] = (dk_f[...] + dk_r[...].astype(F32)).astype(B16)
    local(dk_x, skg_o.at[0], out_s.at[1])
    dv_x[...] = (dv_f[...] + dv_r[...].astype(F32)).astype(B16)
    local(dv_x, svg_o.at[0], out_s.at[2])

    await_bytes(tqg_r, a2a_rs.at[5])
    local(tqg_r, tqg_o.at[0], out_s.at[3])
    await_bytes(tkg_r, a2a_rs.at[6])
    local(tkg_r, tkg_o.at[0], out_s.at[4])

    await_bytes(k_s.at[own_k], kv_ss.at[0])
    await_bytes(v_s.at[own_k], kv_ss.at[1])
    for i in range(6):
        await_bytes(u_half(0, 0), y_ss.at[i])
    await_bytes(c_b, a2a_ss.at[4])
    await_bytes(a_b, a2a_ss.at[5])
    await_bytes(d_b, a2a_ss.at[6])
    for unit in range(8):
        await_bytes(hop.at[unit], hop_ss.at[unit])
    await_bytes(csend, c_ss)
    for k in range(1, 4):
        await_bytes(rsend.at[0], r_ss.at[k])
    await_bytes(rsend.at[0, pl.ds(0, 3 * OUT_ROWS)], r_ss.at[0])
    for k in range(8):
        yd, zld = (y + k // 2) % YS, (zl + k) % 2
        mine = (yd == y) & (zh_own == zh) & (zld == zl) & (core_own == core)

        @pl.when(jnp.logical_not(mine))
        def _():
            await_bytes(red, g_ss.at[k])

    await_bytes(g_r, g_rs)
    local(g_r, wg_o, out_s.at[5])
    await_bytes(tqg_r, out_s.at[3])
    await_bytes(tkg_r, out_s.at[4])
    await_bytes(g_r, out_s.at[5])
    await_bytes(b_b, out_s.at[0])
    await_bytes(dk_x, out_s.at[1])
    await_bytes(dv_x, out_s.at[2])


def store(a, b, c, d, e, wg, a_o, b_o, c_o, d_o, e_o, wg_o, held, low, wide, loads, stores):
    ins = [
        pltpu.make_async_copy(src, dst, loads.at[i])
        for i, (src, dst) in enumerate(
            [(wg, low)] + [(r, held.at[pl.ds(k, 1)]) for k, r in enumerate((a, b, c, d, e))]
        )
    ]
    outs = [pltpu.make_async_copy(wide, wg_o, stores.at[0])] + [
        pltpu.make_async_copy(held.at[pl.ds(k, 1)], r, stores.at[k + 1])
        for k, r in enumerate((a_o, b_o, c_o, d_o, e_o))
    ]
    for copy in ins:
        copy.start()
    for k, copy in enumerate(ins):
        copy.wait()
        if k == 0:
            wide[...] = low[...].astype(F32)
        outs[k].start()
    for copy in outs:
        copy.wait()


def local(qs, ks, vs, qt, kt, up, w, mask):
    hbm = pl.BlockSpec(memory_space=pl.ANY)
    vm = pltpu.VMEM
    dma = pltpu.SemaphoreType.DMA
    unit = jax.ShapeDtypeStruct((1, ROWS, HH), B16)
    own = vm((ROWS, HH), B16)
    outs = pl.pallas_call(
        kernel,
        out_shape=(unit,) * 5 + (jax.ShapeDtypeStruct((OUT_ROWS, D), B16),),
        in_specs=[hbm] * 7 + [pl.BlockSpec(memory_space=pltpu.VMEM)],
        out_specs=(hbm,) * 6,
        scratch_shapes=[
            own, vm((P_SIZE, HH), B16), vm((P_SIZE, HH), B16), vm((HH, D), B16),
            vm((YS * ROWS, D), B16), own, own, own, own, own, vm((YS * ROWS, BLOCK), B16),
            own, own, own, own,
            vm((HEADS, P_SIZE, ROWS), F32), vm((HEADS, ROWS, ROWS), F32),
            vm((P_SIZE, ROWS), F32), vm((ROWS, ROWS), F32),
            vm((BLOCK, YS * ROWS), B16), vm((4, BLOCK, COLS), F32),
            vm((4, BLOCK, COLS), B16), vm((4, BLOCK, COLS), B16),
            vm((4, BLOCK, COLS), B16), vm((16, OUT_ROWS, COLS), B16), vm((OUT_ROWS, COLS), B16),
            vm((ROWS, HH), F32), vm((ROWS, HH), F32), own, own, own, own,
            vm((8, 2 * PIX, HH), B16), vm((GROUPS, ROWS, GC), F32),
            own, own, vm((OUT_ROWS, D), B16),
            dma((6 + WCH,)), dma((2,)), dma((2,)), dma((6,)), dma((6,)), dma((8,)), dma((7,)),
            dma((GROUPS,)), dma((GROUPS,)), dma, dma((8,)), dma((8, GROUPS)), dma, dma((4,)), dma((4,)), dma,
            dma((8,)), dma, dma, dma((2, GROUPS)), dma((6,)),
        ],
        compiler_params=pltpu.CompilerParams(
            has_side_effects=True, vmem_limit_bytes=62 * 1024 * 1024
        ),
        cost_estimate=pl.CostEstimate(
            flops=8 * 10**9, bytes_accessed=20 * 10**6, transcendentals=3 * 10**6
        ),
    )(qs, ks, vs, qt, kt, up, w, mask)
    return pl.pallas_call(
        store,
        out_shape=(unit,) * 5 + (jax.ShapeDtypeStruct((OUT_ROWS, D), F32),),
        in_specs=[hbm] * 6,
        out_specs=(hbm,) * 6,
        scratch_shapes=[
            vm((5, ROWS, HH), B16), vm((OUT_ROWS, D), B16), vm((OUT_ROWS, D), F32), dma((6,)), dma((6,)),
        ],
        compiler_params=pltpu.CompilerParams(vmem_limit_bytes=62 * 1024 * 1024),
    )(*outs)


def solution(mesh):
    tokens = P("dp", "seq", None)
    return jax.shard_map(
        local,
        mesh=mesh,
        in_specs=(tokens,) * 6 + (P(), P()),
        out_specs=(tokens,) * 5 + (P("seq", None),),
        check_vma=False,
    )
```

```python
import math

import jax
import jax.numpy as jnp
from jax import lax
from jax.experimental import pallas as pl
from jax.experimental.pallas import tpu as pltpu
from jax.sharding import PartitionSpec as P

HEADS = 12
HD = 128
HH = HEADS * HD
D = 3072
ROWS = 256
P_SIZE = 512
TILE = 32
NT = 16
FRAMES = 8
PIX = ROWS // FRAMES
HALF = PIX // 2
YS = 4
BLOCK = HH // YS
COLS = D // 8
OUT_ROWS = 96
SUB = OUT_ROWS // 2
SIDE = BLOCK // 2
GROUPS = 4
GH = HEADS // GROUPS
GC = GH * HD
WCH = 6
WROWS = HH // WCH
SCALE = 1.0 / math.sqrt(HD)
NEG = -1e30
MESH = pl.DeviceIdType.MESH
F32 = jnp.float32
B16 = jnp.bfloat16


def mm(a, b, ca, cb):
    return lax.dot_general(a, b, (((ca,), (cb,)), ((), ())), preferred_element_type=F32)


def kernel(
    qs, ks, vs, qt, kt, up, w, mask,
    sqg_o, skg_o, svg_o, tqg_o, tkg_o, wg_o,
    q_s, k_s, v_s, w_s, u_s, tq_r, tk_r, so_r, oc_r, sc_r, t_r,
    a_b, b_b, c_b, d_b, pw, tw, bias, tbias, tt, wgf, csend, crecv, rsend, ra, rb, ra2, rb2, sa, sb, red,
    dk_f, dv_f, dk_x, dv_x, dk_r, dv_r, hop, t_f, tqg_r, tkg_r, g_r,
    ld, kv_ss, kv_rs, y_ss, y_rs, a2a_ss, a2a_rs, so_rs, sc_rs, t_rs, hop_ss, hop_rs,
    c_ss, c_rs, r_ss, r_rs, g_ss, g_rs, x_ss, x_rs, out_s,
):
    dp = lax.axis_index("dp")
    seq = lax.axis_index("seq")
    y, zl = dp // 2, dp % 2
    x, zh, core = seq // 4, (seq // 2) % 2, seq % 2
    frame = x * 2 + zh

    def dev(x_, y_, zh_, zl_, c_):
        return {"dp": y_ * 2 + zl_, "seq": x_ * 4 + zh_ * 2 + c_}

    def send(src, dst, ss, rs, to):
        pltpu.make_async_remote_copy(
            src_ref=src, dst_ref=dst, send_sem=ss, recv_sem=rs, device_id=to, device_id_type=MESH
        ).start()

    def await_bytes(ref, sem):
        pltpu.make_async_copy(ref, ref, sem).wait()

    def local(src, dst, sem):
        pltpu.make_async_copy(src, dst, sem).start()

    def rows(start, size):
        return pl.ds(pl.multiple_of(start, size), size)

    def spread(src, cols, put, unit, part):
        for zd in range(2):
            for side in range(2):
                far = ((x + 2) % 4 * 2 + zd) * PIX + side * HALF
                send(
                    src.at[rows(far, HALF), cols],
                    hop.at[unit, rows(side * PIX + zh * HALF, HALF), cols],
                    a2a_ss.at[unit], hop_rs.at[unit, part],
                    dev((x + 1 + 2 * side) % 4, y, zd, 1 - zl, core),
                )
        for step in (1, 3, 0):
            xd = (x + step) % 4
            for zd in range(2):
                put(
                    src, rows((xd * 2 + zd) * PIX, PIX), frame * PIX, PIX, a2a_ss.at[unit],
                    xd, zd, 1 - zl,
                )

    def forward(cols, put, unit, part):
        await_bytes(hop.at[unit, :, cols], hop_rs.at[unit, part])
        for side in range(2):
            came = (x + 3 + 2 * side) % 4
            for zs in range(2):
                put(
                    hop.at[unit], pl.ds(side * PIX + zs * HALF, HALF),
                    (came * 2 + zs) * PIX + side * HALF, HALF, hop_ss.at[unit],
                    (x + 1 + 2 * side) % 4, zh, zl,
                )

    def putter(dst, cols, rs):
        def put(src, src_rows, start, size, ss, xd, zd, zld):
            send(
                src.at[src_rows, cols], dst.at[rows(start, size), cols], ss, rs,
                dev(xd, y, zd, zld, core),
            )

        return put

    whole = pl.ds(0, HH)
    group_cols = [pl.ds(g * GC, GC) for g in range(GROUPS)]
    put_tq = putter(tq_r, whole, a2a_rs.at[0])
    put_tk = putter(tk_r, whole, a2a_rs.at[1])
    put_oc = putter(oc_r, whole, a2a_rs.at[2])
    put_so = [putter(so_r, group_cols[g], so_rs.at[g]) for g in range(GROUPS)]
    put_sc = [putter(sc_r, group_cols[g], sc_rs.at[g]) for g in range(GROUPS)]
    put_tqg = putter(tqg_r, whole, a2a_rs.at[5])
    put_tkg = putter(tkg_r, whole, a2a_rs.at[6])

    def put_out(src, src_rows, start, size, ss, xd, zd, zld):
        for k in range(YS):
            yd = (y + k) % YS
            send(
                src.at[src_rows, rows(yd * BLOCK, BLOCK)], t_r.at[rows(y * ROWS + start, size)],
                ss, t_rs, dev(xd, yd, zd, zld, core),
            )

    other = dev(x, y, zh, zl, 1 - core)
    y_up = dev(x, (y + 1) % YS, zh, zl, core)
    y_dn = dev(x, (y + 3) % YS, zh, zl, core)

    half = ROWS // 2
    own_k, far_k = pl.ds(0, ROWS), pl.ds(ROWS, ROWS)
    own_u = pl.ds(pl.multiple_of(y * ROWS, ROWS), ROWS)

    def u_half(owner, part):
        return u_s.at[pl.ds(pl.multiple_of(owner * ROWS + part * half, half), half)]

    loads = (
        (ks.at[0], k_s.at[own_k]), (vs.at[0], v_s.at[own_k]), (qt.at[0], b_b), (kt.at[0], d_b),
        (up.at[0], u_s.at[own_u]), (qs.at[0], q_s),
    )
    for i, (src, dst) in enumerate(loads):
        local(src, dst, ld.at[i])
    for i in range(WCH):
        local(w.at[pl.ds(i * WROWS, WROWS)], w_s.at[pl.ds(i * WROWS, WROWS)], ld.at[6 + i])

    await_bytes(k_s.at[own_k], ld.at[0])
    send(k_s.at[own_k], k_s.at[far_k], kv_ss.at[0], kv_rs.at[0], other)
    await_bytes(v_s.at[own_k], ld.at[1])
    send(v_s.at[own_k], v_s.at[far_k], kv_ss.at[1], kv_rs.at[1], other)
    await_bytes(b_b, ld.at[2])
    spread(b_b, whole, put_tq, 0, 0)
    await_bytes(u_s.at[own_u], ld.at[4])
    send(u_half(y, 0), u_half(y, 0), y_ss.at[0], y_rs.at[0], y_up)
    send(u_half(y, 1), u_half(y, 1), y_ss.at[1], y_rs.at[1], y_dn)
    await_bytes(d_b, ld.at[3])
    spread(d_b, whole, put_tk, 1, 0)
    send(u_half(y, 0), u_half(y, 0), y_ss.at[2], y_rs.at[2], y_dn)
    send(u_half(y, 1), u_half(y, 1), y_ss.at[3], y_rs.at[3], y_up)

    key_row = lax.broadcasted_iota(jnp.int32, (P_SIZE, NT), 0)
    key_tile = jnp.where(
        key_row < ROWS, core * (NT // 2) + key_row // TILE,
        (1 - core) * (NT // 2) + (key_row - ROWS) // TILE,
    )
    key_hot = (key_tile == lax.broadcasted_iota(jnp.int32, (P_SIZE, NT), 1)).astype(F32)
    query_tile = core * (NT // 2) + lax.broadcasted_iota(jnp.int32, (ROWS, NT), 0) // TILE
    query_hot = (query_tile == lax.broadcasted_iota(jnp.int32, (ROWS, NT), 1)).astype(F32)
    rows_mask = mm(query_hot, mask[...].astype(F32), 1, 0)
    bias[...] = jnp.where(mm(key_hot, rows_mask, 1, 1) > 0.5, 0.0, NEG)
    same = (
        lax.broadcasted_iota(jnp.int32, (ROWS, ROWS), 0) % PIX
        == lax.broadcasted_iota(jnp.int32, (ROWS, ROWS), 1) % PIX
    )
    tbias[...] = jnp.where(same, 0.0, NEG)

    for i in range(WCH):
        await_bytes(w_s.at[pl.ds(i * WROWS, WROWS)], ld.at[6 + i])
        c_b[:, pl.ds(i * WROWS, WROWS)] = mm(
            u_s[own_u, :], w_s[pl.ds(i * WROWS, WROWS), :], 1, 1
        ).astype(B16)

    await_bytes(q_s, ld.at[5])
    await_bytes(k_s.at[far_k], kv_rs.at[0])
    await_bytes(v_s.at[far_k], kv_rs.at[1])

    def space_forward(h):
        hs = pl.ds(h * HD, HD)
        scores = mm(k_s[:, hs], q_s[:, hs], 1, 1) * SCALE + bias[...]
        powers = jnp.exp(scores - jnp.max(scores, axis=0, keepdims=True))
        weights = powers * (1.0 / jnp.sum(powers, axis=0, keepdims=True))
        pw[h] = weights
        a_b[:, hs] = mm(weights.astype(B16), v_s[:, hs], 0, 0).astype(B16)

    for g in range(GROUPS):
        for h in range(g * GH, (g + 1) * GH):
            space_forward(h)
        spread(a_b, group_cols[g], put_so[g], 3, g)
        if g == 1:
            forward(whole, put_tq, 0, 0)
        if g == 3:
            forward(whole, put_tk, 1, 0)

    spread(c_b, whole, put_oc, 2, 0)

    await_bytes(tq_r, a2a_rs.at[0])
    await_bytes(tk_r, a2a_rs.at[1])

    def time_forward(h):
        hs = pl.ds(h * HD, HD)
        scores = mm(tk_r[:, hs], tq_r[:, hs], 1, 1) * SCALE + tbias[...]
        powers = jnp.exp(scores - jnp.max(scores, axis=0, keepdims=True))
        weights = powers * (1.0 / jnp.sum(powers, axis=0, keepdims=True))
        tw[h] = weights

    for h in range(HEADS):
        time_forward(h)
    for g in range(GROUPS):
        forward(group_cols[g], put_so[g], 3, g)

    y_m, y_p = (y + 3) % YS, (y + 1) % YS
    await_bytes(u_half(y_m, 0), y_rs.at[0])
    send(u_half(y_m, 0), u_half(y_m, 0), y_ss.at[4], y_rs.at[4], y_up)
    await_bytes(u_half(y_p, 1), y_rs.at[1])
    send(u_half(y_p, 1), u_half(y_p, 1), y_ss.at[5], y_rs.at[5], y_dn)

    await_bytes(b_b, a2a_ss.at[0])
    for g in range(GROUPS):
        await_bytes(so_r.at[:, group_cols[g]], so_rs.at[g])
        heads = [
            mm(tw[h].astype(B16), so_r[:, h * HD:(h + 1) * HD], 0, 0)
            for h in range(g * GH, (g + 1) * GH)
        ]
        t_f[g] = jnp.concatenate(heads, axis=1)
    for k in range(YS):
        block = [
            t_f[g, :, k * OUT_ROWS + part * SUB:k * OUT_ROWS + (part + 1) * SUB]
            for part in range(2)
            for g in range(GROUPS)
        ]
        b_b[:, k * BLOCK:(k + 1) * BLOCK] = jnp.concatenate(block, axis=1).astype(B16)

    spread(b_b, whole, put_out, 7, 0)
    forward(whole, put_oc, 2, 0)

    await_bytes(oc_r, a2a_rs.at[2])
    await_bytes(c_b, a2a_ss.at[2])
    await_bytes(a_b, a2a_ss.at[3])
    await_bytes(d_b, a2a_ss.at[1])

    def time_backward(h):
        hs = pl.ds(h * HD, HD)
        weights = tw[h]
        cot = oc_r[:, hs]
        c_b[:, hs] = mm(weights.astype(B16), cot, 1, 0).astype(B16)
        prob = mm(so_r[:, hs], cot, 1, 1)
        centre = jnp.sum(weights * prob, axis=0, keepdims=True)
        grad = (weights * (prob - centre)).astype(B16)
        a_b[:, hs] = (mm(grad, tk_r[:, hs], 0, 0) * SCALE).astype(B16)
        d_b[:, hs] = (mm(grad, tq_r[:, hs], 1, 0) * SCALE).astype(B16)

    for g in range(GROUPS):
        for h in range(g * GH, (g + 1) * GH):
            time_backward(h)
        spread(c_b, group_cols[g], put_sc[g], 4, g)
        if g == 0:
            forward(whole, put_out, 7, 0)
        else:
            forward(group_cols[g - 1], put_sc[g - 1], 4, g - 1)

    spread(a_b, whole, put_tqg, 5, 0)
    forward(group_cols[GROUPS - 1], put_sc[GROUPS - 1], 4, GROUPS - 1)

    await_bytes(b_b, a2a_ss.at[7])

    def space_backward(h):
        hs = pl.ds(h * HD, HD)
        weights = pw[h]
        cot = sc_r[:, hs]
        key = k_s[:, hs]
        prob = mm(v_s[:, hs], cot, 1, 1)
        centre = jnp.sum(weights * prob, axis=0, keepdims=True)
        grad = (weights * (prob - centre)).astype(B16)
        b_b[:, hs] = (mm(grad, key, 0, 0) * SCALE).astype(B16)
        dk = mm(grad, q_s[:, hs], 1, 0) * SCALE
        dv = mm(weights.astype(B16), cot, 1, 0)
        dk_f[:, hs] = dk[:ROWS]
        dv_f[:, hs] = dv[:ROWS]
        dk_x[:, hs] = dk[ROWS:].astype(B16)
        dv_x[:, hs] = dv[ROWS:].astype(B16)

    def backward_group(g):
        cols = pl.ds(g * GC, GC)
        await_bytes(sc_r.at[:, cols], sc_rs.at[g])
        for h in range(g * GH, (g + 1) * GH):
            space_backward(h)
        send(dk_x.at[:, cols], dk_r.at[:, cols], x_ss, x_rs.at[0, g], other)
        send(dv_x.at[:, cols], dv_r.at[:, cols], x_ss, x_rs.at[1, g], other)

    backward_group(0)
    forward(whole, put_tqg, 5, 0)
    backward_group(1)

    await_bytes(t_r, t_rs)
    tt[...] = t_r[...].T
    await_bytes(u_half(y_m, 1), y_rs.at[3])
    await_bytes(u_half(y_p, 0), y_rs.at[2])
    y_f = (y + 2) % YS
    await_bytes(u_half(y_f, 0), y_rs.at[4])
    await_bytes(u_half(y_f, 1), y_rs.at[5])

    z = zh * 2 + zl

    def chip(k):
        zd = (z + k) % 4
        return zd // 2, zd % 2

    def weight_part(k, which):
        zd = (z + k) % 4
        return mm(tt[...], u_s[:, rows((zd * 2 + which) * COLS, COLS)], 1, 0)

    def pair_sum(k):
        await_bytes(crecv.at[k], c_rs.at[k])
        rsend[k] = (wgf[k] + crecv[k].astype(F32)).astype(B16)
        for step in range(1, 4):
            xd = (x + step) % 4
            send(rsend.at[k, rows(xd * SUB, SUB)], ra.at[x, k], r_ss.at[0], r_rs.at[0], dev(xd, y, zh, zl, core))
        if k > 0:
            zhd, zld = chip(k)
            send(rsend.at[k, pl.ds(SIDE, SIDE)], rb.at[z], r_ss.at[1], r_rs.at[1], dev(x, y, zhd, zld, core))

    order = (1, 2, 3, 0)
    for n, k in enumerate(order):
        csend[k] = weight_part(k, 1 - core).astype(B16)
        send(csend.at[k], crecv.at[k], c_ss, c_rs.at[k], other)
        wgf[k] = weight_part(k, core)
        if n > 0:
            pair_sum(order[n - 1])
    pair_sum(0)
    spread(d_b, whole, put_tkg, 6, 0)
    backward_group(2)

    for k in range(4):
        ra[x, k] = rsend[k, rows(x * SUB, SUB)]
    rb[z] = rsend[0, SIDE:]
    await_bytes(ra.at[pl.ds(0, 3)], r_rs.at[0])
    for k in range(4):
        total = ra[0, k].astype(F32)
        for n in range(1, 4):
            total = total + ra[n, k].astype(F32)
        sa[k] = total.astype(B16)
        if k > 0:
            zhd, zld = chip(k)
            send(sa.at[k], ra2.at[z], r_ss.at[2], r_rs.at[2], dev(x, y, zhd, zld, core))
    ra2[z] = sa[0]
    await_bytes(rb.at[pl.ds(0, 3)], r_rs.at[1])
    total = rb[0].astype(F32)
    for n in range(1, 4):
        total = total + rb[n].astype(F32)
    sb[...] = total.astype(B16)
    for step in range(1, 4):
        xd = (x + step) % 4
        send(sb.at[rows(xd * SUB, SUB)], rb2.at[x], r_ss.at[3], r_rs.at[3], dev(xd, y, zh, zl, core))
    rb2[x] = sb[rows(x * SUB, SUB)]
    backward_group(3)

    for part, (held, n) in enumerate(((ra2, 2), (rb2, 3))):
        await_bytes(held.at[pl.ds(0, 3)], r_rs.at[n])
        total = held[0].astype(F32)
        for k in range(1, 4):
            total = total + held[k].astype(F32)
        red[part * SUB:(part + 1) * SUB] = total.astype(B16)
    out_cols = rows(((zh * 2 + zl) * 2 + core) * COLS, COLS)
    zh_own, core_own = y // 2, y % 2
    for k in range(8):
        yd, zld = (y + k // 2) % YS, (zl + k) % 2
        mine = (yd == y) & (zh_own == zh) & (zld == zl) & (core_own == core)

        @pl.when(mine)
        def _():
            local(red, g_r.at[:, out_cols], g_rs)

        @pl.when(jnp.logical_not(mine))
        def _():
            send(red, g_r.at[:, out_cols], g_ss.at[k], g_rs, dev(x, yd, zh_own, zld, core_own))

    forward(whole, put_tkg, 6, 0)

    local(b_b, sqg_o.at[0], out_s.at[0])
    for g in range(GROUPS):
        cols = pl.ds(g * GC, GC)
        await_bytes(dk_r.at[:, cols], x_rs.at[0, g])
        await_bytes(dv_r.at[:, cols], x_rs.at[1, g])
    await_bytes(dk_x, x_ss)
    await_bytes(dv_x, x_ss)
    dk_x[...] = (dk_f[...] + dk_r[...].astype(F32)).astype(B16)
    local(dk_x, skg_o.at[0], out_s.at[1])
    dv_x[...] = (dv_f[...] + dv_r[...].astype(F32)).astype(B16)
    local(dv_x, svg_o.at[0], out_s.at[2])

    await_bytes(tqg_r, a2a_rs.at[5])
    local(tqg_r, tqg_o.at[0], out_s.at[3])
    await_bytes(tkg_r, a2a_rs.at[6])
    local(tkg_r, tkg_o.at[0], out_s.at[4])

    await_bytes(k_s.at[own_k], kv_ss.at[0])
    await_bytes(v_s.at[own_k], kv_ss.at[1])
    for i in range(6):
        await_bytes(u_half(0, 0), y_ss.at[i])
    await_bytes(c_b, a2a_ss.at[4])
    await_bytes(a_b, a2a_ss.at[5])
    await_bytes(d_b, a2a_ss.at[6])
    for unit in range(8):
        await_bytes(hop.at[unit], hop_ss.at[unit])
    await_bytes(csend, c_ss)
    for n, held in enumerate((ra, rb, ra2, rb2)):
        await_bytes(held.at[pl.ds(0, 3)], r_ss.at[n])
    for k in range(8):
        yd, zld = (y + k // 2) % YS, (zl + k) % 2
        mine = (yd == y) & (zh_own == zh) & (zld == zl) & (core_own == core)

        @pl.when(jnp.logical_not(mine))
        def _():
            await_bytes(red, g_ss.at[k])

    await_bytes(g_r, g_rs)
    local(g_r, wg_o, out_s.at[5])
    await_bytes(tqg_r, out_s.at[3])
    await_bytes(tkg_r, out_s.at[4])
    await_bytes(g_r, out_s.at[5])
    await_bytes(b_b, out_s.at[0])
    await_bytes(dk_x, out_s.at[1])
    await_bytes(dv_x, out_s.at[2])


def store(a, b, c, d, e, wg, a_o, b_o, c_o, d_o, e_o, wg_o, held, low, wide, loads, stores):
    ins = [
        pltpu.make_async_copy(src, dst, loads.at[i])
        for i, (src, dst) in enumerate(
            [(wg, low)] + [(r, held.at[pl.ds(k, 1)]) for k, r in enumerate((a, b, c, d, e))]
        )
    ]
    outs = [pltpu.make_async_copy(wide, wg_o, stores.at[0])] + [
        pltpu.make_async_copy(held.at[pl.ds(k, 1)], r, stores.at[k + 1])
        for k, r in enumerate((a_o, b_o, c_o, d_o, e_o))
    ]
    for copy in ins:
        copy.start()
    for k, copy in enumerate(ins):
        copy.wait()
        if k == 0:
            wide[...] = low[...].astype(F32)
        outs[k].start()
    for copy in outs:
        copy.wait()


def local(qs, ks, vs, qt, kt, up, w, mask):
    hbm = pl.BlockSpec(memory_space=pl.ANY)
    vm = pltpu.VMEM
    dma = pltpu.SemaphoreType.DMA
    unit = jax.ShapeDtypeStruct((1, ROWS, HH), B16)
    own = vm((ROWS, HH), B16)
    outs = pl.pallas_call(
        kernel,
        out_shape=(unit,) * 5 + (jax.ShapeDtypeStruct((OUT_ROWS, D), B16),),
        in_specs=[hbm] * 7 + [pl.BlockSpec(memory_space=pltpu.VMEM)],
        out_specs=(hbm,) * 6,
        scratch_shapes=[
            own, vm((P_SIZE, HH), B16), vm((P_SIZE, HH), B16), vm((HH, D), B16),
            vm((YS * ROWS, D), B16), own, own, own, own, own, vm((YS * ROWS, BLOCK), B16),
            own, own, own, own,
            vm((HEADS, P_SIZE, ROWS), F32), vm((HEADS, ROWS, ROWS), F32),
            vm((P_SIZE, ROWS), F32), vm((ROWS, ROWS), F32),
            vm((BLOCK, YS * ROWS), B16), vm((4, BLOCK, COLS), F32),
            vm((4, BLOCK, COLS), B16), vm((4, BLOCK, COLS), B16),
            vm((4, BLOCK, COLS), B16), vm((4, 4, SUB, COLS), B16), vm((4, SIDE, COLS), B16),
            vm((4, SUB, COLS), B16), vm((4, SUB, COLS), B16), vm((4, SUB, COLS), B16),
            vm((SIDE, COLS), B16), vm((OUT_ROWS, COLS), B16),
            vm((ROWS, HH), F32), vm((ROWS, HH), F32), own, own, own, own,
            vm((8, 2 * PIX, HH), B16), vm((GROUPS, ROWS, GC), F32),
            own, own, vm((OUT_ROWS, D), B16),
            dma((6 + WCH,)), dma((2,)), dma((2,)), dma((6,)), dma((6,)), dma((8,)), dma((7,)),
            dma((GROUPS,)), dma((GROUPS,)), dma, dma((8,)), dma((8, GROUPS)), dma, dma((4,)), dma((4,)), dma((4,)),
            dma((8,)), dma, dma, dma((2, GROUPS)), dma((6,)),
        ],
        compiler_params=pltpu.CompilerParams(
            has_side_effects=True, vmem_limit_bytes=62 * 1024 * 1024
        ),
        cost_estimate=pl.CostEstimate(
            flops=8 * 10**9, bytes_accessed=20 * 10**6, transcendentals=3 * 10**6
        ),
    )(qs, ks, vs, qt, kt, up, w, mask)
    return pl.pallas_call(
        store,
        out_shape=(unit,) * 5 + (jax.ShapeDtypeStruct((OUT_ROWS, D), F32),),
        in_specs=[hbm] * 6,
        out_specs=(hbm,) * 6,
        scratch_shapes=[
            vm((5, ROWS, HH), B16), vm((OUT_ROWS, D), B16), vm((OUT_ROWS, D), F32), dma((6,)), dma((6,)),
        ],
        compiler_params=pltpu.CompilerParams(vmem_limit_bytes=62 * 1024 * 1024),
    )(*outs)


def solution(mesh):
    tokens = P("dp", "seq", None)
    return jax.shard_map(
        local,
        mesh=mesh,
        in_specs=(tokens,) * 6 + (P(), P()),
        out_specs=(tokens,) * 5 + (P("seq", None),),
        check_vma=False,
    )
```

```python
import math

import jax
import jax.numpy as jnp
from jax import lax
from jax.experimental import pallas as pl
from jax.experimental.pallas import tpu as pltpu
from jax.sharding import PartitionSpec as P

HEADS = 12
HD = 128
HH = HEADS * HD
D = 3072
ROWS = 256
P_SIZE = 512
TILE = 32
NT = 16
FRAMES = 8
PIX = ROWS // FRAMES
HALF = PIX // 2
YS = 4
BLOCK = HH // YS
COLS = D // 8
OUT_ROWS = 96
SUB = OUT_ROWS // 2
SIDE = BLOCK // 2
GROUPS = 4
GH = HEADS // GROUPS
GC = GH * HD
WCH = 6
WROWS = HH // WCH
SCALE = 1.0 / math.sqrt(HD)
POWER = SCALE / math.log(2.0)
NEG = -1e30
BAND = PIX // 2
GROUP = ROWS // 2
MESH = pl.DeviceIdType.MESH
F32 = jnp.float32
B16 = jnp.bfloat16


def mm(a, b, ca, cb):
    return lax.dot_general(a, b, (((ca,), (cb,)), ((), ())), preferred_element_type=F32)


def kernel(
    qs, ks, vs, qt, kt, up, w, mask,
    sqg_o, skg_o, svg_o, tqg_o, tkg_o, wg_o,
    q_s, k_s, v_s, w_s, u_s, tq_r, tk_r, so_r, oc_r, sc_r, t_r,
    a_b, b_b, c_b, d_b, pw, tw, bias, tbias, tt, wgf, csend, crecv, rsend, ra, rb, ra2, rb2, sa, sb, red,
    dk_f, dv_f, dk_x, dv_x, dk_r, dv_r, hop, t_f, tqg_r, tkg_r, g_r,
    ld, kv_ss, kv_rs, y_ss, y_rs, a2a_ss, a2a_rs, so_rs, sc_rs, t_rs, hop_ss, hop_rs,
    c_ss, c_rs, r_ss, r_rs, g_ss, g_rs, x_ss, x_rs, out_s,
):
    dp = lax.axis_index("dp")
    seq = lax.axis_index("seq")
    y, zl = dp // 2, dp % 2
    x, zh, core = seq // 4, (seq // 2) % 2, seq % 2
    frame = x * 2 + zh

    def dev(x_, y_, zh_, zl_, c_):
        return {"dp": y_ * 2 + zl_, "seq": x_ * 4 + zh_ * 2 + c_}

    def send(src, dst, ss, rs, to):
        pltpu.make_async_remote_copy(
            src_ref=src, dst_ref=dst, send_sem=ss, recv_sem=rs, device_id=to, device_id_type=MESH
        ).start()

    def await_bytes(ref, sem):
        pltpu.make_async_copy(ref, ref, sem).wait()

    def local(src, dst, sem):
        pltpu.make_async_copy(src, dst, sem).start()

    def rows(start, size):
        return pl.ds(pl.multiple_of(start, size), size)

    def spread(src, cols, put, unit, part):
        for zd in range(2):
            for side in range(2):
                far = ((x + 2) % 4 * 2 + zd) * PIX + side * HALF
                send(
                    src.at[rows(far, HALF), cols],
                    hop.at[unit, rows(side * PIX + zh * HALF, HALF), cols],
                    a2a_ss.at[unit], hop_rs.at[unit, part],
                    dev((x + 1 + 2 * side) % 4, y, zd, 1 - zl, core),
                )
        for step in (1, 3, 0):
            xd = (x + step) % 4
            for zd in range(2):
                put(
                    src, rows((xd * 2 + zd) * PIX, PIX), frame * PIX, PIX, a2a_ss.at[unit],
                    xd, zd, 1 - zl,
                )

    def forward(cols, put, unit, part):
        await_bytes(hop.at[unit, :, cols], hop_rs.at[unit, part])
        for side in range(2):
            came = (x + 3 + 2 * side) % 4
            for zs in range(2):
                put(
                    hop.at[unit], pl.ds(side * PIX + zs * HALF, HALF),
                    (came * 2 + zs) * PIX + side * HALF, HALF, hop_ss.at[unit],
                    (x + 1 + 2 * side) % 4, zh, zl,
                )

    def putter(dst, cols, rs):
        def put(src, src_rows, start, size, ss, xd, zd, zld):
            send(
                src.at[src_rows, cols], dst.at[rows(start, size), cols], ss, rs,
                dev(xd, y, zd, zld, core),
            )

        return put

    whole = pl.ds(0, HH)
    group_cols = [pl.ds(g * GC, GC) for g in range(GROUPS)]
    put_tq = putter(tq_r, whole, a2a_rs.at[0])
    put_tk = putter(tk_r, whole, a2a_rs.at[1])
    put_oc = putter(oc_r, whole, a2a_rs.at[2])
    put_so = [putter(so_r, group_cols[g], so_rs.at[g]) for g in range(GROUPS)]
    put_sc = [putter(sc_r, group_cols[g], sc_rs.at[g]) for g in range(GROUPS)]
    put_tqg = putter(tqg_r, whole, a2a_rs.at[5])
    put_tkg = putter(tkg_r, whole, a2a_rs.at[6])

    def put_out(src, src_rows, start, size, ss, xd, zd, zld):
        for k in range(YS):
            yd = (y + k) % YS
            send(
                src.at[src_rows, rows(yd * BLOCK, BLOCK)], t_r.at[rows(y * ROWS + start, size)],
                ss, t_rs, dev(xd, yd, zd, zld, core),
            )

    other = dev(x, y, zh, zl, 1 - core)
    y_up = dev(x, (y + 1) % YS, zh, zl, core)
    y_dn = dev(x, (y + 3) % YS, zh, zl, core)

    half = ROWS // 2
    own_k, far_k = pl.ds(0, ROWS), pl.ds(ROWS, ROWS)
    own_u = pl.ds(pl.multiple_of(y * ROWS, ROWS), ROWS)

    def u_half(owner, part):
        return u_s.at[pl.ds(pl.multiple_of(owner * ROWS + part * half, half), half)]

    loads = (
        (ks.at[0], k_s.at[own_k]), (vs.at[0], v_s.at[own_k]), (qt.at[0], b_b), (kt.at[0], d_b),
        (up.at[0], u_s.at[own_u]), (qs.at[0], q_s),
    )
    for i, (src, dst) in enumerate(loads):
        local(src, dst, ld.at[i])
    for i in range(WCH):
        local(w.at[pl.ds(i * WROWS, WROWS)], w_s.at[pl.ds(i * WROWS, WROWS)], ld.at[6 + i])

    await_bytes(k_s.at[own_k], ld.at[0])
    send(k_s.at[own_k], k_s.at[far_k], kv_ss.at[0], kv_rs.at[0], other)
    await_bytes(v_s.at[own_k], ld.at[1])
    send(v_s.at[own_k], v_s.at[far_k], kv_ss.at[1], kv_rs.at[1], other)
    await_bytes(b_b, ld.at[2])
    spread(b_b, whole, put_tq, 0, 0)
    await_bytes(u_s.at[own_u], ld.at[4])
    send(u_half(y, 0), u_half(y, 0), y_ss.at[0], y_rs.at[0], y_up)
    send(u_half(y, 1), u_half(y, 1), y_ss.at[1], y_rs.at[1], y_dn)
    await_bytes(d_b, ld.at[3])
    spread(d_b, whole, put_tk, 1, 0)
    send(u_half(y, 0), u_half(y, 0), y_ss.at[2], y_rs.at[2], y_dn)
    send(u_half(y, 1), u_half(y, 1), y_ss.at[3], y_rs.at[3], y_up)

    key_row = lax.broadcasted_iota(jnp.int32, (P_SIZE, NT), 0)
    key_tile = jnp.where(
        key_row < ROWS, core * (NT // 2) + key_row // TILE,
        (1 - core) * (NT // 2) + (key_row - ROWS) // TILE,
    )
    key_hot = (key_tile == lax.broadcasted_iota(jnp.int32, (P_SIZE, NT), 1)).astype(F32)
    query_tile = core * (NT // 2) + lax.broadcasted_iota(jnp.int32, (ROWS, NT), 0) // TILE
    query_hot = (query_tile == lax.broadcasted_iota(jnp.int32, (ROWS, NT), 1)).astype(F32)
    rows_mask = mm(query_hot, mask[...].astype(F32), 1, 0)
    bias[...] = jnp.where(mm(key_hot, rows_mask, 1, 1) > 0.5, 0.0, NEG)
    same = (
        lax.broadcasted_iota(jnp.int32, (GROUP, GROUP), 0) % BAND
        == lax.broadcasted_iota(jnp.int32, (GROUP, GROUP), 1) % BAND
    )
    tbias[...] = jnp.where(same, 0.0, NEG)

    for i in range(WCH):
        await_bytes(w_s.at[pl.ds(i * WROWS, WROWS)], ld.at[6 + i])
        c_b[:, pl.ds(i * WROWS, WROWS)] = mm(
            w_s[pl.ds(i * WROWS, WROWS), :], u_s[own_u, :], 1, 1
        ).T.astype(B16)

    await_bytes(q_s, ld.at[5])
    await_bytes(k_s.at[far_k], kv_rs.at[0])
    await_bytes(v_s.at[far_k], kv_rs.at[1])

    def space_forward(h):
        hs = pl.ds(h * HD, HD)
        scores = mm(k_s[:, hs], q_s[:, hs], 1, 1) + bias[...]
        powers = jnp.exp2((scores - jnp.max(scores, axis=0, keepdims=True)) * POWER)
        weights = powers * (1.0 / jnp.sum(powers, axis=0, keepdims=True))
        pw[h] = weights
        a_b[:, hs] = mm(weights.astype(B16), v_s[:, hs], 0, 0).astype(B16)

    for g in range(GROUPS):
        for h in range(g * GH, (g + 1) * GH):
            space_forward(h)
        spread(a_b, group_cols[g], put_so[g], 3, g)
        if g == 1:
            forward(whole, put_tq, 0, 0)
        if g == 3:
            forward(whole, put_tk, 1, 0)

    spread(c_b, whole, put_oc, 2, 0)

    await_bytes(tq_r, a2a_rs.at[0])
    await_bytes(tk_r, a2a_rs.at[1])

    def band(ref, h, b):
        hs = pl.ds(h * HD, HD)
        return jnp.concatenate(
            [ref[f * PIX + b * BAND:f * PIX + (b + 1) * BAND, hs] for f in range(FRAMES)], axis=0
        )

    def put_band(ref, h, b, value):
        hs = pl.ds(h * HD, HD)
        for f in range(FRAMES):
            ref[f * PIX + b * BAND:f * PIX + (b + 1) * BAND, hs] = value[f * BAND:(f + 1) * BAND]

    def time_forward(h):
        for b in range(2):
            scores = mm(band(tk_r, h, b), band(tq_r, h, b), 1, 1) + tbias[...]
            powers = jnp.exp2((scores - jnp.max(scores, axis=0, keepdims=True)) * POWER)
            tw[h, b] = powers * (1.0 / jnp.sum(powers, axis=0, keepdims=True))

    for h in range(HEADS):
        time_forward(h)
    for g in range(GROUPS):
        forward(group_cols[g], put_so[g], 3, g)

    y_m, y_p = (y + 3) % YS, (y + 1) % YS
    await_bytes(u_half(y_m, 0), y_rs.at[0])
    send(u_half(y_m, 0), u_half(y_m, 0), y_ss.at[4], y_rs.at[4], y_up)
    await_bytes(u_half(y_p, 1), y_rs.at[1])
    send(u_half(y_p, 1), u_half(y_p, 1), y_ss.at[5], y_rs.at[5], y_dn)

    await_bytes(b_b, a2a_ss.at[0])
    for g in range(GROUPS):
        await_bytes(so_r.at[:, group_cols[g]], so_rs.at[g])
        for n in range(GH):
            h = g * GH + n
            for b in range(2):
                out = mm(tw[h, b].astype(B16), band(so_r, h, b), 0, 0)
                for f in range(FRAMES):
                    t_f[g, f * PIX + b * BAND:f * PIX + (b + 1) * BAND, n * HD:(n + 1) * HD] = (
                        out[f * BAND:(f + 1) * BAND]
                    )
    for k in range(YS):
        block = [
            t_f[g, :, k * OUT_ROWS + part * SUB:k * OUT_ROWS + (part + 1) * SUB]
            for part in range(2)
            for g in range(GROUPS)
        ]
        b_b[:, k * BLOCK:(k + 1) * BLOCK] = jnp.concatenate(block, axis=1).astype(B16)

    spread(b_b, whole, put_out, 7, 0)
    forward(whole, put_oc, 2, 0)

    await_bytes(oc_r, a2a_rs.at[2])
    await_bytes(c_b, a2a_ss.at[2])
    await_bytes(a_b, a2a_ss.at[3])
    await_bytes(d_b, a2a_ss.at[1])

    def time_backward(h):
        for b in range(2):
            weights = tw[h, b]
            cot = band(oc_r, h, b)
            put_band(c_b, h, b, mm(weights.astype(B16), cot, 1, 0).astype(B16))
            prob = mm(band(so_r, h, b), cot, 1, 1)
            centre = jnp.sum(weights * prob, axis=0, keepdims=True)
            grad = (weights * (prob - centre)).astype(B16)
            put_band(a_b, h, b, (mm(grad, band(tk_r, h, b), 0, 0) * SCALE).astype(B16))
            put_band(d_b, h, b, (mm(grad, band(tq_r, h, b), 1, 0) * SCALE).astype(B16))

    for g in range(GROUPS):
        for h in range(g * GH, (g + 1) * GH):
            time_backward(h)
        spread(c_b, group_cols[g], put_sc[g], 4, g)
        if g == 0:
            forward(whole, put_out, 7, 0)
        else:
            forward(group_cols[g - 1], put_sc[g - 1], 4, g - 1)

    spread(a_b, whole, put_tqg, 5, 0)

    await_bytes(b_b, a2a_ss.at[7])

    def space_backward(h):
        hs = pl.ds(h * HD, HD)
        weights = pw[h]
        cot = sc_r[:, hs]
        key = k_s[:, hs]
        prob = mm(v_s[:, hs], cot, 1, 1)
        centre = jnp.sum(weights * prob, axis=0, keepdims=True)
        grad = (weights * (prob - centre)).astype(B16)
        b_b[:, hs] = (mm(grad, key, 0, 0) * SCALE).astype(B16)
        dk = mm(grad, q_s[:, hs], 1, 0) * SCALE
        dv = mm(weights.astype(B16), cot, 1, 0)
        dk_f[:, hs] = dk[:ROWS]
        dv_f[:, hs] = dv[:ROWS]
        dk_x[:, hs] = dk[ROWS:].astype(B16)
        dv_x[:, hs] = dv[ROWS:].astype(B16)

    def backward_group(g):
        cols = pl.ds(g * GC, GC)
        await_bytes(sc_r.at[:, cols], sc_rs.at[g])
        for h in range(g * GH, (g + 1) * GH):
            space_backward(h)
        send(dk_x.at[:, cols], dk_r.at[:, cols], x_ss, x_rs.at[0, g], other)
        send(dv_x.at[:, cols], dv_r.at[:, cols], x_ss, x_rs.at[1, g], other)

    await_bytes(t_r, t_rs)
    tt[...] = t_r[...].T
    forward(group_cols[GROUPS - 1], put_sc[GROUPS - 1], 4, GROUPS - 1)
    await_bytes(u_half(y_m, 1), y_rs.at[3])
    await_bytes(u_half(y_p, 0), y_rs.at[2])
    y_f = (y + 2) % YS
    await_bytes(u_half(y_f, 0), y_rs.at[4])
    await_bytes(u_half(y_f, 1), y_rs.at[5])

    z = zh * 2 + zl

    def chip(k):
        zd = (z + k) % 4
        return zd // 2, zd % 2

    def weight_part(k):
        zd = (z + k) % 4
        part = mm(tt[...], u_s[:, rows(zd * 2 * COLS, 2 * COLS)], 1, 0)
        wgf[k, 0] = part[:, :COLS]
        wgf[k, 1] = part[:, COLS:]

    def pair_sum(k):
        await_bytes(crecv.at[k], c_rs.at[k])
        rsend[k] = (wgf[k, core] + crecv[k].astype(F32)).astype(B16)
        for step in range(1, 4):
            xd = (x + step) % 4
            send(rsend.at[k, rows(xd * SUB, SUB)], ra.at[x, k], r_ss.at[0], r_rs.at[0], dev(xd, y, zh, zl, core))
        if k > 0:
            zhd, zld = chip(k)
            send(rsend.at[k, pl.ds(SIDE, SIDE)], rb.at[z], r_ss.at[1], r_rs.at[1], dev(x, y, zhd, zld, core))

    order = (1, 2, 3, 0)
    for n, k in enumerate(order):
        weight_part(k)
        csend[k] = wgf[k, 1 - core].astype(B16)
        send(csend.at[k], crecv.at[k], c_ss, c_rs.at[k], other)
        if n > 0:
            pair_sum(order[n - 1])
    pair_sum(0)
    spread(d_b, whole, put_tkg, 6, 0)
    forward(whole, put_tqg, 5, 0)
    backward_group(0)

    for k in range(4):
        ra[x, k] = rsend[k, rows(x * SUB, SUB)]
    rb[z] = rsend[0, SIDE:]
    await_bytes(ra.at[pl.ds(0, 3)], r_rs.at[0])
    for k in range(4):
        total = ra[0, k].astype(F32)
        for n in range(1, 4):
            total = total + ra[n, k].astype(F32)
        sa[k] = total.astype(B16)
        if k > 0:
            zhd, zld = chip(k)
            send(sa.at[k], ra2.at[z], r_ss.at[2], r_rs.at[2], dev(x, y, zhd, zld, core))
    ra2[z] = sa[0]
    await_bytes(rb.at[pl.ds(0, 3)], r_rs.at[1])
    total = rb[0].astype(F32)
    for n in range(1, 4):
        total = total + rb[n].astype(F32)
    sb[...] = total.astype(B16)
    for step in range(1, 4):
        xd = (x + step) % 4
        send(sb.at[rows(xd * SUB, SUB)], rb2.at[x], r_ss.at[3], r_rs.at[3], dev(xd, y, zh, zl, core))
    rb2[x] = sb[rows(x * SUB, SUB)]
    backward_group(1)

    for part, (held, n) in enumerate(((ra2, 2), (rb2, 3))):
        await_bytes(held.at[pl.ds(0, 3)], r_rs.at[n])
        total = held[0].astype(F32)
        for k in range(1, 4):
            total = total + held[k].astype(F32)
        red[part * SUB:(part + 1) * SUB] = total.astype(B16)
    out_cols = rows(((zh * 2 + zl) * 2 + core) * COLS, COLS)
    zh_own, core_own = y // 2, y % 2
    for k in range(8):
        yd, zld = (y + k // 2) % YS, (zl + k) % 2
        mine = (yd == y) & (zh_own == zh) & (zld == zl) & (core_own == core)

        @pl.when(mine)
        def _():
            local(red, g_r.at[:, out_cols], g_rs)

        @pl.when(jnp.logical_not(mine))
        def _():
            send(red, g_r.at[:, out_cols], g_ss.at[k], g_rs, dev(x, yd, zh_own, zld, core_own))

    forward(whole, put_tkg, 6, 0)
    backward_group(2)
    backward_group(3)

    local(b_b, sqg_o.at[0], out_s.at[0])
    for g in range(GROUPS):
        cols = pl.ds(g * GC, GC)
        await_bytes(dk_r.at[:, cols], x_rs.at[0, g])
        await_bytes(dv_r.at[:, cols], x_rs.at[1, g])
    await_bytes(dk_x, x_ss)
    await_bytes(dv_x, x_ss)
    dk_x[...] = (dk_f[...] + dk_r[...].astype(F32)).astype(B16)
    local(dk_x, skg_o.at[0], out_s.at[1])
    dv_x[...] = (dv_f[...] + dv_r[...].astype(F32)).astype(B16)
    local(dv_x, svg_o.at[0], out_s.at[2])

    await_bytes(tqg_r, a2a_rs.at[5])
    local(tqg_r, tqg_o.at[0], out_s.at[3])
    await_bytes(tkg_r, a2a_rs.at[6])
    local(tkg_r, tkg_o.at[0], out_s.at[4])

    await_bytes(k_s.at[own_k], kv_ss.at[0])
    await_bytes(v_s.at[own_k], kv_ss.at[1])
    for i in range(6):
        await_bytes(u_half(0, 0), y_ss.at[i])
    await_bytes(c_b, a2a_ss.at[4])
    await_bytes(a_b, a2a_ss.at[5])
    await_bytes(d_b, a2a_ss.at[6])
    for unit in range(8):
        await_bytes(hop.at[unit], hop_ss.at[unit])
    await_bytes(csend, c_ss)
    for n, held in enumerate((ra, rb, ra2, rb2)):
        await_bytes(held.at[pl.ds(0, 3)], r_ss.at[n])
    for k in range(8):
        yd, zld = (y + k // 2) % YS, (zl + k) % 2
        mine = (yd == y) & (zh_own == zh) & (zld == zl) & (core_own == core)

        @pl.when(jnp.logical_not(mine))
        def _():
            await_bytes(red, g_ss.at[k])

    await_bytes(g_r, g_rs)
    local(g_r, wg_o, out_s.at[5])
    await_bytes(tqg_r, out_s.at[3])
    await_bytes(tkg_r, out_s.at[4])
    await_bytes(g_r, out_s.at[5])
    await_bytes(b_b, out_s.at[0])
    await_bytes(dk_x, out_s.at[1])
    await_bytes(dv_x, out_s.at[2])


def store(a, b, c, d, e, wg, a_o, b_o, c_o, d_o, e_o, wg_o, held, low, wide, loads, stores):
    ins = [
        pltpu.make_async_copy(src, dst, loads.at[i])
        for i, (src, dst) in enumerate(
            [(wg, low)] + [(r, held.at[pl.ds(k, 1)]) for k, r in enumerate((a, b, c, d, e))]
        )
    ]
    outs = [pltpu.make_async_copy(wide, wg_o, stores.at[0])] + [
        pltpu.make_async_copy(held.at[pl.ds(k, 1)], r, stores.at[k + 1])
        for k, r in enumerate((a_o, b_o, c_o, d_o, e_o))
    ]
    for copy in ins:
        copy.start()
    for k, copy in enumerate(ins):
        copy.wait()
        if k == 0:
            wide[...] = low[...].astype(F32)
        outs[k].start()
    for copy in outs:
        copy.wait()


def local(qs, ks, vs, qt, kt, up, w, mask):
    hbm = pl.BlockSpec(memory_space=pl.ANY)
    vm = pltpu.VMEM
    dma = pltpu.SemaphoreType.DMA
    unit = jax.ShapeDtypeStruct((1, ROWS, HH), B16)
    own = vm((ROWS, HH), B16)
    outs = pl.pallas_call(
        kernel,
        out_shape=(unit,) * 5 + (jax.ShapeDtypeStruct((OUT_ROWS, D), B16),),
        in_specs=[hbm] * 7 + [pl.BlockSpec(memory_space=pltpu.VMEM)],
        out_specs=(hbm,) * 6,
        scratch_shapes=[
            own, vm((P_SIZE, HH), B16), vm((P_SIZE, HH), B16), vm((HH, D), B16),
            vm((YS * ROWS, D), B16), own, own, own, own, own, vm((YS * ROWS, BLOCK), B16),
            own, own, own, own,
            vm((HEADS, P_SIZE, ROWS), F32), vm((HEADS, 2, GROUP, GROUP), F32),
            vm((P_SIZE, ROWS), F32), vm((GROUP, GROUP), F32),
            vm((BLOCK, YS * ROWS), B16), vm((4, 2, BLOCK, COLS), F32),
            vm((4, BLOCK, COLS), B16), vm((4, BLOCK, COLS), B16),
            vm((4, BLOCK, COLS), B16), vm((4, 4, SUB, COLS), B16), vm((4, SIDE, COLS), B16),
            vm((4, SUB, COLS), B16), vm((4, SUB, COLS), B16), vm((4, SUB, COLS), B16),
            vm((SIDE, COLS), B16), vm((OUT_ROWS, COLS), B16),
            vm((ROWS, HH), F32), vm((ROWS, HH), F32), own, own, own, own,
            vm((8, 2 * PIX, HH), B16), vm((GROUPS, ROWS, GC), F32),
            own, own, vm((OUT_ROWS, D), B16),
            dma((6 + WCH,)), dma((2,)), dma((2,)), dma((6,)), dma((6,)), dma((8,)), dma((7,)),
            dma((GROUPS,)), dma((GROUPS,)), dma, dma((8,)), dma((8, GROUPS)), dma, dma((4,)), dma((4,)), dma((4,)),
            dma((8,)), dma, dma, dma((2, GROUPS)), dma((6,)),
        ],
        compiler_params=pltpu.CompilerParams(
            has_side_effects=True, vmem_limit_bytes=62 * 1024 * 1024
        ),
        cost_estimate=pl.CostEstimate(
            flops=8 * 10**9, bytes_accessed=20 * 10**6, transcendentals=3 * 10**6
        ),
    )(qs, ks, vs, qt, kt, up, w, mask)
    return pl.pallas_call(
        store,
        out_shape=(unit,) * 5 + (jax.ShapeDtypeStruct((OUT_ROWS, D), F32),),
        in_specs=[hbm] * 6,
        out_specs=(hbm,) * 6,
        scratch_shapes=[
            vm((5, ROWS, HH), B16), vm((OUT_ROWS, D), B16), vm((OUT_ROWS, D), F32), dma((6,)), dma((6,)),
        ],
        compiler_params=pltpu.CompilerParams(vmem_limit_bytes=62 * 1024 * 1024),
    )(*outs)


def solution(mesh):
    tokens = P("dp", "seq", None)
    return jax.shard_map(
        local,
        mesh=mesh,
        in_specs=(tokens,) * 6 + (P(), P()),
        out_specs=(tokens,) * 5 + (P("seq", None),),
        check_vma=False,
    )
```

```python
import math

import jax
import jax.numpy as jnp
from jax import lax
from jax.experimental import pallas as pl
from jax.experimental.pallas import tpu as pltpu
from jax.sharding import PartitionSpec as P

HEADS = 12
HD = 128
HH = HEADS * HD
D = 3072
ROWS = 256
P_SIZE = 512
TILE = 32
NT = 16
FRAMES = 8
PIX = ROWS // FRAMES
HALF = PIX // 2
YS = 4
BLOCK = HH // YS
COLS = D // 8
OUT_ROWS = 96
SUB = OUT_ROWS // 2
SIDE = BLOCK // 2
GROUPS = 4
GH = HEADS // GROUPS
GC = GH * HD
WCH = 6
WROWS = HH // WCH
SCALE = 1.0 / math.sqrt(HD)
POWER = SCALE / math.log(2.0)
NEG = -1e30
BAND = PIX // 2
GROUP = ROWS // 2
MESH = pl.DeviceIdType.MESH
F32 = jnp.float32
B16 = jnp.bfloat16


def mm(a, b, ca, cb):
    return lax.dot_general(a, b, (((ca,), (cb,)), ((), ())), preferred_element_type=F32)


def kernel(
    qs, ks, vs, qt, kt, up, w, mask,
    sqg_o, skg_o, svg_o, tqg_o, tkg_o, wg_o,
    q_s, k_s, v_s, w_s, u_s, tq_r, tk_r, so_r, oc_r, sc_r, t_r,
    a_b, b_b, c_b, d_b, pw, tw, bias, tbias, tt, wgf, csend, crecv, rsend, ra, rb, ra2, rb2, sa, sb, red,
    dk_f, dv_f, dk_x, dv_x, dk_r, dv_r, hop, t_f, tqg_r, tkg_r, g_r,
    ld, kv_ss, kv_rs, y_ss, y_rs, a2a_ss, a2a_rs, so_rs, sc_rs, t_rs, hop_ss, hop_rs,
    c_ss, c_rs, r_ss, r_rs, g_ss, g_rs, x_ss, x_rs, out_s,
):
    dp = lax.axis_index("dp")
    seq = lax.axis_index("seq")
    y, zl = dp // 2, dp % 2
    x, zh, core = seq // 4, (seq // 2) % 2, seq % 2
    frame = x * 2 + zh

    def dev(x_, y_, zh_, zl_, c_):
        return {"dp": y_ * 2 + zl_, "seq": x_ * 4 + zh_ * 2 + c_}

    def send(src, dst, ss, rs, to):
        pltpu.make_async_remote_copy(
            src_ref=src, dst_ref=dst, send_sem=ss, recv_sem=rs, device_id=to, device_id_type=MESH
        ).start()

    def await_bytes(ref, sem):
        pltpu.make_async_copy(ref, ref, sem).wait()

    def local(src, dst, sem):
        pltpu.make_async_copy(src, dst, sem).start()

    def rows(start, size):
        return pl.ds(pl.multiple_of(start, size), size)

    def spread(src, cols, put, unit, part):
        for zd in range(2):
            for side in range(2):
                far = ((x + 2) % 4 * 2 + zd) * PIX + side * HALF
                send(
                    src.at[rows(far, HALF), cols],
                    hop.at[unit, rows(side * PIX + zh * HALF, HALF), cols],
                    a2a_ss.at[unit], hop_rs.at[unit, part],
                    dev((x + 1 + 2 * side) % 4, y, zd, 1 - zl, core),
                )
        for step in (1, 3, 0):
            xd = (x + step) % 4
            for zd in range(2):
                put(
                    src, rows((xd * 2 + zd) * PIX, PIX), frame * PIX, PIX, a2a_ss.at[unit],
                    xd, zd, 1 - zl,
                )

    def forward(cols, put, unit, part):
        await_bytes(hop.at[unit, :, cols], hop_rs.at[unit, part])
        for side in range(2):
            came = (x + 3 + 2 * side) % 4
            for zs in range(2):
                put(
                    hop.at[unit], pl.ds(side * PIX + zs * HALF, HALF),
                    (came * 2 + zs) * PIX + side * HALF, HALF, hop_ss.at[unit],
                    (x + 1 + 2 * side) % 4, zh, zl,
                )

    def putter(dst, cols, rs):
        def put(src, src_rows, start, size, ss, xd, zd, zld):
            send(
                src.at[src_rows, cols], dst.at[rows(start, size), cols], ss, rs,
                dev(xd, y, zd, zld, core),
            )

        return put

    whole = pl.ds(0, HH)
    group_cols = [pl.ds(g * GC, GC) for g in range(GROUPS)]
    put_tq = putter(tq_r, whole, a2a_rs.at[0])
    put_tk = putter(tk_r, whole, a2a_rs.at[1])
    put_oc = putter(oc_r, whole, a2a_rs.at[2])
    put_so = [putter(so_r, group_cols[g], so_rs.at[g]) for g in range(GROUPS)]
    put_sc = [putter(sc_r, group_cols[g], sc_rs.at[g]) for g in range(GROUPS)]
    put_tqg = putter(tqg_r, whole, a2a_rs.at[5])
    put_tkg = putter(tkg_r, whole, a2a_rs.at[6])

    def put_out(src, src_rows, start, size, ss, xd, zd, zld):
        for k in range(YS):
            yd = (y + k) % YS
            send(
                src.at[src_rows, rows(yd * BLOCK, BLOCK)], t_r.at[rows(y * ROWS + start, size)],
                ss, t_rs, dev(xd, yd, zd, zld, core),
            )

    other = dev(x, y, zh, zl, 1 - core)
    y_up = dev(x, (y + 1) % YS, zh, zl, core)
    y_dn = dev(x, (y + 3) % YS, zh, zl, core)

    cut = 160
    own_k, far_k = pl.ds(0, ROWS), pl.ds(ROWS, ROWS)
    own_u = pl.ds(pl.multiple_of(y * ROWS, ROWS), ROWS)

    def u_half(owner, part):
        start, size = (0, cut) if part == 0 else (cut, ROWS - cut)
        return u_s.at[pl.ds(pl.multiple_of(owner * ROWS + start, PIX), size)]

    loads = (
        (ks.at[0], k_s.at[own_k]), (vs.at[0], v_s.at[own_k]), (qt.at[0], b_b), (kt.at[0], d_b),
        (up.at[0], u_s.at[own_u]), (qs.at[0], q_s),
    )
    for i, (src, dst) in enumerate(loads):
        local(src, dst, ld.at[i])
    for i in range(WCH):
        local(w.at[pl.ds(i * WROWS, WROWS)], w_s.at[pl.ds(i * WROWS, WROWS)], ld.at[6 + i])

    await_bytes(k_s.at[own_k], ld.at[0])
    send(k_s.at[own_k], k_s.at[far_k], kv_ss.at[0], kv_rs.at[0], other)
    await_bytes(v_s.at[own_k], ld.at[1])
    send(v_s.at[own_k], v_s.at[far_k], kv_ss.at[1], kv_rs.at[1], other)
    await_bytes(b_b, ld.at[2])
    spread(b_b, whole, put_tq, 0, 0)
    await_bytes(u_s.at[own_u], ld.at[4])
    send(u_half(y, 0), u_half(y, 0), y_ss.at[0], y_rs.at[0], y_up)
    send(u_half(y, 1), u_half(y, 1), y_ss.at[1], y_rs.at[1], y_dn)
    await_bytes(d_b, ld.at[3])
    spread(d_b, whole, put_tk, 1, 0)
    send(u_half(y, 0), u_half(y, 0), y_ss.at[2], y_rs.at[2], y_dn)
    send(u_half(y, 1), u_half(y, 1), y_ss.at[3], y_rs.at[3], y_up)

    key_row = lax.broadcasted_iota(jnp.int32, (P_SIZE, NT), 0)
    key_tile = jnp.where(
        key_row < ROWS, core * (NT // 2) + key_row // TILE,
        (1 - core) * (NT // 2) + (key_row - ROWS) // TILE,
    )
    key_hot = (key_tile == lax.broadcasted_iota(jnp.int32, (P_SIZE, NT), 1)).astype(F32)
    query_tile = core * (NT // 2) + lax.broadcasted_iota(jnp.int32, (ROWS, NT), 0) // TILE
    query_hot = (query_tile == lax.broadcasted_iota(jnp.int32, (ROWS, NT), 1)).astype(F32)
    rows_mask = mm(query_hot, mask[...].astype(F32), 1, 0)
    bias[...] = jnp.where(mm(key_hot, rows_mask, 1, 1) > 0.5, 0.0, NEG)
    same = (
        lax.broadcasted_iota(jnp.int32, (GROUP, GROUP), 0) % BAND
        == lax.broadcasted_iota(jnp.int32, (GROUP, GROUP), 1) % BAND
    )
    tbias[...] = jnp.where(same, 0.0, NEG)

    for i in range(WCH):
        await_bytes(w_s.at[pl.ds(i * WROWS, WROWS)], ld.at[6 + i])
        c_b[:, pl.ds(i * WROWS, WROWS)] = mm(
            w_s[pl.ds(i * WROWS, WROWS), :], u_s[own_u, :], 1, 1
        ).T.astype(B16)

    await_bytes(q_s, ld.at[5])
    await_bytes(k_s.at[far_k], kv_rs.at[0])
    await_bytes(v_s.at[far_k], kv_rs.at[1])

    def space_forward(h):
        hs = pl.ds(h * HD, HD)
        scores = mm(k_s[:, hs], q_s[:, hs], 1, 1) + bias[...]
        powers = jnp.exp2((scores - jnp.max(scores, axis=0, keepdims=True)) * POWER)
        weights = powers * (1.0 / jnp.sum(powers, axis=0, keepdims=True))
        pw[h] = weights
        a_b[:, hs] = mm(weights.astype(B16), v_s[:, hs], 0, 0).astype(B16)

    for g in range(GROUPS):
        for h in range(g * GH, (g + 1) * GH):
            space_forward(h)
        spread(a_b, group_cols[g], put_so[g], 3, g)
        if g == 1:
            forward(whole, put_tq, 0, 0)
        if g == 3:
            forward(whole, put_tk, 1, 0)

    spread(c_b, whole, put_oc, 2, 0)

    y_m, y_p = (y + 3) % YS, (y + 1) % YS
    await_bytes(u_half(y_m, 0), y_rs.at[0])
    send(u_half(y_m, 0), u_half(y_m, 0), y_ss.at[4], y_rs.at[4], y_up)
    await_bytes(u_half(y_p, 1), y_rs.at[1])
    send(u_half(y_p, 1), u_half(y_p, 1), y_ss.at[5], y_rs.at[5], y_dn)

    await_bytes(tq_r, a2a_rs.at[0])
    await_bytes(tk_r, a2a_rs.at[1])

    def band(ref, h, b):
        hs = pl.ds(h * HD, HD)
        return jnp.concatenate(
            [ref[f * PIX + b * BAND:f * PIX + (b + 1) * BAND, hs] for f in range(FRAMES)], axis=0
        )

    def put_band(ref, h, b, value):
        hs = pl.ds(h * HD, HD)
        for f in range(FRAMES):
            ref[f * PIX + b * BAND:f * PIX + (b + 1) * BAND, hs] = value[f * BAND:(f + 1) * BAND]

    def time_forward(h):
        for b in range(2):
            scores = mm(band(tk_r, h, b), band(tq_r, h, b), 1, 1) + tbias[...]
            powers = jnp.exp2((scores - jnp.max(scores, axis=0, keepdims=True)) * POWER)
            tw[h, b] = powers * (1.0 / jnp.sum(powers, axis=0, keepdims=True))

    for h in range(HEADS):
        time_forward(h)
    for g in range(GROUPS):
        forward(group_cols[g], put_so[g], 3, g)

    await_bytes(b_b, a2a_ss.at[0])
    for g in range(GROUPS):
        await_bytes(so_r.at[:, group_cols[g]], so_rs.at[g])
        for n in range(GH):
            h = g * GH + n
            for b in range(2):
                out = mm(tw[h, b].astype(B16), band(so_r, h, b), 0, 0)
                for f in range(FRAMES):
                    t_f[g, f * PIX + b * BAND:f * PIX + (b + 1) * BAND, n * HD:(n + 1) * HD] = (
                        out[f * BAND:(f + 1) * BAND]
                    )
    for k in range(YS):
        block = [
            t_f[g, :, k * OUT_ROWS + part * SUB:k * OUT_ROWS + (part + 1) * SUB]
            for part in range(2)
            for g in range(GROUPS)
        ]
        b_b[:, k * BLOCK:(k + 1) * BLOCK] = jnp.concatenate(block, axis=1).astype(B16)

    spread(b_b, whole, put_out, 7, 0)
    forward(whole, put_oc, 2, 0)

    await_bytes(oc_r, a2a_rs.at[2])
    await_bytes(c_b, a2a_ss.at[2])
    await_bytes(a_b, a2a_ss.at[3])
    await_bytes(d_b, a2a_ss.at[1])

    def time_backward(h):
        for b in range(2):
            weights = tw[h, b]
            cot = band(oc_r, h, b)
            put_band(c_b, h, b, mm(weights.astype(B16), cot, 1, 0).astype(B16))
            prob = mm(band(so_r, h, b), cot, 1, 1)
            centre = jnp.sum(weights * prob, axis=0, keepdims=True)
            grad = (weights * (prob - centre)).astype(B16)
            put_band(a_b, h, b, (mm(grad, band(tk_r, h, b), 0, 0) * SCALE).astype(B16))
            put_band(d_b, h, b, (mm(grad, band(tq_r, h, b), 1, 0) * SCALE).astype(B16))

    for g in range(GROUPS):
        for h in range(g * GH, (g + 1) * GH):
            time_backward(h)
        spread(c_b, group_cols[g], put_sc[g], 4, g)
        if g == 0:
            forward(whole, put_out, 7, 0)
        else:
            forward(group_cols[g - 1], put_sc[g - 1], 4, g - 1)

    spread(a_b, whole, put_tqg, 5, 0)
    forward(group_cols[GROUPS - 1], put_sc[GROUPS - 1], 4, GROUPS - 1)
    spread(d_b, whole, put_tkg, 6, 0)

    await_bytes(b_b, a2a_ss.at[7])

    def space_backward(h):
        hs = pl.ds(h * HD, HD)
        weights = pw[h]
        cot = sc_r[:, hs]
        key = k_s[:, hs]
        prob = mm(v_s[:, hs], cot, 1, 1)
        centre = jnp.sum(weights * prob, axis=0, keepdims=True)
        grad = (weights * (prob - centre)).astype(B16)
        b_b[:, hs] = (mm(grad, key, 0, 0) * SCALE).astype(B16)
        dk = mm(grad, q_s[:, hs], 1, 0) * SCALE
        dv = mm(weights.astype(B16), cot, 1, 0)
        dk_f[:, hs] = dk[:ROWS]
        dv_f[:, hs] = dv[:ROWS]
        dk_x[:, hs] = dk[ROWS:].astype(B16)
        dv_x[:, hs] = dv[ROWS:].astype(B16)

    def backward_group(g):
        cols = pl.ds(g * GC, GC)
        await_bytes(sc_r.at[:, cols], sc_rs.at[g])
        for h in range(g * GH, (g + 1) * GH):
            space_backward(h)
        send(dk_x.at[:, cols], dk_r.at[:, cols], x_ss, x_rs.at[0, g], other)
        send(dv_x.at[:, cols], dv_r.at[:, cols], x_ss, x_rs.at[1, g], other)

    backward_group(0)
    forward(whole, put_tqg, 5, 0)
    backward_group(1)
    forward(whole, put_tkg, 6, 0)

    await_bytes(t_r, t_rs)
    tt[...] = t_r[...].T
    await_bytes(u_half(y_m, 1), y_rs.at[3])
    await_bytes(u_half(y_p, 0), y_rs.at[2])
    y_f = (y + 2) % YS
    await_bytes(u_half(y_f, 0), y_rs.at[4])
    await_bytes(u_half(y_f, 1), y_rs.at[5])

    z = zh * 2 + zl

    def chip(k):
        zd = (z + k) % 4
        return zd // 2, zd % 2

    def weight_part(k):
        zd = (z + k) % 4
        part = mm(tt[...], u_s[:, rows(zd * 2 * COLS, 2 * COLS)], 1, 0)
        wgf[k, 0] = part[:, :COLS]
        wgf[k, 1] = part[:, COLS:]

    def pair_sum(k):
        await_bytes(crecv.at[k], c_rs.at[k])
        rsend[k] = (wgf[k, core] + crecv[k].astype(F32)).astype(B16)
        for step in range(1, 4):
            xd = (x + step) % 4
            send(rsend.at[k, rows(xd * SUB, SUB)], ra.at[x, k], r_ss.at[0], r_rs.at[0], dev(xd, y, zh, zl, core))
        if k > 0:
            zhd, zld = chip(k)
            send(rsend.at[k, pl.ds(SIDE, SIDE)], rb.at[z], r_ss.at[1], r_rs.at[1], dev(x, y, zhd, zld, core))

    order = (1, 2, 3, 0)
    for n, k in enumerate(order):
        weight_part(k)
        csend[k] = wgf[k, 1 - core].astype(B16)
        send(csend.at[k], crecv.at[k], c_ss, c_rs.at[k], other)
        if n > 0:
            pair_sum(order[n - 1])
    pair_sum(0)
    backward_group(2)

    for k in range(4):
        ra[x, k] = rsend[k, rows(x * SUB, SUB)]
    rb[z] = rsend[0, SIDE:]
    await_bytes(ra.at[pl.ds(0, 3)], r_rs.at[0])
    for k in range(4):
        total = ra[0, k].astype(F32)
        for n in range(1, 4):
            total = total + ra[n, k].astype(F32)
        sa[k] = total.astype(B16)
        if k > 0:
            zhd, zld = chip(k)
            send(sa.at[k], ra2.at[z], r_ss.at[2], r_rs.at[2], dev(x, y, zhd, zld, core))
    ra2[z] = sa[0]
    await_bytes(rb.at[pl.ds(0, 3)], r_rs.at[1])
    total = rb[0].astype(F32)
    for n in range(1, 4):
        total = total + rb[n].astype(F32)
    sb[...] = total.astype(B16)
    for step in range(1, 4):
        xd = (x + step) % 4
        send(sb.at[rows(xd * SUB, SUB)], rb2.at[x], r_ss.at[3], r_rs.at[3], dev(xd, y, zh, zl, core))
    rb2[x] = sb[rows(x * SUB, SUB)]
    backward_group(3)

    for part, (held, n) in enumerate(((ra2, 2), (rb2, 3))):
        await_bytes(held.at[pl.ds(0, 3)], r_rs.at[n])
        total = held[0].astype(F32)
        for k in range(1, 4):
            total = total + held[k].astype(F32)
        red[part * SUB:(part + 1) * SUB] = total.astype(B16)
    out_cols = rows(((zh * 2 + zl) * 2 + core) * COLS, COLS)
    zh_own, core_own = y // 2, y % 2
    for k in range(8):
        yd, zld = (y + k // 2) % YS, (zl + k) % 2
        mine = (yd == y) & (zh_own == zh) & (zld == zl) & (core_own == core)

        @pl.when(mine)
        def _():
            local(red, g_r.at[:, out_cols], g_rs)

        @pl.when(jnp.logical_not(mine))
        def _():
            send(red, g_r.at[:, out_cols], g_ss.at[k], g_rs, dev(x, yd, zh_own, zld, core_own))

    local(b_b, sqg_o.at[0], out_s.at[0])
    for g in range(GROUPS):
        cols = pl.ds(g * GC, GC)
        await_bytes(dk_r.at[:, cols], x_rs.at[0, g])
        await_bytes(dv_r.at[:, cols], x_rs.at[1, g])
    await_bytes(dk_x, x_ss)
    await_bytes(dv_x, x_ss)
    dk_x[...] = (dk_f[...] + dk_r[...].astype(F32)).astype(B16)
    local(dk_x, skg_o.at[0], out_s.at[1])
    dv_x[...] = (dv_f[...] + dv_r[...].astype(F32)).astype(B16)
    local(dv_x, svg_o.at[0], out_s.at[2])

    await_bytes(tqg_r, a2a_rs.at[5])
    local(tqg_r, tqg_o.at[0], out_s.at[3])
    await_bytes(tkg_r, a2a_rs.at[6])
    local(tkg_r, tkg_o.at[0], out_s.at[4])

    await_bytes(k_s.at[own_k], kv_ss.at[0])
    await_bytes(v_s.at[own_k], kv_ss.at[1])
    for i, part in enumerate((0, 1, 0, 1, 0, 1)):
        await_bytes(u_half(0, part), y_ss.at[i])
    await_bytes(c_b, a2a_ss.at[4])
    await_bytes(a_b, a2a_ss.at[5])
    await_bytes(d_b, a2a_ss.at[6])
    for unit in range(8):
        await_bytes(hop.at[unit], hop_ss.at[unit])
    await_bytes(csend, c_ss)
    for n, held in enumerate((ra, rb, ra2, rb2)):
        await_bytes(held.at[pl.ds(0, 3)], r_ss.at[n])
    for k in range(8):
        yd, zld = (y + k // 2) % YS, (zl + k) % 2
        mine = (yd == y) & (zh_own == zh) & (zld == zl) & (core_own == core)

        @pl.when(jnp.logical_not(mine))
        def _():
            await_bytes(red, g_ss.at[k])

    await_bytes(g_r, g_rs)
    local(g_r, wg_o, out_s.at[5])
    await_bytes(tqg_r, out_s.at[3])
    await_bytes(tkg_r, out_s.at[4])
    await_bytes(g_r, out_s.at[5])
    await_bytes(b_b, out_s.at[0])
    await_bytes(dk_x, out_s.at[1])
    await_bytes(dv_x, out_s.at[2])


def store(a, b, c, d, e, wg, a_o, b_o, c_o, d_o, e_o, wg_o, held, low, wide, loads, stores):
    ins = [
        pltpu.make_async_copy(src, dst, loads.at[i])
        for i, (src, dst) in enumerate(
            [(wg, low)] + [(r, held.at[pl.ds(k, 1)]) for k, r in enumerate((a, b, c, d, e))]
        )
    ]
    outs = [pltpu.make_async_copy(wide, wg_o, stores.at[0])] + [
        pltpu.make_async_copy(held.at[pl.ds(k, 1)], r, stores.at[k + 1])
        for k, r in enumerate((a_o, b_o, c_o, d_o, e_o))
    ]
    for copy in ins:
        copy.start()
    for k, copy in enumerate(ins):
        copy.wait()
        if k == 0:
            wide[...] = low[...].astype(F32)
        outs[k].start()
    for copy in outs:
        copy.wait()


def local(qs, ks, vs, qt, kt, up, w, mask):
    hbm = pl.BlockSpec(memory_space=pl.ANY)
    vm = pltpu.VMEM
    dma = pltpu.SemaphoreType.DMA
    unit = jax.ShapeDtypeStruct((1, ROWS, HH), B16)
    own = vm((ROWS, HH), B16)
    outs = pl.pallas_call(
        kernel,
        out_shape=(unit,) * 5 + (jax.ShapeDtypeStruct((OUT_ROWS, D), B16),),
        in_specs=[hbm] * 7 + [pl.BlockSpec(memory_space=pltpu.VMEM)],
        out_specs=(hbm,) * 6,
        scratch_shapes=[
            own, vm((P_SIZE, HH), B16), vm((P_SIZE, HH), B16), vm((HH, D), B16),
            vm((YS * ROWS, D), B16), own, own, own, own, own, vm((YS * ROWS, BLOCK), B16),
            own, own, own, own,
            vm((HEADS, P_SIZE, ROWS), F32), vm((HEADS, 2, GROUP, GROUP), F32),
            vm((P_SIZE, ROWS), F32), vm((GROUP, GROUP), F32),
            vm((BLOCK, YS * ROWS), B16), vm((4, 2, BLOCK, COLS), F32),
            vm((4, BLOCK, COLS), B16), vm((4, BLOCK, COLS), B16),
            vm((4, BLOCK, COLS), B16), vm((4, 4, SUB, COLS), B16), vm((4, SIDE, COLS), B16),
            vm((4, SUB, COLS), B16), vm((4, SUB, COLS), B16), vm((4, SUB, COLS), B16),
            vm((SIDE, COLS), B16), vm((OUT_ROWS, COLS), B16),
            vm((ROWS, HH), F32), vm((ROWS, HH), F32), own, own, own, own,
            vm((8, 2 * PIX, HH), B16), vm((GROUPS, ROWS, GC), F32),
            own, own, vm((OUT_ROWS, D), B16),
            dma((6 + WCH,)), dma((2,)), dma((2,)), dma((6,)), dma((6,)), dma((8,)), dma((7,)),
            dma((GROUPS,)), dma((GROUPS,)), dma, dma((8,)), dma((8, GROUPS)), dma, dma((4,)), dma((4,)), dma((4,)),
            dma((8,)), dma, dma, dma((2, GROUPS)), dma((6,)),
        ],
        compiler_params=pltpu.CompilerParams(
            has_side_effects=True, vmem_limit_bytes=62 * 1024 * 1024
        ),
        cost_estimate=pl.CostEstimate(
            flops=8 * 10**9, bytes_accessed=20 * 10**6, transcendentals=3 * 10**6
        ),
    )(qs, ks, vs, qt, kt, up, w, mask)
    return pl.pallas_call(
        store,
        out_shape=(unit,) * 5 + (jax.ShapeDtypeStruct((OUT_ROWS, D), F32),),
        in_specs=[hbm] * 6,
        out_specs=(hbm,) * 6,
        scratch_shapes=[
            vm((5, ROWS, HH), B16), vm((OUT_ROWS, D), B16), vm((OUT_ROWS, D), F32), dma((6,)), dma((6,)),
        ],
        compiler_params=pltpu.CompilerParams(vmem_limit_bytes=62 * 1024 * 1024),
    )(*outs)


def solution(mesh):
    tokens = P("dp", "seq", None)
    return jax.shard_map(
        local,
        mesh=mesh,
        in_specs=(tokens,) * 6 + (P(), P()),
        out_specs=(tokens,) * 5 + (P("seq", None),),
        check_vma=False,
    )
```

```python
import math

import jax
import jax.numpy as jnp
from jax import lax
from jax.experimental import pallas as pl
from jax.experimental.pallas import tpu as pltpu
from jax.sharding import PartitionSpec as P

HEADS = 12
HD = 128
HH = HEADS * HD
D = 3072
ROWS = 256
P_SIZE = 512
TILE = 32
NT = 16
FRAMES = 8
PIX = ROWS // FRAMES
HALF = PIX // 2
YS = 4
BLOCK = HH // YS
COLS = D // 8
OUT_ROWS = 96
SUB = OUT_ROWS // 2
SIDE = BLOCK // 2
GROUPS = 4
GH = HEADS // GROUPS
GC = GH * HD
WCH = 6
WROWS = HH // WCH
SCALE = 1.0 / math.sqrt(HD)
POWER = SCALE / math.log(2.0)
NEG = -1e30
BAND = PIX // 2
GROUP = ROWS // 2
MESH = pl.DeviceIdType.MESH
F32 = jnp.float32
B16 = jnp.bfloat16


def mm(a, b, ca, cb):
    return lax.dot_general(a, b, (((ca,), (cb,)), ((), ())), preferred_element_type=F32)


def kernel(
    qs, ks, vs, qt, kt, up, w, mask,
    sqg_o, skg_o, svg_o, tqg_o, tkg_o, wg_o,
    q_s, k_s, v_s, w_s, u_s, tq_r, tk_r, so_r, oc_r, sc_r, t_r,
    a_b, b_b, c_b, d_b, pw, tw, bias, tbias, tt, wgf, csend, crecv, rsend, ra, rb, ra2, rb2, sa, sb, red,
    dk_f, dv_f, dk_x, dv_x, dk_r, dv_r, hop, t_f, tqg_r, tkg_r, g_r,
    ld, kv_ss, kv_rs, y_ss, y_rs, a2a_ss, a2a_rs, so_rs, sc_rs, t_rs, hop_ss, hop_rs,
    c_ss, c_rs, r_ss, r_rs, g_ss, g_rs, x_ss, x_rs, out_s,
):
    dp = lax.axis_index("dp")
    seq = lax.axis_index("seq")
    y, zl = dp // 2, dp % 2
    x, zh, core = seq // 4, (seq // 2) % 2, seq % 2
    frame = x * 2 + zh

    def dev(x_, y_, zh_, zl_, c_):
        return {"dp": y_ * 2 + zl_, "seq": x_ * 4 + zh_ * 2 + c_}

    def send(src, dst, ss, rs, to):
        pltpu.make_async_remote_copy(
            src_ref=src, dst_ref=dst, send_sem=ss, recv_sem=rs, device_id=to, device_id_type=MESH
        ).start()

    def await_bytes(ref, sem):
        pltpu.make_async_copy(ref, ref, sem).wait()

    def local(src, dst, sem):
        pltpu.make_async_copy(src, dst, sem).start()

    def rows(start, size):
        return pl.ds(pl.multiple_of(start, size), size)

    def spread(src, cols, put, unit, part):
        for zd in range(2):
            for side in range(2):
                far = ((x + 2) % 4 * 2 + zd) * PIX + side * HALF
                send(
                    src.at[rows(far, HALF), cols],
                    hop.at[unit, rows(side * PIX + zh * HALF, HALF), cols],
                    a2a_ss.at[unit], hop_rs.at[unit, part],
                    dev((x + 1 + 2 * side) % 4, y, zd, 1 - zl, core),
                )
        for step in (1, 3, 0):
            xd = (x + step) % 4
            for zd in range(2):
                put(
                    src, rows((xd * 2 + zd) * PIX, PIX), frame * PIX, PIX, a2a_ss.at[unit],
                    xd, zd, 1 - zl,
                )

    def forward(cols, put, unit, part):
        await_bytes(hop.at[unit, :, cols], hop_rs.at[unit, part])
        for side in range(2):
            came = (x + 3 + 2 * side) % 4
            for zs in range(2):
                put(
                    hop.at[unit], pl.ds(side * PIX + zs * HALF, HALF),
                    (came * 2 + zs) * PIX + side * HALF, HALF, hop_ss.at[unit],
                    (x + 1 + 2 * side) % 4, zh, zl,
                )

    def putter(dst, cols, rs):
        def put(src, src_rows, start, size, ss, xd, zd, zld):
            send(
                src.at[src_rows, cols], dst.at[rows(start, size), cols], ss, rs,
                dev(xd, y, zd, zld, core),
            )

        return put

    whole = pl.ds(0, HH)

    def group_cols(g):
        return rows(g * GC, GC)

    put_tq = putter(tq_r, whole, a2a_rs.at[0])
    put_tk = putter(tk_r, whole, a2a_rs.at[1])
    put_oc = putter(oc_r, whole, a2a_rs.at[2])

    def put_so(g):
        return putter(so_r, group_cols(g), so_rs.at[g])

    def put_sc(g):
        return putter(sc_r, group_cols(g), sc_rs.at[g])

    put_tqg = putter(tqg_r, whole, a2a_rs.at[5])
    put_tkg = putter(tkg_r, whole, a2a_rs.at[6])

    def put_out(src, src_rows, start, size, ss, xd, zd, zld):
        for k in range(YS):
            yd = (y + k) % YS
            send(
                src.at[src_rows, rows(yd * BLOCK, BLOCK)], t_r.at[rows(y * ROWS + start, size)],
                ss, t_rs, dev(xd, yd, zd, zld, core),
            )

    other = dev(x, y, zh, zl, 1 - core)
    y_up = dev(x, (y + 1) % YS, zh, zl, core)
    y_dn = dev(x, (y + 3) % YS, zh, zl, core)

    half = ROWS // 2
    own_k, far_k = pl.ds(0, ROWS), pl.ds(ROWS, ROWS)
    own_u = pl.ds(pl.multiple_of(y * ROWS, ROWS), ROWS)

    def u_half(owner, part):
        return u_s.at[pl.ds(pl.multiple_of(owner * ROWS + part * half, half), half)]

    loads = (
        (ks.at[0], k_s.at[own_k]), (vs.at[0], v_s.at[own_k]), (qt.at[0], b_b), (kt.at[0], d_b),
        (up.at[0], u_s.at[own_u]), (qs.at[0], q_s),
    )
    for i, (src, dst) in enumerate(loads):
        local(src, dst, ld.at[i])
    for i in range(WCH):
        local(w.at[pl.ds(i * WROWS, WROWS)], w_s.at[pl.ds(i * WROWS, WROWS)], ld.at[6 + i])

    await_bytes(k_s.at[own_k], ld.at[0])
    send(k_s.at[own_k], k_s.at[far_k], kv_ss.at[0], kv_rs.at[0], other)
    await_bytes(v_s.at[own_k], ld.at[1])
    send(v_s.at[own_k], v_s.at[far_k], kv_ss.at[1], kv_rs.at[1], other)
    await_bytes(b_b, ld.at[2])
    spread(b_b, whole, put_tq, 0, 0)
    await_bytes(u_s.at[own_u], ld.at[4])
    send(u_half(y, 0), u_half(y, 0), y_ss.at[0], y_rs.at[0], y_up)
    send(u_half(y, 1), u_half(y, 1), y_ss.at[1], y_rs.at[1], y_dn)
    await_bytes(d_b, ld.at[3])
    spread(d_b, whole, put_tk, 1, 0)
    send(u_half(y, 0), u_half(y, 0), y_ss.at[2], y_rs.at[2], y_dn)
    send(u_half(y, 1), u_half(y, 1), y_ss.at[3], y_rs.at[3], y_up)

    key_row = lax.broadcasted_iota(jnp.int32, (P_SIZE, NT), 0)
    key_tile = jnp.where(
        key_row < ROWS, core * (NT // 2) + key_row // TILE,
        (1 - core) * (NT // 2) + (key_row - ROWS) // TILE,
    )
    key_hot = (key_tile == lax.broadcasted_iota(jnp.int32, (P_SIZE, NT), 1)).astype(F32)
    query_tile = core * (NT // 2) + lax.broadcasted_iota(jnp.int32, (ROWS, NT), 0) // TILE
    query_hot = (query_tile == lax.broadcasted_iota(jnp.int32, (ROWS, NT), 1)).astype(F32)
    rows_mask = mm(query_hot, mask[...].astype(F32), 1, 0)
    bias[...] = jnp.where(mm(key_hot, rows_mask, 1, 1) > 0.5, 0.0, NEG)
    same = (
        lax.broadcasted_iota(jnp.int32, (GROUP, GROUP), 0) % BAND
        == lax.broadcasted_iota(jnp.int32, (GROUP, GROUP), 1) % BAND
    )
    tbias[...] = jnp.where(same, 0.0, NEG)

    def cot_chunk(i, carry):
        part = rows(i * WROWS, WROWS)
        await_bytes(w_s.at[part], ld.at[6 + i])
        c_b[:, part] = mm(w_s[part, :], u_s[own_u, :], 1, 1).T.astype(B16)
        return carry

    lax.fori_loop(0, WCH, cot_chunk, 0)

    await_bytes(q_s, ld.at[5])
    await_bytes(k_s.at[far_k], kv_rs.at[0])
    await_bytes(v_s.at[far_k], kv_rs.at[1])

    def space_forward(h):
        hs = rows(h * HD, HD)
        scores = mm(k_s[:, hs], q_s[:, hs], 1, 1) + bias[...]
        powers = jnp.exp2((scores - jnp.max(scores, axis=0, keepdims=True)) * POWER)
        weights = powers * (1.0 / jnp.sum(powers, axis=0, keepdims=True))
        pw[h] = weights
        a_b[:, hs] = mm(weights.astype(B16), v_s[:, hs], 0, 0).astype(B16)

    def space_group(g, carry):
        for n in range(GH):
            space_forward(g * GH + n)
        spread(a_b, group_cols(g), put_so(g), 3, g)
        return carry

    lax.fori_loop(0, GROUPS, space_group, 0)
    forward(whole, put_tq, 0, 0)
    forward(whole, put_tk, 1, 0)
    spread(c_b, whole, put_oc, 2, 0)

    await_bytes(tq_r, a2a_rs.at[0])
    await_bytes(tk_r, a2a_rs.at[1])

    def band(ref, h, b):
        hs = rows(h * HD, HD)
        return jnp.concatenate(
            [ref[f * PIX + b * BAND:f * PIX + (b + 1) * BAND, hs] for f in range(FRAMES)], axis=0
        )

    def put_band(ref, h, b, value):
        hs = rows(h * HD, HD)
        for f in range(FRAMES):
            ref[f * PIX + b * BAND:f * PIX + (b + 1) * BAND, hs] = value[f * BAND:(f + 1) * BAND]

    def time_forward(h):
        for b in range(2):
            scores = mm(band(tk_r, h, b), band(tq_r, h, b), 1, 1) + tbias[...]
            powers = jnp.exp2((scores - jnp.max(scores, axis=0, keepdims=True)) * POWER)
            tw[h, b] = powers * (1.0 / jnp.sum(powers, axis=0, keepdims=True))

    def time_group(g, carry):
        for n in range(GH):
            time_forward(g * GH + n)
        return carry

    lax.fori_loop(0, GROUPS, time_group, 0)

    def forward_space(g, carry):
        forward(group_cols(g), put_so(g), 3, g)
        return carry

    lax.fori_loop(0, GROUPS, forward_space, 0)

    y_m, y_p = (y + 3) % YS, (y + 1) % YS
    await_bytes(u_half(y_m, 0), y_rs.at[0])
    send(u_half(y_m, 0), u_half(y_m, 0), y_ss.at[4], y_rs.at[4], y_up)
    await_bytes(u_half(y_p, 1), y_rs.at[1])
    send(u_half(y_p, 1), u_half(y_p, 1), y_ss.at[5], y_rs.at[5], y_dn)

    await_bytes(b_b, a2a_ss.at[0])
    def apply_group(g, carry):
        await_bytes(so_r.at[:, group_cols(g)], so_rs.at[g])
        for n in range(GH):
            h = g * GH + n
            for b in range(2):
                out = mm(tw[h, b].astype(B16), band(so_r, h, b), 0, 0)
                for f in range(FRAMES):
                    t_f[g, f * PIX + b * BAND:f * PIX + (b + 1) * BAND, n * HD:(n + 1) * HD] = (
                        out[f * BAND:(f + 1) * BAND]
                    )
        return carry

    lax.fori_loop(0, GROUPS, apply_group, 0)
    for k in range(YS):
        block = [
            t_f[g, :, k * OUT_ROWS + part * SUB:k * OUT_ROWS + (part + 1) * SUB]
            for part in range(2)
            for g in range(GROUPS)
        ]
        b_b[:, k * BLOCK:(k + 1) * BLOCK] = jnp.concatenate(block, axis=1).astype(B16)

    spread(b_b, whole, put_out, 7, 0)
    forward(whole, put_oc, 2, 0)

    await_bytes(oc_r, a2a_rs.at[2])
    await_bytes(c_b, a2a_ss.at[2])
    await_bytes(a_b, a2a_ss.at[3])
    await_bytes(d_b, a2a_ss.at[1])

    def time_backward(h):
        for b in range(2):
            weights = tw[h, b]
            cot = band(oc_r, h, b)
            put_band(c_b, h, b, mm(weights.astype(B16), cot, 1, 0).astype(B16))
            prob = mm(band(so_r, h, b), cot, 1, 1)
            centre = jnp.sum(weights * prob, axis=0, keepdims=True)
            grad = (weights * (prob - centre)).astype(B16)
            put_band(a_b, h, b, (mm(grad, band(tk_r, h, b), 0, 0) * SCALE).astype(B16))
            put_band(d_b, h, b, (mm(grad, band(tq_r, h, b), 1, 0) * SCALE).astype(B16))

    def time_back_group(g, carry):
        for n in range(GH):
            time_backward(g * GH + n)
        spread(c_b, group_cols(g), put_sc(g), 4, g)

        @pl.when(g == 0)
        def _():
            forward(whole, put_out, 7, 0)

        @pl.when(g > 0)
        def _():
            forward(group_cols(g - 1), put_sc(g - 1), 4, g - 1)

        return carry

    lax.fori_loop(0, GROUPS, time_back_group, 0)
    spread(a_b, whole, put_tqg, 5, 0)

    await_bytes(b_b, a2a_ss.at[7])

    def space_backward(h):
        hs = rows(h * HD, HD)
        weights = pw[h]
        cot = sc_r[:, hs]
        key = k_s[:, hs]
        prob = mm(v_s[:, hs], cot, 1, 1)
        centre = jnp.sum(weights * prob, axis=0, keepdims=True)
        grad = (weights * (prob - centre)).astype(B16)
        b_b[:, hs] = (mm(grad, key, 0, 0) * SCALE).astype(B16)
        dk = mm(grad, q_s[:, hs], 1, 0) * SCALE
        dv = mm(weights.astype(B16), cot, 1, 0)
        dk_f[:, hs] = dk[:ROWS]
        dv_f[:, hs] = dv[:ROWS]
        dk_x[:, hs] = dk[ROWS:].astype(B16)
        dv_x[:, hs] = dv[ROWS:].astype(B16)

    def backward_group(g):
        cols = group_cols(g)
        await_bytes(sc_r.at[:, cols], sc_rs.at[g])
        for n in range(GH):
            space_backward(g * GH + n)
        send(dk_x.at[:, cols], dk_r.at[:, cols], x_ss, x_rs.at[0, g], other)
        send(dv_x.at[:, cols], dv_r.at[:, cols], x_ss, x_rs.at[1, g], other)

    await_bytes(t_r, t_rs)
    tt[...] = t_r[...].T
    forward(group_cols(GROUPS - 1), put_sc(GROUPS - 1), 4, GROUPS - 1)
    await_bytes(u_half(y_m, 1), y_rs.at[3])
    await_bytes(u_half(y_p, 0), y_rs.at[2])
    y_f = (y + 2) % YS
    await_bytes(u_half(y_f, 0), y_rs.at[4])
    await_bytes(u_half(y_f, 1), y_rs.at[5])

    z = zh * 2 + zl

    def chip(k):
        zd = (z + k) % 4
        return zd // 2, zd % 2

    def weight_part(k):
        zd = (z + k) % 4
        part = mm(tt[...], u_s[:, rows(zd * 2 * COLS, 2 * COLS)], 1, 0)
        wgf[k, 0] = part[:, :COLS]
        wgf[k, 1] = part[:, COLS:]

    def pair_sum(k, along_z):
        await_bytes(crecv.at[k], c_rs.at[k])
        rsend[k] = (wgf[k, core] + crecv[k].astype(F32)).astype(B16)
        for step in range(1, 4):
            xd = (x + step) % 4
            send(rsend.at[k, rows(xd * SUB, SUB)], ra.at[x, k], r_ss.at[0], r_rs.at[0], dev(xd, y, zh, zl, core))
        if along_z:
            zhd, zld = chip(k)
            send(rsend.at[k, pl.ds(SIDE, SIDE)], rb.at[z], r_ss.at[1], r_rs.at[1], dev(x, y, zhd, zld, core))

    def weight_step(n, carry):
        k = (n + 1) % 4
        weight_part(k)
        csend[k] = wgf[k, 1 - core].astype(B16)
        send(csend.at[k], crecv.at[k], c_ss, c_rs.at[k], other)

        @pl.when(n > 0)
        def _():
            pair_sum(n, True)

        return carry

    lax.fori_loop(0, 4, weight_step, 0)
    pair_sum(0, False)
    spread(d_b, whole, put_tkg, 6, 0)
    forward(whole, put_tqg, 5, 0)
    def first_stage():
        for k in range(4):
            ra[x, k] = rsend[k, rows(x * SUB, SUB)]
        rb[z] = rsend[0, SIDE:]
        await_bytes(ra.at[pl.ds(0, 3)], r_rs.at[0])
        for k in range(4):
            total = ra[0, k].astype(F32)
            for n in range(1, 4):
                total = total + ra[n, k].astype(F32)
            sa[k] = total.astype(B16)
            if k > 0:
                zhd, zld = chip(k)
                send(sa.at[k], ra2.at[z], r_ss.at[2], r_rs.at[2], dev(x, y, zhd, zld, core))
        ra2[z] = sa[0]
        await_bytes(rb.at[pl.ds(0, 3)], r_rs.at[1])
        total = rb[0].astype(F32)
        for n in range(1, 4):
            total = total + rb[n].astype(F32)
        sb[...] = total.astype(B16)
        for step in range(1, 4):
            xd = (x + step) % 4
            send(sb.at[rows(xd * SUB, SUB)], rb2.at[x], r_ss.at[3], r_rs.at[3], dev(xd, y, zh, zl, core))
        rb2[x] = sb[rows(x * SUB, SUB)]

    out_cols = rows((z * 2 + core) * COLS, COLS)
    zh_own, core_own = y // 2, y % 2

    def second_stage():
        for part, (held, n) in enumerate(((ra2, 2), (rb2, 3))):
            await_bytes(held.at[pl.ds(0, 3)], r_rs.at[n])
            total = held[0].astype(F32)
            for k in range(1, 4):
                total = total + held[k].astype(F32)
            red[part * SUB:(part + 1) * SUB] = total.astype(B16)
        for k in range(8):
            yd, zld = (y + k // 2) % YS, (zl + k) % 2
            mine = (yd == y) & (zh_own == zh) & (zld == zl) & (core_own == core)

            @pl.when(mine)
            def _():
                local(red, g_r.at[:, out_cols], g_rs)

            @pl.when(jnp.logical_not(mine))
            def _():
                send(red, g_r.at[:, out_cols], g_ss.at[k], g_rs, dev(x, yd, zh_own, zld, core_own))

    def backward_step(g, carry):
        backward_group(g)

        @pl.when(g == 0)
        def _():
            first_stage()

        @pl.when(g == 1)
        def _():
            second_stage()
            forward(whole, put_tkg, 6, 0)

        return carry

    lax.fori_loop(0, GROUPS, backward_step, 0)

    local(b_b, sqg_o.at[0], out_s.at[0])
    for g in range(GROUPS):
        cols = group_cols(g)
        await_bytes(dk_r.at[:, cols], x_rs.at[0, g])
        await_bytes(dv_r.at[:, cols], x_rs.at[1, g])
    await_bytes(dk_x, x_ss)
    await_bytes(dv_x, x_ss)
    dk_x[...] = (dk_f[...] + dk_r[...].astype(F32)).astype(B16)
    local(dk_x, skg_o.at[0], out_s.at[1])
    dv_x[...] = (dv_f[...] + dv_r[...].astype(F32)).astype(B16)
    local(dv_x, svg_o.at[0], out_s.at[2])

    await_bytes(tqg_r, a2a_rs.at[5])
    local(tqg_r, tqg_o.at[0], out_s.at[3])
    await_bytes(tkg_r, a2a_rs.at[6])
    local(tkg_r, tkg_o.at[0], out_s.at[4])

    await_bytes(k_s.at[own_k], kv_ss.at[0])
    await_bytes(v_s.at[own_k], kv_ss.at[1])
    for i in range(6):
        await_bytes(u_half(0, 0), y_ss.at[i])
    await_bytes(c_b, a2a_ss.at[4])
    await_bytes(a_b, a2a_ss.at[5])
    await_bytes(d_b, a2a_ss.at[6])
    for unit in range(8):
        await_bytes(hop.at[unit], hop_ss.at[unit])
    await_bytes(csend, c_ss)
    for n, held in enumerate((ra, rb, ra2, rb2)):
        await_bytes(held.at[pl.ds(0, 3)], r_ss.at[n])
    for k in range(8):
        yd, zld = (y + k // 2) % YS, (zl + k) % 2
        mine = (yd == y) & (zh_own == zh) & (zld == zl) & (core_own == core)

        @pl.when(jnp.logical_not(mine))
        def _():
            await_bytes(red, g_ss.at[k])

    await_bytes(g_r, g_rs)
    local(g_r, wg_o, out_s.at[5])
    await_bytes(tqg_r, out_s.at[3])
    await_bytes(tkg_r, out_s.at[4])
    await_bytes(g_r, out_s.at[5])
    await_bytes(b_b, out_s.at[0])
    await_bytes(dk_x, out_s.at[1])
    await_bytes(dv_x, out_s.at[2])


def store(a, b, c, d, e, wg, a_o, b_o, c_o, d_o, e_o, wg_o, held, low, wide, loads, stores):
    ins = [
        pltpu.make_async_copy(src, dst, loads.at[i])
        for i, (src, dst) in enumerate(
            [(wg, low)] + [(r, held.at[pl.ds(k, 1)]) for k, r in enumerate((a, b, c, d, e))]
        )
    ]
    outs = [pltpu.make_async_copy(wide, wg_o, stores.at[0])] + [
        pltpu.make_async_copy(held.at[pl.ds(k, 1)], r, stores.at[k + 1])
        for k, r in enumerate((a_o, b_o, c_o, d_o, e_o))
    ]
    for copy in ins:
        copy.start()
    for k, copy in enumerate(ins):
        copy.wait()
        if k == 0:
            wide[...] = low[...].astype(F32)
        outs[k].start()
    for copy in outs:
        copy.wait()


def local(qs, ks, vs, qt, kt, up, w, mask):
    hbm = pl.BlockSpec(memory_space=pl.ANY)
    vm = pltpu.VMEM
    dma = pltpu.SemaphoreType.DMA
    unit = jax.ShapeDtypeStruct((1, ROWS, HH), B16)
    own = vm((ROWS, HH), B16)
    outs = pl.pallas_call(
        kernel,
        out_shape=(unit,) * 5 + (jax.ShapeDtypeStruct((OUT_ROWS, D), B16),),
        in_specs=[hbm] * 7 + [pl.BlockSpec(memory_space=pltpu.VMEM)],
        out_specs=(hbm,) * 6,
        scratch_shapes=[
            own, vm((P_SIZE, HH), B16), vm((P_SIZE, HH), B16), vm((HH, D), B16),
            vm((YS * ROWS, D), B16), own, own, own, own, own, vm((YS * ROWS, BLOCK), B16),
            own, own, own, own,
            vm((HEADS, P_SIZE, ROWS), F32), vm((HEADS, 2, GROUP, GROUP), F32),
            vm((P_SIZE, ROWS), F32), vm((GROUP, GROUP), F32),
            vm((BLOCK, YS * ROWS), B16), vm((4, 2, BLOCK, COLS), F32),
            vm((4, BLOCK, COLS), B16), vm((4, BLOCK, COLS), B16),
            vm((4, BLOCK, COLS), B16), vm((4, 4, SUB, COLS), B16), vm((4, SIDE, COLS), B16),
            vm((4, SUB, COLS), B16), vm((4, SUB, COLS), B16), vm((4, SUB, COLS), B16),
            vm((SIDE, COLS), B16), vm((OUT_ROWS, COLS), B16),
            vm((ROWS, HH), F32), vm((ROWS, HH), F32), own, own, own, own,
            vm((8, 2 * PIX, HH), B16), vm((GROUPS, ROWS, GC), F32),
            own, own, vm((OUT_ROWS, D), B16),
            dma((6 + WCH,)), dma((2,)), dma((2,)), dma((6,)), dma((6,)), dma((8,)), dma((7,)),
            dma((GROUPS,)), dma((GROUPS,)), dma, dma((8,)), dma((8, GROUPS)), dma, dma((4,)), dma((4,)), dma((4,)),
            dma((8,)), dma, dma, dma((2, GROUPS)), dma((6,)),
        ],
        compiler_params=pltpu.CompilerParams(
            has_side_effects=True, vmem_limit_bytes=62 * 1024 * 1024
        ),
        cost_estimate=pl.CostEstimate(
            flops=8 * 10**9, bytes_accessed=20 * 10**6, transcendentals=3 * 10**6
        ),
    )(qs, ks, vs, qt, kt, up, w, mask)
    return pl.pallas_call(
        store,
        out_shape=(unit,) * 5 + (jax.ShapeDtypeStruct((OUT_ROWS, D), F32),),
        in_specs=[hbm] * 6,
        out_specs=(hbm,) * 6,
        scratch_shapes=[
            vm((5, ROWS, HH), B16), vm((OUT_ROWS, D), B16), vm((OUT_ROWS, D), F32), dma((6,)), dma((6,)),
        ],
        compiler_params=pltpu.CompilerParams(vmem_limit_bytes=62 * 1024 * 1024),
    )(*outs)


def solution(mesh):
    tokens = P("dp", "seq", None)
    return jax.shard_map(
        local,
        mesh=mesh,
        in_specs=(tokens,) * 6 + (P(), P()),
        out_specs=(tokens,) * 5 + (P("seq", None),),
        check_vma=False,
    )
```

```python
import math

import jax
import jax.numpy as jnp
from jax import lax
from jax.experimental import pallas as pl
from jax.experimental.pallas import tpu as pltpu
from jax.sharding import PartitionSpec as P

HEADS = 12
HD = 128
HH = HEADS * HD
D = 3072
ROWS = 256
P_SIZE = 512
TILE = 32
NT = 16
FRAMES = 8
PIX = ROWS // FRAMES
HALF = PIX // 2
YS = 4
BLOCK = HH // YS
COLS = D // 8
OUT_ROWS = 96
SUB = OUT_ROWS // 2
SIDE = BLOCK // 2
GROUPS = 4
GH = HEADS // GROUPS
GC = GH * HD
WCH = 6
WROWS = HH // WCH
SCALE = 1.0 / math.sqrt(HD)
POWER = SCALE / math.log(2.0)
NEG = -1e30
BAND = PIX // 2
GROUP = ROWS // 2
MESH = pl.DeviceIdType.MESH
F32 = jnp.float32
B16 = jnp.bfloat16


def mm(a, b, ca, cb):
    return lax.dot_general(a, b, (((ca,), (cb,)), ((), ())), preferred_element_type=F32)


def kernel(
    qs, ks, vs, qt, kt, up, w, mask,
    sqg_o, skg_o, svg_o, tqg_o, tkg_o, wg_o,
    q_s, k_s, v_s, w_s, u_s, tq_r, tk_r, so_r, oc_r, sc_r, t_r,
    a_b, b_b, c_b, d_b, pw, tw, bias, tbias, tt, wgf, csend, crecv, rsend, ra, rb, ra2, rb2, sa, sb, red,
    dk_f, dv_f, dk_x, dv_x, dk_r, dv_r, hop, t_f, tqg_r, tkg_r, g_r,
    ld, kv_ss, kv_rs, y_ss, y_rs, a2a_ss, a2a_rs, so_rs, sc_rs, t_rs, hop_ss, hop_rs,
    c_ss, c_rs, r_ss, r_rs, g_ss, g_rs, x_ss, x_rs, out_s,
):
    dp = lax.axis_index("dp")
    seq = lax.axis_index("seq")
    y, zl = dp // 2, dp % 2
    x, zh, core = seq // 4, (seq // 2) % 2, seq % 2
    frame = x * 2 + zh

    def dev(x_, y_, zh_, zl_, c_):
        return {"dp": y_ * 2 + zl_, "seq": x_ * 4 + zh_ * 2 + c_}

    def send(src, dst, ss, rs, to):
        pltpu.make_async_remote_copy(
            src_ref=src, dst_ref=dst, send_sem=ss, recv_sem=rs, device_id=to, device_id_type=MESH
        ).start()

    def send_pieces(src, dst, count, step, ss, rs, to):
        for i in range(0, count, step):
            send(src.at[pl.ds(i, step)], dst.at[pl.ds(i, step)], ss, rs, to)

    def await_bytes(ref, sem):
        pltpu.make_async_copy(ref, ref, sem).wait()

    def local(src, dst, sem):
        pltpu.make_async_copy(src, dst, sem).start()

    def rows(start, size):
        return pl.ds(pl.multiple_of(start, size), size)

    def spread(src, cols, put, unit, part):
        for zd in range(2):
            for side in range(2):
                far = ((x + 2) % 4 * 2 + zd) * PIX + side * HALF
                send(
                    src.at[rows(far, HALF), cols],
                    hop.at[unit, rows(side * PIX + zh * HALF, HALF), cols],
                    a2a_ss.at[unit], hop_rs.at[unit, part],
                    dev((x + 1 + 2 * side) % 4, y, zd, 1 - zl, core),
                )
        for step in (1, 3, 0):
            xd = (x + step) % 4
            for zd in range(2):
                put(
                    src, rows((xd * 2 + zd) * PIX, PIX), frame * PIX, PIX, a2a_ss.at[unit],
                    xd, zd, 1 - zl,
                )

    def forward(cols, put, unit, part):
        await_bytes(hop.at[unit, :, cols], hop_rs.at[unit, part])
        for side in range(2):
            came = (x + 3 + 2 * side) % 4
            for zs in range(2):
                put(
                    hop.at[unit], pl.ds(side * PIX + zs * HALF, HALF),
                    (came * 2 + zs) * PIX + side * HALF, HALF, hop_ss.at[unit],
                    (x + 1 + 2 * side) % 4, zh, zl,
                )

    def putter(dst, cols, rs):
        def put(src, src_rows, start, size, ss, xd, zd, zld):
            send(
                src.at[src_rows, cols], dst.at[rows(start, size), cols], ss, rs,
                dev(xd, y, zd, zld, core),
            )

        return put

    whole = pl.ds(0, HH)

    def group_cols(g):
        return rows(g * GC, GC)

    put_tq = putter(tq_r, whole, a2a_rs.at[0])
    put_tk = putter(tk_r, whole, a2a_rs.at[1])
    put_oc = putter(oc_r, whole, a2a_rs.at[2])

    def put_so(g):
        return putter(so_r, group_cols(g), so_rs.at[g])

    def put_sc(g):
        return putter(sc_r, group_cols(g), sc_rs.at[g])

    put_tqg = putter(tqg_r, whole, a2a_rs.at[5])
    put_tkg = putter(tkg_r, whole, a2a_rs.at[6])

    def put_out(src, src_rows, start, size, ss, xd, zd, zld):
        for k in range(YS):
            yd = (y + k) % YS
            send(
                src.at[src_rows, rows(yd * BLOCK, BLOCK)], t_r.at[rows(y * ROWS + start, size)],
                ss, t_rs, dev(xd, yd, zd, zld, core),
            )

    other = dev(x, y, zh, zl, 1 - core)
    y_up = dev(x, (y + 1) % YS, zh, zl, core)
    y_dn = dev(x, (y + 3) % YS, zh, zl, core)

    cut = 160
    own_k, far_k = pl.ds(0, ROWS), pl.ds(ROWS, ROWS)
    own_u = pl.ds(pl.multiple_of(y * ROWS, ROWS), ROWS)

    def u_half(owner, part):
        start, size = (0, cut) if part == 0 else (cut, ROWS - cut)
        return u_s.at[pl.ds(pl.multiple_of(owner * ROWS + start, PIX), size)]

    def send_upstream(owner, part, n, to):
        ref = u_half(owner, part)
        send_pieces(ref, ref, ref.shape[0], PIX, y_ss.at[n], y_rs.at[n], to)

    loads = (
        (ks.at[0], k_s.at[own_k]), (vs.at[0], v_s.at[own_k]), (qt.at[0], b_b), (kt.at[0], d_b),
        (up.at[0], u_s.at[own_u]), (qs.at[0], q_s),
    )
    for i, (src, dst) in enumerate(loads):
        local(src, dst, ld.at[i])
    for i in range(WCH):
        local(w.at[pl.ds(i * WROWS, WROWS)], w_s.at[pl.ds(i * WROWS, WROWS)], ld.at[6 + i])

    await_bytes(k_s.at[own_k], ld.at[0])
    send_pieces(k_s.at[own_k], k_s.at[far_k], ROWS, PIX, kv_ss.at[0], kv_rs.at[0], other)
    await_bytes(v_s.at[own_k], ld.at[1])
    send_pieces(v_s.at[own_k], v_s.at[far_k], ROWS, PIX, kv_ss.at[1], kv_rs.at[1], other)
    await_bytes(b_b, ld.at[2])
    spread(b_b, whole, put_tq, 0, 0)
    await_bytes(u_s.at[own_u], ld.at[4])
    send_upstream(y, 0, 0, y_up)
    send_upstream(y, 1, 1, y_dn)
    await_bytes(d_b, ld.at[3])
    spread(d_b, whole, put_tk, 1, 0)
    send_upstream(y, 0, 2, y_dn)
    send_upstream(y, 1, 3, y_up)

    key_row = lax.broadcasted_iota(jnp.int32, (P_SIZE, NT), 0)
    key_tile = jnp.where(
        key_row < ROWS, core * (NT // 2) + key_row // TILE,
        (1 - core) * (NT // 2) + (key_row - ROWS) // TILE,
    )
    key_hot = (key_tile == lax.broadcasted_iota(jnp.int32, (P_SIZE, NT), 1)).astype(F32)
    query_tile = core * (NT // 2) + lax.broadcasted_iota(jnp.int32, (ROWS, NT), 0) // TILE
    query_hot = (query_tile == lax.broadcasted_iota(jnp.int32, (ROWS, NT), 1)).astype(F32)
    rows_mask = mm(query_hot, mask[...].astype(F32), 1, 0)
    bias[...] = jnp.where(mm(key_hot, rows_mask, 1, 1) > 0.5, 0.0, NEG)
    same = (
        lax.broadcasted_iota(jnp.int32, (GROUP, GROUP), 0) % BAND
        == lax.broadcasted_iota(jnp.int32, (GROUP, GROUP), 1) % BAND
    )
    tbias[...] = jnp.where(same, 0.0, NEG)

    def cot_chunk(i, carry):
        part = rows(i * WROWS, WROWS)
        await_bytes(w_s.at[part], ld.at[6 + i])
        c_b[:, part] = mm(w_s[part, :], u_s[own_u, :], 1, 1).T.astype(B16)
        return carry

    lax.fori_loop(0, WCH, cot_chunk, 0)

    await_bytes(q_s, ld.at[5])
    await_bytes(k_s.at[far_k], kv_rs.at[0])
    await_bytes(v_s.at[far_k], kv_rs.at[1])

    def space_forward(h):
        hs = rows(h * HD, HD)
        scores = mm(k_s[:, hs], q_s[:, hs], 1, 1) + bias[...]
        powers = jnp.exp2((scores - jnp.max(scores, axis=0, keepdims=True)) * POWER)
        weights = powers * (1.0 / jnp.sum(powers, axis=0, keepdims=True))
        pw[h] = weights
        a_b[:, hs] = mm(weights.astype(B16), v_s[:, hs], 0, 0).astype(B16)

    def space_group(g, carry):
        for n in range(GH):
            space_forward(g * GH + n)
        spread(a_b, group_cols(g), put_so(g), 3, g)
        return carry

    lax.fori_loop(0, GROUPS, space_group, 0)
    forward(whole, put_tq, 0, 0)
    forward(whole, put_tk, 1, 0)
    spread(c_b, whole, put_oc, 2, 0)

    y_m, y_p = (y + 3) % YS, (y + 1) % YS
    await_bytes(u_half(y_m, 0), y_rs.at[0])
    send_upstream(y_m, 0, 4, y_up)
    await_bytes(u_half(y_p, 1), y_rs.at[1])
    send_upstream(y_p, 1, 5, y_dn)

    await_bytes(tq_r, a2a_rs.at[0])
    await_bytes(tk_r, a2a_rs.at[1])

    def band(ref, h, b):
        hs = rows(h * HD, HD)
        return jnp.concatenate(
            [ref[f * PIX + b * BAND:f * PIX + (b + 1) * BAND, hs] for f in range(FRAMES)], axis=0
        )

    def put_band(ref, h, b, value):
        hs = rows(h * HD, HD)
        for f in range(FRAMES):
            ref[f * PIX + b * BAND:f * PIX + (b + 1) * BAND, hs] = value[f * BAND:(f + 1) * BAND]

    def time_forward(h):
        for b in range(2):
            scores = mm(band(tk_r, h, b), band(tq_r, h, b), 1, 1) + tbias[...]
            powers = jnp.exp2((scores - jnp.max(scores, axis=0, keepdims=True)) * POWER)
            tw[h, b] = powers * (1.0 / jnp.sum(powers, axis=0, keepdims=True))

    def time_group(g, carry):
        for n in range(GH):
            time_forward(g * GH + n)
        return carry

    lax.fori_loop(0, GROUPS, time_group, 0)

    def forward_space(g, carry):
        forward(group_cols(g), put_so(g), 3, g)
        return carry

    lax.fori_loop(0, GROUPS, forward_space, 0)

    await_bytes(b_b, a2a_ss.at[0])
    def apply_group(g, carry):
        await_bytes(so_r.at[:, group_cols(g)], so_rs.at[g])
        for n in range(GH):
            h = g * GH + n
            for b in range(2):
                out = mm(tw[h, b].astype(B16), band(so_r, h, b), 0, 0)
                for f in range(FRAMES):
                    t_f[g, f * PIX + b * BAND:f * PIX + (b + 1) * BAND, n * HD:(n + 1) * HD] = (
                        out[f * BAND:(f + 1) * BAND]
                    )
        return carry

    lax.fori_loop(0, GROUPS, apply_group, 0)
    for k in range(YS):
        block = [
            t_f[g, :, k * OUT_ROWS + part * SUB:k * OUT_ROWS + (part + 1) * SUB]
            for part in range(2)
            for g in range(GROUPS)
        ]
        b_b[:, k * BLOCK:(k + 1) * BLOCK] = jnp.concatenate(block, axis=1).astype(B16)

    spread(b_b, whole, put_out, 7, 0)
    forward(whole, put_oc, 2, 0)

    await_bytes(oc_r, a2a_rs.at[2])
    await_bytes(c_b, a2a_ss.at[2])
    await_bytes(a_b, a2a_ss.at[3])
    await_bytes(d_b, a2a_ss.at[1])

    def time_backward(h):
        for b in range(2):
            weights = tw[h, b]
            cot = band(oc_r, h, b)
            put_band(c_b, h, b, mm(weights.astype(B16), cot, 1, 0).astype(B16))
            prob = mm(band(so_r, h, b), cot, 1, 1)
            centre = jnp.sum(weights * prob, axis=0, keepdims=True)
            grad = (weights * (prob - centre)).astype(B16)
            put_band(a_b, h, b, (mm(grad, band(tk_r, h, b), 0, 0) * SCALE).astype(B16))
            put_band(d_b, h, b, (mm(grad, band(tq_r, h, b), 1, 0) * SCALE).astype(B16))

    def time_back_group(g, carry):
        for n in range(GH):
            time_backward(g * GH + n)
        spread(c_b, group_cols(g), put_sc(g), 4, g)

        @pl.when(g == 0)
        def _():
            forward(whole, put_out, 7, 0)

        @pl.when(g > 0)
        def _():
            forward(group_cols(g - 1), put_sc(g - 1), 4, g - 1)

        return carry

    lax.fori_loop(0, GROUPS, time_back_group, 0)
    spread(a_b, whole, put_tqg, 5, 0)

    await_bytes(b_b, a2a_ss.at[7])

    def space_backward(h):
        hs = rows(h * HD, HD)
        weights = pw[h]
        cot = sc_r[:, hs]
        key = k_s[:, hs]
        prob = mm(v_s[:, hs], cot, 1, 1)
        centre = jnp.sum(weights * prob, axis=0, keepdims=True)
        grad = (weights * (prob - centre)).astype(B16)
        b_b[:, hs] = (mm(grad, key, 0, 0) * SCALE).astype(B16)
        dk = mm(grad, q_s[:, hs], 1, 0) * SCALE
        dv = mm(weights.astype(B16), cot, 1, 0)
        dk_f[:, hs] = dk[:ROWS]
        dv_f[:, hs] = dv[:ROWS]
        dk_x[:, hs] = dk[ROWS:].astype(B16)
        dv_x[:, hs] = dv[ROWS:].astype(B16)

    def backward_group(g):
        cols = group_cols(g)
        await_bytes(sc_r.at[:, cols], sc_rs.at[g])
        for n in range(GH):
            space_backward(g * GH + n)
        send_pieces(dk_x.at[:, cols], dk_r.at[:, cols], ROWS, 64, x_ss, x_rs.at[0, g], other)
        send_pieces(dv_x.at[:, cols], dv_r.at[:, cols], ROWS, 64, x_ss, x_rs.at[1, g], other)

    await_bytes(t_r, t_rs)
    tt[...] = t_r[...].T
    forward(group_cols(GROUPS - 1), put_sc(GROUPS - 1), 4, GROUPS - 1)
    await_bytes(u_half(y_m, 1), y_rs.at[3])
    await_bytes(u_half(y_p, 0), y_rs.at[2])
    y_f = (y + 2) % YS
    await_bytes(u_half(y_f, 0), y_rs.at[4])
    await_bytes(u_half(y_f, 1), y_rs.at[5])

    z = zh * 2 + zl

    def chip(k):
        zd = (z + k) % 4
        return zd // 2, zd % 2

    def weight_part(k):
        zd = (z + k) % 4
        part = mm(tt[...], u_s[:, rows(zd * 2 * COLS, 2 * COLS)], 1, 0)
        wgf[k, 0] = part[:, :COLS]
        wgf[k, 1] = part[:, COLS:]

    def pair_sum(k, along_z):
        await_bytes(crecv.at[k], c_rs.at[k])
        rsend[k] = (wgf[k, core] + crecv[k].astype(F32)).astype(B16)
        for step in range(1, 4):
            xd = (x + step) % 4
            send(rsend.at[k, rows(xd * SUB, SUB)], ra.at[x, k], r_ss.at[0], r_rs.at[0], dev(xd, y, zh, zl, core))
        if along_z:
            zhd, zld = chip(k)
            send(rsend.at[k, pl.ds(SIDE, SIDE)], rb.at[z], r_ss.at[1], r_rs.at[1], dev(x, y, zhd, zld, core))

    def weight_step(n, carry):
        k = (n + 1) % 4
        weight_part(k)
        csend[k] = wgf[k, 1 - core].astype(B16)
        send_pieces(csend.at[k], crecv.at[k], BLOCK, OUT_ROWS, c_ss, c_rs.at[k], other)

        @pl.when(n > 0)
        def _():
            pair_sum(n, True)

        return carry

    lax.fori_loop(0, 4, weight_step, 0)
    pair_sum(0, False)
    spread(d_b, whole, put_tkg, 6, 0)
    forward(whole, put_tqg, 5, 0)

    def first_stage():
        for k in range(4):
            ra[x, k] = rsend[k, rows(x * SUB, SUB)]
        rb[z] = rsend[0, SIDE:]
        await_bytes(ra.at[pl.ds(0, 3)], r_rs.at[0])
        for k in range(4):
            total = ra[0, k].astype(F32)
            for n in range(1, 4):
                total = total + ra[n, k].astype(F32)
            sa[k] = total.astype(B16)
            if k > 0:
                zhd, zld = chip(k)
                send(sa.at[k], ra2.at[z], r_ss.at[2], r_rs.at[2], dev(x, y, zhd, zld, core))
        ra2[z] = sa[0]
        await_bytes(rb.at[pl.ds(0, 3)], r_rs.at[1])
        total = rb[0].astype(F32)
        for n in range(1, 4):
            total = total + rb[n].astype(F32)
        sb[...] = total.astype(B16)
        for step in range(1, 4):
            xd = (x + step) % 4
            send(sb.at[rows(xd * SUB, SUB)], rb2.at[x], r_ss.at[3], r_rs.at[3], dev(xd, y, zh, zl, core))
        rb2[x] = sb[rows(x * SUB, SUB)]

    out_cols = rows((z * 2 + core) * COLS, COLS)
    zh_own, core_own = y // 2, y % 2

    def second_stage():
        for part, (held, n) in enumerate(((ra2, 2), (rb2, 3))):
            await_bytes(held.at[pl.ds(0, 3)], r_rs.at[n])
            total = held[0].astype(F32)
            for k in range(1, 4):
                total = total + held[k].astype(F32)
            red[part * SUB:(part + 1) * SUB] = total.astype(B16)
        for k in range(8):
            yd, zld = (y + k // 2) % YS, (zl + k) % 2
            mine = (yd == y) & (zh_own == zh) & (zld == zl) & (core_own == core)

            @pl.when(mine)
            def _():
                local(red, g_r.at[:, out_cols], g_rs)

            @pl.when(jnp.logical_not(mine))
            def _():
                send(red, g_r.at[:, out_cols], g_ss.at[k], g_rs, dev(x, yd, zh_own, zld, core_own))

    def backward_step(g, carry):
        backward_group(g)

        @pl.when(g == 0)
        def _():
            first_stage()

        @pl.when(g == 1)
        def _():
            second_stage()
            forward(whole, put_tkg, 6, 0)

        return carry

    lax.fori_loop(0, GROUPS, backward_step, 0)

    local(b_b, sqg_o.at[0], out_s.at[0])
    for g in range(GROUPS):
        cols = group_cols(g)
        await_bytes(dk_r.at[:, cols], x_rs.at[0, g])
        await_bytes(dv_r.at[:, cols], x_rs.at[1, g])
    await_bytes(dk_x, x_ss)
    await_bytes(dv_x, x_ss)
    dk_x[...] = (dk_f[...] + dk_r[...].astype(F32)).astype(B16)
    local(dk_x, skg_o.at[0], out_s.at[1])
    dv_x[...] = (dv_f[...] + dv_r[...].astype(F32)).astype(B16)
    local(dv_x, svg_o.at[0], out_s.at[2])

    await_bytes(tqg_r, a2a_rs.at[5])
    local(tqg_r, tqg_o.at[0], out_s.at[3])
    await_bytes(tkg_r, a2a_rs.at[6])
    local(tkg_r, tkg_o.at[0], out_s.at[4])

    await_bytes(k_s.at[own_k], kv_ss.at[0])
    await_bytes(v_s.at[own_k], kv_ss.at[1])
    for i, part in enumerate((0, 1, 0, 1, 0, 1)):
        await_bytes(u_half(0, part), y_ss.at[i])
    await_bytes(c_b, a2a_ss.at[4])
    await_bytes(a_b, a2a_ss.at[5])
    await_bytes(d_b, a2a_ss.at[6])
    for unit in range(8):
        await_bytes(hop.at[unit], hop_ss.at[unit])
    await_bytes(csend, c_ss)
    for n, held in enumerate((ra, rb, ra2, rb2)):
        await_bytes(held.at[pl.ds(0, 3)], r_ss.at[n])
    for k in range(8):
        yd, zld = (y + k // 2) % YS, (zl + k) % 2
        mine = (yd == y) & (zh_own == zh) & (zld == zl) & (core_own == core)

        @pl.when(jnp.logical_not(mine))
        def _():
            await_bytes(red, g_ss.at[k])

    await_bytes(g_r, g_rs)
    local(g_r, wg_o, out_s.at[5])
    await_bytes(tqg_r, out_s.at[3])
    await_bytes(tkg_r, out_s.at[4])
    await_bytes(g_r, out_s.at[5])
    await_bytes(b_b, out_s.at[0])
    await_bytes(dk_x, out_s.at[1])
    await_bytes(dv_x, out_s.at[2])


def store(a, b, c, d, e, wg, a_o, b_o, c_o, d_o, e_o, wg_o, held, low, wide, loads, stores):
    ins = [
        pltpu.make_async_copy(src, dst, loads.at[i])
        for i, (src, dst) in enumerate(
            [(wg, low)] + [(r, held.at[pl.ds(k, 1)]) for k, r in enumerate((a, b, c, d, e))]
        )
    ]
    outs = [pltpu.make_async_copy(wide, wg_o, stores.at[0])] + [
        pltpu.make_async_copy(held.at[pl.ds(k, 1)], r, stores.at[k + 1])
        for k, r in enumerate((a_o, b_o, c_o, d_o, e_o))
    ]
    for copy in ins:
        copy.start()
    for k, copy in enumerate(ins):
        copy.wait()
        if k == 0:
            wide[...] = low[...].astype(F32)
        outs[k].start()
    for copy in outs:
        copy.wait()


def local(qs, ks, vs, qt, kt, up, w, mask):
    hbm = pl.BlockSpec(memory_space=pl.ANY)
    vm = pltpu.VMEM
    dma = pltpu.SemaphoreType.DMA
    unit = jax.ShapeDtypeStruct((1, ROWS, HH), B16)
    own = vm((ROWS, HH), B16)
    outs = pl.pallas_call(
        kernel,
        out_shape=(unit,) * 5 + (jax.ShapeDtypeStruct((OUT_ROWS, D), B16),),
        in_specs=[hbm] * 7 + [pl.BlockSpec(memory_space=pltpu.VMEM)],
        out_specs=(hbm,) * 6,
        scratch_shapes=[
            own, vm((P_SIZE, HH), B16), vm((P_SIZE, HH), B16), vm((HH, D), B16),
            vm((YS * ROWS, D), B16), own, own, own, own, own, vm((YS * ROWS, BLOCK), B16),
            own, own, own, own,
            vm((HEADS, P_SIZE, ROWS), F32), vm((HEADS, 2, GROUP, GROUP), F32),
            vm((P_SIZE, ROWS), F32), vm((GROUP, GROUP), F32),
            vm((BLOCK, YS * ROWS), B16), vm((4, 2, BLOCK, COLS), F32),
            vm((4, BLOCK, COLS), B16), vm((4, BLOCK, COLS), B16),
            vm((4, BLOCK, COLS), B16), vm((4, 4, SUB, COLS), B16), vm((4, SIDE, COLS), B16),
            vm((4, SUB, COLS), B16), vm((4, SUB, COLS), B16), vm((4, SUB, COLS), B16),
            vm((SIDE, COLS), B16), vm((OUT_ROWS, COLS), B16),
            vm((ROWS, HH), F32), vm((ROWS, HH), F32), own, own, own, own,
            vm((8, 2 * PIX, HH), B16), vm((GROUPS, ROWS, GC), F32),
            own, own, vm((OUT_ROWS, D), B16),
            dma((6 + WCH,)), dma((2,)), dma((2,)), dma((6,)), dma((6,)), dma((8,)), dma((7,)),
            dma((GROUPS,)), dma((GROUPS,)), dma, dma((8,)), dma((8, GROUPS)), dma, dma((4,)), dma((4,)), dma((4,)),
            dma((8,)), dma, dma, dma((2, GROUPS)), dma((6,)),
        ],
        compiler_params=pltpu.CompilerParams(
            has_side_effects=True, vmem_limit_bytes=62 * 1024 * 1024
        ),
        cost_estimate=pl.CostEstimate(
            flops=8 * 10**9, bytes_accessed=20 * 10**6, transcendentals=3 * 10**6
        ),
    )(qs, ks, vs, qt, kt, up, w, mask)
    return pl.pallas_call(
        store,
        out_shape=(unit,) * 5 + (jax.ShapeDtypeStruct((OUT_ROWS, D), F32),),
        in_specs=[hbm] * 6,
        out_specs=(hbm,) * 6,
        scratch_shapes=[
            vm((5, ROWS, HH), B16), vm((OUT_ROWS, D), B16), vm((OUT_ROWS, D), F32), dma((6,)), dma((6,)),
        ],
        compiler_params=pltpu.CompilerParams(vmem_limit_bytes=62 * 1024 * 1024),
    )(*outs)


def solution(mesh):
    tokens = P("dp", "seq", None)
    return jax.shard_map(
        local,
        mesh=mesh,
        in_specs=(tokens,) * 6 + (P(), P()),
        out_specs=(tokens,) * 5 + (P("seq", None),),
        check_vma=False,
    )
```

```python
import math

import jax
import jax.numpy as jnp
from jax import lax
from jax.experimental import pallas as pl
from jax.experimental.pallas import tpu as pltpu
from jax.sharding import PartitionSpec as P

HEADS = 12
HD = 128
HH = HEADS * HD
D = 3072
ROWS = 256
P_SIZE = 512
TILE = 32
NT = 16
FRAMES = 8
PIX = ROWS // FRAMES
HALF = PIX // 2
YS = 4
BLOCK = HH // YS
COLS = D // 8
OUT_ROWS = 96
SUB = OUT_ROWS // 2
SIDE = BLOCK // 2
LONG = 32
SHORT = SUB - LONG
GROUPS = 4
GH = HEADS // GROUPS
GC = GH * HD
WCH = 6
WROWS = HH // WCH
SCALE = 1.0 / math.sqrt(HD)
POWER = SCALE / math.log(2.0)
NEG = -1e30
BAND = PIX // 2
GROUP = ROWS // 2
MESH = pl.DeviceIdType.MESH
F32 = jnp.float32
B16 = jnp.bfloat16


def mm(a, b, ca, cb):
    return lax.dot_general(a, b, (((ca,), (cb,)), ((), ())), preferred_element_type=F32)


def kernel(
    qs, ks, vs, qt, kt, up, w, mask,
    sqg_o, skg_o, svg_o, tqg_o, tkg_o, wg_o,
    q_s, k_s, v_s, w_s, u_s, tq_r, tk_r, so_r, oc_r, sc_r, t_r,
    a_b, b_b, c_b, d_b, pw, tw, bias, tbias, tt, wgf, csend, crecv, rsend, ra, rb, fx_up, fx_dn, fz, ra2, rb2, sa, sb, red,
    dk_f, dv_f, dk_x, dv_x, dk_r, dv_r, hop, t_f, tqg_r, tkg_r, g_r,
    ld, kv_ss, kv_rs, y_ss, y_rs, a2a_ss, a2a_rs, so_rs, sc_rs, t_rs, hop_ss, hop_rs,
    c_ss, c_rs, r_ss, r_rs, fx_rs, fz_rs, g_ss, g_rs, x_ss, x_rs, out_s,
):
    dp = lax.axis_index("dp")
    seq = lax.axis_index("seq")
    y, zl = dp // 2, dp % 2
    x, zh, core = seq // 4, (seq // 2) % 2, seq % 2
    frame = x * 2 + zh

    def dev(x_, y_, zh_, zl_, c_):
        return {"dp": y_ * 2 + zl_, "seq": x_ * 4 + zh_ * 2 + c_}

    def send(src, dst, ss, rs, to):
        pltpu.make_async_remote_copy(
            src_ref=src, dst_ref=dst, send_sem=ss, recv_sem=rs, device_id=to, device_id_type=MESH
        ).start()

    def await_bytes(ref, sem):
        pltpu.make_async_copy(ref, ref, sem).wait()

    def local(src, dst, sem):
        pltpu.make_async_copy(src, dst, sem).start()

    def rows(start, size):
        return pl.ds(pl.multiple_of(start, size), size)

    def spread(src, cols, put, unit, part):
        for zd in range(2):
            for side in range(2):
                far = ((x + 2) % 4 * 2 + zd) * PIX + side * HALF
                send(
                    src.at[rows(far, HALF), cols],
                    hop.at[unit, rows(side * PIX + zh * HALF, HALF), cols],
                    a2a_ss.at[unit], hop_rs.at[unit, part],
                    dev((x + 1 + 2 * side) % 4, y, zd, 1 - zl, core),
                )
        for step in (1, 3, 0):
            xd = (x + step) % 4
            for zd in range(2):
                put(
                    src, rows((xd * 2 + zd) * PIX, PIX), frame * PIX, PIX, a2a_ss.at[unit],
                    xd, zd, 1 - zl,
                )

    def forward(cols, put, unit, part):
        await_bytes(hop.at[unit, :, cols], hop_rs.at[unit, part])
        for side in range(2):
            came = (x + 3 + 2 * side) % 4
            for zs in range(2):
                put(
                    hop.at[unit], pl.ds(side * PIX + zs * HALF, HALF),
                    (came * 2 + zs) * PIX + side * HALF, HALF, hop_ss.at[unit],
                    (x + 1 + 2 * side) % 4, zh, zl,
                )

    def putter(dst, cols, rs):
        def put(src, src_rows, start, size, ss, xd, zd, zld):
            send(
                src.at[src_rows, cols], dst.at[rows(start, size), cols], ss, rs,
                dev(xd, y, zd, zld, core),
            )

        return put

    whole = pl.ds(0, HH)

    def group_cols(g):
        return rows(g * GC, GC)

    put_tq = putter(tq_r, whole, a2a_rs.at[0])
    put_tk = putter(tk_r, whole, a2a_rs.at[1])
    put_oc = putter(oc_r, whole, a2a_rs.at[2])

    def put_so(g):
        return putter(so_r, group_cols(g), so_rs.at[g])

    def put_sc(g):
        return putter(sc_r, group_cols(g), sc_rs.at[g])

    put_tqg = putter(tqg_r, whole, a2a_rs.at[5])
    put_tkg = putter(tkg_r, whole, a2a_rs.at[6])

    def put_out(src, src_rows, start, size, ss, xd, zd, zld):
        for k in range(YS):
            yd = (y + k) % YS
            send(
                src.at[src_rows, rows(yd * BLOCK, BLOCK)], t_r.at[rows(y * ROWS + start, size)],
                ss, t_rs, dev(xd, yd, zd, zld, core),
            )

    other = dev(x, y, zh, zl, 1 - core)
    y_up = dev(x, (y + 1) % YS, zh, zl, core)
    y_dn = dev(x, (y + 3) % YS, zh, zl, core)

    half = ROWS // 2
    own_k, far_k = pl.ds(0, ROWS), pl.ds(ROWS, ROWS)
    own_u = pl.ds(pl.multiple_of(y * ROWS, ROWS), ROWS)

    def u_half(owner, part):
        return u_s.at[pl.ds(pl.multiple_of(owner * ROWS + part * half, half), half)]

    loads = (
        (ks.at[0], k_s.at[own_k]), (vs.at[0], v_s.at[own_k]), (qt.at[0], b_b), (kt.at[0], d_b),
        (up.at[0], u_s.at[own_u]), (qs.at[0], q_s),
    )
    for i, (src, dst) in enumerate(loads):
        local(src, dst, ld.at[i])
    for i in range(WCH):
        local(w.at[pl.ds(i * WROWS, WROWS)], w_s.at[pl.ds(i * WROWS, WROWS)], ld.at[6 + i])

    await_bytes(k_s.at[own_k], ld.at[0])
    send(k_s.at[own_k], k_s.at[far_k], kv_ss.at[0], kv_rs.at[0], other)
    await_bytes(v_s.at[own_k], ld.at[1])
    send(v_s.at[own_k], v_s.at[far_k], kv_ss.at[1], kv_rs.at[1], other)
    await_bytes(b_b, ld.at[2])
    spread(b_b, whole, put_tq, 0, 0)
    await_bytes(u_s.at[own_u], ld.at[4])
    send(u_half(y, 0), u_half(y, 0), y_ss.at[0], y_rs.at[0], y_up)
    send(u_half(y, 1), u_half(y, 1), y_ss.at[1], y_rs.at[1], y_dn)
    await_bytes(d_b, ld.at[3])
    spread(d_b, whole, put_tk, 1, 0)
    send(u_half(y, 0), u_half(y, 0), y_ss.at[2], y_rs.at[2], y_dn)
    send(u_half(y, 1), u_half(y, 1), y_ss.at[3], y_rs.at[3], y_up)

    key_row = lax.broadcasted_iota(jnp.int32, (P_SIZE, NT), 0)
    key_tile = jnp.where(
        key_row < ROWS, core * (NT // 2) + key_row // TILE,
        (1 - core) * (NT // 2) + (key_row - ROWS) // TILE,
    )
    key_hot = (key_tile == lax.broadcasted_iota(jnp.int32, (P_SIZE, NT), 1)).astype(F32)
    query_tile = core * (NT // 2) + lax.broadcasted_iota(jnp.int32, (ROWS, NT), 0) // TILE
    query_hot = (query_tile == lax.broadcasted_iota(jnp.int32, (ROWS, NT), 1)).astype(F32)
    rows_mask = mm(query_hot, mask[...].astype(F32), 1, 0)
    bias[...] = jnp.where(mm(key_hot, rows_mask, 1, 1) > 0.5, 0.0, NEG)
    same = (
        lax.broadcasted_iota(jnp.int32, (GROUP, GROUP), 0) % BAND
        == lax.broadcasted_iota(jnp.int32, (GROUP, GROUP), 1) % BAND
    )
    tbias[...] = jnp.where(same, 0.0, NEG)

    def cot_chunk(i, carry):
        part = rows(i * WROWS, WROWS)
        await_bytes(w_s.at[part], ld.at[6 + i])
        c_b[:, part] = mm(w_s[part, :], u_s[own_u, :], 1, 1).T.astype(B16)
        return carry

    lax.fori_loop(0, WCH, cot_chunk, 0)

    await_bytes(q_s, ld.at[5])
    await_bytes(k_s.at[far_k], kv_rs.at[0])
    await_bytes(v_s.at[far_k], kv_rs.at[1])

    def space_forward(h):
        hs = rows(h * HD, HD)
        scores = mm(k_s[:, hs], q_s[:, hs], 1, 1) + bias[...]
        powers = jnp.exp2((scores - jnp.max(scores, axis=0, keepdims=True)) * POWER)
        weights = powers * (1.0 / jnp.sum(powers, axis=0, keepdims=True))
        pw[h] = weights
        a_b[:, hs] = mm(weights.astype(B16), v_s[:, hs], 0, 0).astype(B16)

    def space_group(g, carry):
        for n in range(GH):
            space_forward(g * GH + n)
        spread(a_b, group_cols(g), put_so(g), 3, g)
        return carry

    lax.fori_loop(0, GROUPS, space_group, 0)
    forward(whole, put_tq, 0, 0)
    forward(whole, put_tk, 1, 0)
    spread(c_b, whole, put_oc, 2, 0)

    await_bytes(tq_r, a2a_rs.at[0])
    await_bytes(tk_r, a2a_rs.at[1])

    def band(ref, h, b):
        hs = rows(h * HD, HD)
        return jnp.concatenate(
            [ref[f * PIX + b * BAND:f * PIX + (b + 1) * BAND, hs] for f in range(FRAMES)], axis=0
        )

    def put_band(ref, h, b, value):
        hs = rows(h * HD, HD)
        for f in range(FRAMES):
            ref[f * PIX + b * BAND:f * PIX + (b + 1) * BAND, hs] = value[f * BAND:(f + 1) * BAND]

    def time_forward(h):
        for b in range(2):
            scores = mm(band(tk_r, h, b), band(tq_r, h, b), 1, 1) + tbias[...]
            powers = jnp.exp2((scores - jnp.max(scores, axis=0, keepdims=True)) * POWER)
            tw[h, b] = powers * (1.0 / jnp.sum(powers, axis=0, keepdims=True))

    def time_group(g, carry):
        for n in range(GH):
            time_forward(g * GH + n)
        return carry

    lax.fori_loop(0, GROUPS, time_group, 0)

    def forward_space(g, carry):
        forward(group_cols(g), put_so(g), 3, g)
        return carry

    lax.fori_loop(0, GROUPS, forward_space, 0)

    y_m, y_p = (y + 3) % YS, (y + 1) % YS
    await_bytes(u_half(y_m, 0), y_rs.at[0])
    send(u_half(y_m, 0), u_half(y_m, 0), y_ss.at[4], y_rs.at[4], y_up)
    await_bytes(u_half(y_p, 1), y_rs.at[1])
    send(u_half(y_p, 1), u_half(y_p, 1), y_ss.at[5], y_rs.at[5], y_dn)

    await_bytes(b_b, a2a_ss.at[0])
    def apply_group(g, carry):
        await_bytes(so_r.at[:, group_cols(g)], so_rs.at[g])
        for n in range(GH):
            h = g * GH + n
            for b in range(2):
                out = mm(tw[h, b].astype(B16), band(so_r, h, b), 0, 0)
                for f in range(FRAMES):
                    t_f[g, f * PIX + b * BAND:f * PIX + (b + 1) * BAND, n * HD:(n + 1) * HD] = (
                        out[f * BAND:(f + 1) * BAND]
                    )
        return carry

    lax.fori_loop(0, GROUPS, apply_group, 0)
    for k in range(YS):
        block = [
            t_f[g, :, k * OUT_ROWS + part * SUB:k * OUT_ROWS + (part + 1) * SUB]
            for part in range(2)
            for g in range(GROUPS)
        ]
        b_b[:, k * BLOCK:(k + 1) * BLOCK] = jnp.concatenate(block, axis=1).astype(B16)

    spread(b_b, whole, put_out, 7, 0)
    forward(whole, put_oc, 2, 0)

    await_bytes(oc_r, a2a_rs.at[2])
    await_bytes(c_b, a2a_ss.at[2])
    await_bytes(a_b, a2a_ss.at[3])
    await_bytes(d_b, a2a_ss.at[1])

    def time_backward(h):
        for b in range(2):
            weights = tw[h, b]
            cot = band(oc_r, h, b)
            put_band(c_b, h, b, mm(weights.astype(B16), cot, 1, 0).astype(B16))
            prob = mm(band(so_r, h, b), cot, 1, 1)
            centre = jnp.sum(weights * prob, axis=0, keepdims=True)
            grad = (weights * (prob - centre)).astype(B16)
            put_band(a_b, h, b, (mm(grad, band(tk_r, h, b), 0, 0) * SCALE).astype(B16))
            put_band(d_b, h, b, (mm(grad, band(tq_r, h, b), 1, 0) * SCALE).astype(B16))

    def time_back_group(g, carry):
        for n in range(GH):
            time_backward(g * GH + n)
        spread(c_b, group_cols(g), put_sc(g), 4, g)

        @pl.when(g == 0)
        def _():
            forward(whole, put_out, 7, 0)

        @pl.when(g > 0)
        def _():
            forward(group_cols(g - 1), put_sc(g - 1), 4, g - 1)

        return carry

    lax.fori_loop(0, GROUPS, time_back_group, 0)
    spread(a_b, whole, put_tqg, 5, 0)

    await_bytes(b_b, a2a_ss.at[7])

    def space_backward(h):
        hs = rows(h * HD, HD)
        weights = pw[h]
        cot = sc_r[:, hs]
        key = k_s[:, hs]
        prob = mm(v_s[:, hs], cot, 1, 1)
        centre = jnp.sum(weights * prob, axis=0, keepdims=True)
        grad = (weights * (prob - centre)).astype(B16)
        b_b[:, hs] = (mm(grad, key, 0, 0) * SCALE).astype(B16)
        dk = mm(grad, q_s[:, hs], 1, 0) * SCALE
        dv = mm(weights.astype(B16), cot, 1, 0)
        dk_f[:, hs] = dk[:ROWS]
        dv_f[:, hs] = dv[:ROWS]
        dk_x[:, hs] = dk[ROWS:].astype(B16)
        dv_x[:, hs] = dv[ROWS:].astype(B16)

    def backward_group(g):
        cols = group_cols(g)
        await_bytes(sc_r.at[:, cols], sc_rs.at[g])
        for n in range(GH):
            space_backward(g * GH + n)
        send(dk_x.at[:, cols], dk_r.at[:, cols], x_ss, x_rs.at[0, g], other)
        send(dv_x.at[:, cols], dv_r.at[:, cols], x_ss, x_rs.at[1, g], other)

    await_bytes(t_r, t_rs)
    tt[...] = t_r[...].T
    forward(group_cols(GROUPS - 1), put_sc(GROUPS - 1), 4, GROUPS - 1)
    await_bytes(u_half(y_m, 1), y_rs.at[3])
    await_bytes(u_half(y_p, 0), y_rs.at[2])
    y_f = (y + 2) % YS
    await_bytes(u_half(y_f, 0), y_rs.at[4])
    await_bytes(u_half(y_f, 1), y_rs.at[5])

    z = zh * 2 + zl

    def chip(k):
        zd = (z + k) % 4
        return zd // 2, zd % 2

    def weight_part(k):
        zd = (z + k) % 4
        part = mm(tt[...], u_s[:, rows(zd * 2 * COLS, 2 * COLS)], 1, 0)
        wgf[k, 0] = part[:, :COLS]
        wgf[k, 1] = part[:, COLS:]

    x_up, x_dn = dev((x + 1) % 4, y, zh, zl, core), dev((x + 3) % 4, y, zh, zl, core)
    z_up, z_dn = dev(x, y, *chip(1), core), dev(x, y, *chip(3), core)

    def piece(step, start, size):
        return pl.ds(pl.multiple_of((x + step) % 4 * SUB + start, BAND), size)

    def pair_sum(k):
        await_bytes(crecv.at[k], c_rs.at[k])
        rsend[k] = (wgf[k, core] + crecv[k].astype(F32)).astype(B16)
        send(rsend.at[k, piece(2, 0, LONG)], fx_up.at[k], r_ss.at[4], fx_rs.at[0, k], x_up)
        send(rsend.at[k, piece(2, LONG, SHORT)], fx_dn.at[k], r_ss.at[4], fx_rs.at[1, k], x_dn)
        if k == 2:
            send(rsend.at[k, pl.ds(SIDE, OUT_ROWS)], fz.at[0], r_ss.at[5], fz_rs.at[0], z_up)
            send(rsend.at[k, pl.ds(SIDE + OUT_ROWS, OUT_ROWS)], fz.at[1], r_ss.at[5], fz_rs.at[1], z_dn)

    def add_to(k, where, part):
        rsend[k, where] = (rsend[k, where].astype(F32) + part.astype(F32)).astype(B16)

    def pass_on(k):
        await_bytes(fx_up.at[k], fx_rs.at[0, k])
        add_to(k, piece(1, 0, LONG), fx_up[k])
        send(rsend.at[k, piece(1, 0, SUB)], ra.at[0, k], r_ss.at[0], r_rs.at[0], x_up)
        await_bytes(fx_dn.at[k], fx_rs.at[1, k])
        add_to(k, piece(3, LONG, SHORT), fx_dn[k])
        send(rsend.at[k, piece(3, 0, SUB)], ra.at[1, k], r_ss.at[0], r_rs.at[0], x_dn)
        if k == 1:
            await_bytes(fz.at[0], fz_rs.at[0])
            add_to(k, pl.ds(SIDE, OUT_ROWS), fz[0])
            send(rsend.at[k, pl.ds(SIDE, SIDE)], rb.at[0], r_ss.at[1], r_rs.at[1], z_up)
        if k == 3:
            await_bytes(fz.at[1], fz_rs.at[1])
            add_to(k, pl.ds(SIDE + OUT_ROWS, OUT_ROWS), fz[1])
            send(rsend.at[k, pl.ds(SIDE, SIDE)], rb.at[1], r_ss.at[1], r_rs.at[1], z_dn)

    order = (2, 1, 3, 0)
    for n, k in enumerate(order):
        weight_part(k)
        csend[k] = wgf[k, 1 - core].astype(B16)
        send(csend.at[k], crecv.at[k], c_ss, c_rs.at[k], other)
        if n > 0:
            pair_sum(order[n - 1])
        if n > 1:
            pass_on(order[n - 2])
    pair_sum(order[3])
    pass_on(order[2])
    pass_on(order[3])
    spread(d_b, whole, put_tkg, 6, 0)
    forward(whole, put_tqg, 5, 0)
    def first_stage():
        await_bytes(ra, r_rs.at[0])
        for k in range(4):
            total = ra[0, k].astype(F32) + ra[1, k].astype(F32) + rsend[k, piece(0, 0, SUB)].astype(F32)
            sa[k] = total.astype(B16)
            if k > 0:
                zhd, zld = chip(k)
                send(sa.at[k], ra2.at[z], r_ss.at[2], r_rs.at[2], dev(x, y, zhd, zld, core))
        ra2[z] = sa[0]
        await_bytes(rb, r_rs.at[1])
        total = rb[0].astype(F32) + rb[1].astype(F32) + rsend[0, SIDE:].astype(F32)
        sb[...] = total.astype(B16)
        for step in range(1, 4):
            xd = (x + step) % 4
            send(sb.at[rows(xd * SUB, SUB)], rb2.at[x], r_ss.at[3], r_rs.at[3], dev(xd, y, zh, zl, core))
        rb2[x] = sb[rows(x * SUB, SUB)]

    out_cols = rows((z * 2 + core) * COLS, COLS)
    zh_own, core_own = y // 2, y % 2

    def second_stage():
        for part, (held, n) in enumerate(((ra2, 2), (rb2, 3))):
            await_bytes(held.at[pl.ds(0, 3)], r_rs.at[n])
            total = held[0].astype(F32)
            for k in range(1, 4):
                total = total + held[k].astype(F32)
            red[part * SUB:(part + 1) * SUB] = total.astype(B16)
        for k in range(8):
            yd, zld = (y + k // 2) % YS, (zl + k) % 2
            mine = (yd == y) & (zh_own == zh) & (zld == zl) & (core_own == core)

            @pl.when(mine)
            def _():
                local(red, g_r.at[:, out_cols], g_rs)

            @pl.when(jnp.logical_not(mine))
            def _():
                send(red, g_r.at[:, out_cols], g_ss.at[k], g_rs, dev(x, yd, zh_own, zld, core_own))

    def backward_step(g, carry):
        backward_group(g)

        @pl.when(g == 0)
        def _():
            first_stage()

        @pl.when(g == 1)
        def _():
            second_stage()
            forward(whole, put_tkg, 6, 0)

        return carry

    lax.fori_loop(0, GROUPS, backward_step, 0)

    local(b_b, sqg_o.at[0], out_s.at[0])
    for g in range(GROUPS):
        cols = group_cols(g)
        await_bytes(dk_r.at[:, cols], x_rs.at[0, g])
        await_bytes(dv_r.at[:, cols], x_rs.at[1, g])
    await_bytes(dk_x, x_ss)
    await_bytes(dv_x, x_ss)
    dk_x[...] = (dk_f[...] + dk_r[...].astype(F32)).astype(B16)
    local(dk_x, skg_o.at[0], out_s.at[1])
    dv_x[...] = (dv_f[...] + dv_r[...].astype(F32)).astype(B16)
    local(dv_x, svg_o.at[0], out_s.at[2])

    await_bytes(tqg_r, a2a_rs.at[5])
    local(tqg_r, tqg_o.at[0], out_s.at[3])
    await_bytes(tkg_r, a2a_rs.at[6])
    local(tkg_r, tkg_o.at[0], out_s.at[4])

    await_bytes(k_s.at[own_k], kv_ss.at[0])
    await_bytes(v_s.at[own_k], kv_ss.at[1])
    for i in range(6):
        await_bytes(u_half(0, 0), y_ss.at[i])
    await_bytes(c_b, a2a_ss.at[4])
    await_bytes(a_b, a2a_ss.at[5])
    await_bytes(d_b, a2a_ss.at[6])
    for unit in range(8):
        await_bytes(hop.at[unit], hop_ss.at[unit])
    await_bytes(csend, c_ss)
    for n, held in enumerate((ra, rb, ra2.at[pl.ds(0, 3)], rb2.at[pl.ds(0, 3)], ra.at[0], rb.at[0])):
        await_bytes(held, r_ss.at[n])
    for k in range(8):
        yd, zld = (y + k // 2) % YS, (zl + k) % 2
        mine = (yd == y) & (zh_own == zh) & (zld == zl) & (core_own == core)

        @pl.when(jnp.logical_not(mine))
        def _():
            await_bytes(red, g_ss.at[k])

    await_bytes(g_r, g_rs)
    local(g_r, wg_o, out_s.at[5])
    await_bytes(tqg_r, out_s.at[3])
    await_bytes(tkg_r, out_s.at[4])
    await_bytes(g_r, out_s.at[5])
    await_bytes(b_b, out_s.at[0])
    await_bytes(dk_x, out_s.at[1])
    await_bytes(dv_x, out_s.at[2])


def store(a, b, c, d, e, wg, a_o, b_o, c_o, d_o, e_o, wg_o, held, low, wide, loads, stores):
    ins = [
        pltpu.make_async_copy(src, dst, loads.at[i])
        for i, (src, dst) in enumerate(
            [(wg, low)] + [(r, held.at[pl.ds(k, 1)]) for k, r in enumerate((a, b, c, d, e))]
        )
    ]
    outs = [pltpu.make_async_copy(wide, wg_o, stores.at[0])] + [
        pltpu.make_async_copy(held.at[pl.ds(k, 1)], r, stores.at[k + 1])
        for k, r in enumerate((a_o, b_o, c_o, d_o, e_o))
    ]
    for copy in ins:
        copy.start()
    for k, copy in enumerate(ins):
        copy.wait()
        if k == 0:
            wide[...] = low[...].astype(F32)
        outs[k].start()
    for copy in outs:
        copy.wait()


def local(qs, ks, vs, qt, kt, up, w, mask):
    hbm = pl.BlockSpec(memory_space=pl.ANY)
    vm = pltpu.VMEM
    dma = pltpu.SemaphoreType.DMA
    unit = jax.ShapeDtypeStruct((1, ROWS, HH), B16)
    own = vm((ROWS, HH), B16)
    outs = pl.pallas_call(
        kernel,
        out_shape=(unit,) * 5 + (jax.ShapeDtypeStruct((OUT_ROWS, D), B16),),
        in_specs=[hbm] * 7 + [pl.BlockSpec(memory_space=pltpu.VMEM)],
        out_specs=(hbm,) * 6,
        scratch_shapes=[
            own, vm((P_SIZE, HH), B16), vm((P_SIZE, HH), B16), vm((HH, D), B16),
            vm((YS * ROWS, D), B16), own, own, own, own, own, vm((YS * ROWS, BLOCK), B16),
            own, own, own, own,
            vm((HEADS, P_SIZE, ROWS), F32), vm((HEADS, 2, GROUP, GROUP), F32),
            vm((P_SIZE, ROWS), F32), vm((GROUP, GROUP), F32),
            vm((BLOCK, YS * ROWS), B16), vm((4, 2, BLOCK, COLS), F32),
            vm((4, BLOCK, COLS), B16), vm((4, BLOCK, COLS), B16),
            vm((4, BLOCK, COLS), B16), vm((2, 4, SUB, COLS), B16), vm((2, SIDE, COLS), B16),
            vm((4, LONG, COLS), B16), vm((4, SHORT, COLS), B16), vm((2, OUT_ROWS, COLS), B16),
            vm((4, SUB, COLS), B16), vm((4, SUB, COLS), B16), vm((4, SUB, COLS), B16),
            vm((SIDE, COLS), B16), vm((OUT_ROWS, COLS), B16),
            vm((ROWS, HH), F32), vm((ROWS, HH), F32), own, own, own, own,
            vm((8, 2 * PIX, HH), B16), vm((GROUPS, ROWS, GC), F32),
            own, own, vm((OUT_ROWS, D), B16),
            dma((6 + WCH,)), dma((2,)), dma((2,)), dma((6,)), dma((6,)), dma((8,)), dma((7,)),
            dma((GROUPS,)), dma((GROUPS,)), dma, dma((8,)), dma((8, GROUPS)), dma, dma((4,)), dma((6,)), dma((4,)),
            dma((2, 4)), dma((2,)), dma((8,)), dma, dma, dma((2, GROUPS)), dma((6,)),
        ],
        compiler_params=pltpu.CompilerParams(
            has_side_effects=True, vmem_limit_bytes=62 * 1024 * 1024
        ),
        cost_estimate=pl.CostEstimate(
            flops=8 * 10**9, bytes_accessed=20 * 10**6, transcendentals=3 * 10**6
        ),
    )(qs, ks, vs, qt, kt, up, w, mask)
    return pl.pallas_call(
        store,
        out_shape=(unit,) * 5 + (jax.ShapeDtypeStruct((OUT_ROWS, D), F32),),
        in_specs=[hbm] * 6,
        out_specs=(hbm,) * 6,
        scratch_shapes=[
            vm((5, ROWS, HH), B16), vm((OUT_ROWS, D), B16), vm((OUT_ROWS, D), F32), dma((6,)), dma((6,)),
        ],
        compiler_params=pltpu.CompilerParams(vmem_limit_bytes=62 * 1024 * 1024),
    )(*outs)


def solution(mesh):
    tokens = P("dp", "seq", None)
    return jax.shard_map(
        local,
        mesh=mesh,
        in_specs=(tokens,) * 6 + (P(), P()),
        out_specs=(tokens,) * 5 + (P("seq", None),),
        check_vma=False,
    )
```

```python
import math

import jax
import jax.numpy as jnp
from jax import lax
from jax.experimental import pallas as pl
from jax.experimental.pallas import tpu as pltpu
from jax.sharding import PartitionSpec as P

HEADS = 12
HD = 128
HH = HEADS * HD
D = 3072
ROWS = 256
P_SIZE = 512
TILE = 32
NT = 16
FRAMES = 8
PIX = ROWS // FRAMES
HALF = PIX // 2
YS = 4
BLOCK = HH // YS
COLS = D // 8
OUT_ROWS = 96
SUB = OUT_ROWS // 2
SIDE = BLOCK // 2
GROUPS = 4
GH = HEADS // GROUPS
GC = GH * HD
WCH = 6
WROWS = HH // WCH
SCALE = 1.0 / math.sqrt(HD)
POWER = SCALE / math.log(2.0)
NEG = -1e30
BAND = PIX // 2
GROUP = ROWS // 2
MESH = pl.DeviceIdType.MESH
F32 = jnp.float32
B16 = jnp.bfloat16


def mm(a, b, ca, cb):
    return lax.dot_general(a, b, (((ca,), (cb,)), ((), ())), preferred_element_type=F32)


def kernel(
    qs, ks, vs, qt, kt, up, w, mask,
    sqg_o, skg_o, svg_o, tqg_o, tkg_o, wg_o,
    q_s, k_s, v_s, w_s, u_s, tq_r, tk_r, so_r, oc_r, sc_r, t_r,
    a_b, b_b, c_b, d_b, pw, tw, bias, tbias, tt, wgf, csend, crecv, rsend, ra, rb, ra2, rb2, sa, sb, red,
    dk_f, dv_f, dk_x, dv_x, dk_r, dv_r, hop, t_f, tqg_r, tkg_r, g_r,
    ld, kv_ss, kv_rs, y_ss, y_rs, a2a_ss, a2a_rs, so_rs, sc_rs, t_rs, hop_ss, hop_rs,
    c_ss, c_rs, r_ss, r_rs, g_ss, g_rs, x_ss, x_rs, out_s,
):
    dp = lax.axis_index("dp")
    seq = lax.axis_index("seq")
    y, zl = dp // 2, dp % 2
    x, zh, core = seq // 4, (seq // 2) % 2, seq % 2
    frame = x * 2 + zh

    def dev(x_, y_, zh_, zl_, c_):
        return {"dp": y_ * 2 + zl_, "seq": x_ * 4 + zh_ * 2 + c_}

    def send(src, dst, ss, rs, to):
        pltpu.make_async_remote_copy(
            src_ref=src, dst_ref=dst, send_sem=ss, recv_sem=rs, device_id=to, device_id_type=MESH
        ).start()

    def await_bytes(ref, sem):
        pltpu.make_async_copy(ref, ref, sem).wait()

    def local(src, dst, sem):
        pltpu.make_async_copy(src, dst, sem).start()

    def rows(start, size):
        return pl.ds(pl.multiple_of(start, size), size)

    def spread(src, cols, put, unit, part):
        for zd in range(2):
            for side in range(2):
                far = ((x + 2) % 4 * 2 + zd) * PIX + side * HALF
                send(
                    src.at[rows(far, HALF), cols],
                    hop.at[unit, rows(side * PIX + zh * HALF, HALF), cols],
                    a2a_ss.at[unit], hop_rs.at[unit, part],
                    dev((x + 1 + 2 * side) % 4, y, zd, 1 - zl, core),
                )
        for step in (1, 3, 0):
            xd = (x + step) % 4
            for zd in range(2):
                put(
                    src, rows((xd * 2 + zd) * PIX, PIX), frame * PIX, PIX, a2a_ss.at[unit],
                    xd, zd, 1 - zl,
                )

    def forward(cols, put, unit, part):
        await_bytes(hop.at[unit, :, cols], hop_rs.at[unit, part])
        for side in range(2):
            came = (x + 3 + 2 * side) % 4
            for zs in range(2):
                put(
                    hop.at[unit], pl.ds(side * PIX + zs * HALF, HALF),
                    (came * 2 + zs) * PIX + side * HALF, HALF, hop_ss.at[unit],
                    (x + 1 + 2 * side) % 4, zh, zl,
                )

    def putter(dst, cols, rs):
        def put(src, src_rows, start, size, ss, xd, zd, zld):
            send(
                src.at[src_rows, cols], dst.at[rows(start, size), cols], ss, rs,
                dev(xd, y, zd, zld, core),
            )

        return put

    whole = pl.ds(0, HH)

    def group_cols(g):
        return rows(g * GC, GC)

    put_tq = putter(tq_r, whole, a2a_rs.at[0])
    put_tk = putter(tk_r, whole, a2a_rs.at[1])
    put_oc = putter(oc_r, whole, a2a_rs.at[2])

    def put_so(g):
        return putter(so_r, group_cols(g), so_rs.at[g])

    def put_sc(g):
        return putter(sc_r, group_cols(g), sc_rs.at[g])

    put_tqg = putter(tqg_r, whole, a2a_rs.at[5])
    put_tkg = putter(tkg_r, whole, a2a_rs.at[6])

    def put_out(src, src_rows, start, size, ss, xd, zd, zld):
        for k in range(YS):
            yd = (y + k) % YS
            send(
                src.at[src_rows, rows(yd * BLOCK, BLOCK)], t_r.at[rows(y * ROWS + start, size)],
                ss, t_rs, dev(xd, yd, zd, zld, core),
            )

    other = dev(x, y, zh, zl, 1 - core)
    y_up = dev(x, (y + 1) % YS, zh, zl, core)
    y_dn = dev(x, (y + 3) % YS, zh, zl, core)

    cut = 160
    own_k, far_k = pl.ds(0, ROWS), pl.ds(ROWS, ROWS)
    own_u = pl.ds(pl.multiple_of(y * ROWS, ROWS), ROWS)

    def u_half(owner, part):
        start, size = (0, cut) if part == 0 else (cut, ROWS - cut)
        return u_s.at[pl.ds(pl.multiple_of(owner * ROWS + start, PIX), size)]

    loads = (
        (ks.at[0], k_s.at[own_k]), (vs.at[0], v_s.at[own_k]), (qt.at[0], b_b), (kt.at[0], d_b),
        (up.at[0], u_s.at[own_u]), (qs.at[0], q_s),
    )
    for i, (src, dst) in enumerate(loads):
        local(src, dst, ld.at[i])
    for i in range(WCH):
        local(w.at[pl.ds(i * WROWS, WROWS)], w_s.at[pl.ds(i * WROWS, WROWS)], ld.at[6 + i])

    await_bytes(k_s.at[own_k], ld.at[0])
    send(k_s.at[own_k], k_s.at[far_k], kv_ss.at[0], kv_rs.at[0], other)
    await_bytes(v_s.at[own_k], ld.at[1])
    send(v_s.at[own_k], v_s.at[far_k], kv_ss.at[1], kv_rs.at[1], other)
    await_bytes(b_b, ld.at[2])
    spread(b_b, whole, put_tq, 0, 0)
    await_bytes(u_s.at[own_u], ld.at[4])
    send(u_half(y, 0), u_half(y, 0), y_ss.at[0], y_rs.at[0], y_up)
    send(u_half(y, 1), u_half(y, 1), y_ss.at[1], y_rs.at[1], y_dn)
    await_bytes(d_b, ld.at[3])
    spread(d_b, whole, put_tk, 1, 0)
    send(u_half(y, 0), u_half(y, 0), y_ss.at[2], y_rs.at[2], y_dn)
    send(u_half(y, 1), u_half(y, 1), y_ss.at[3], y_rs.at[3], y_up)

    key_row = lax.broadcasted_iota(jnp.int32, (P_SIZE, NT), 0)
    key_tile = jnp.where(
        key_row < ROWS, core * (NT // 2) + key_row // TILE,
        (1 - core) * (NT // 2) + (key_row - ROWS) // TILE,
    )
    key_hot = (key_tile == lax.broadcasted_iota(jnp.int32, (P_SIZE, NT), 1)).astype(F32)
    query_tile = core * (NT // 2) + lax.broadcasted_iota(jnp.int32, (ROWS, NT), 0) // TILE
    query_hot = (query_tile == lax.broadcasted_iota(jnp.int32, (ROWS, NT), 1)).astype(F32)
    rows_mask = mm(query_hot, mask[...].astype(F32), 1, 0)
    bias[...] = jnp.where(mm(key_hot, rows_mask, 1, 1) > 0.5, 0.0, NEG)
    same = (
        lax.broadcasted_iota(jnp.int32, (GROUP, GROUP), 0) % BAND
        == lax.broadcasted_iota(jnp.int32, (GROUP, GROUP), 1) % BAND
    )
    tbias[...] = jnp.where(same, 0.0, NEG)

    def cot_chunk(i, carry):
        part = rows(i * WROWS, WROWS)
        await_bytes(w_s.at[part], ld.at[6 + i])
        c_b[:, part] = mm(w_s[part, :], u_s[own_u, :], 1, 1).T.astype(B16)
        return carry

    lax.fori_loop(0, WCH, cot_chunk, 0)

    await_bytes(q_s, ld.at[5])
    await_bytes(k_s.at[far_k], kv_rs.at[0])
    await_bytes(v_s.at[far_k], kv_rs.at[1])

    def space_forward(h):
        hs = rows(h * HD, HD)
        scores = mm(k_s[:, hs], q_s[:, hs], 1, 1) + bias[...]
        powers = jnp.exp2((scores - jnp.max(scores, axis=0, keepdims=True)) * POWER)
        weights = powers * (1.0 / jnp.sum(powers, axis=0, keepdims=True))
        pw[h] = weights
        a_b[:, hs] = mm(weights.astype(B16), v_s[:, hs], 0, 0).astype(B16)

    def space_group(g, carry):
        for n in range(GH):
            space_forward(g * GH + n)
        spread(a_b, group_cols(g), put_so(g), 3, g)
        return carry

    lax.fori_loop(0, GROUPS, space_group, 0)
    forward(whole, put_tq, 0, 0)
    forward(whole, put_tk, 1, 0)
    spread(c_b, whole, put_oc, 2, 0)

    y_m, y_p = (y + 3) % YS, (y + 1) % YS
    await_bytes(u_half(y_m, 0), y_rs.at[0])
    send(u_half(y_m, 0), u_half(y_m, 0), y_ss.at[4], y_rs.at[4], y_up)
    await_bytes(u_half(y_p, 1), y_rs.at[1])
    send(u_half(y_p, 1), u_half(y_p, 1), y_ss.at[5], y_rs.at[5], y_dn)

    await_bytes(tq_r, a2a_rs.at[0])
    await_bytes(tk_r, a2a_rs.at[1])

    def band(ref, h, b):
        hs = rows(h * HD, HD)
        return jnp.concatenate(
            [ref[f * PIX + b * BAND:f * PIX + (b + 1) * BAND, hs] for f in range(FRAMES)], axis=0
        )

    def put_band(ref, h, b, value):
        hs = rows(h * HD, HD)
        for f in range(FRAMES):
            ref[f * PIX + b * BAND:f * PIX + (b + 1) * BAND, hs] = value[f * BAND:(f + 1) * BAND]

    def time_forward(h):
        for b in range(2):
            scores = mm(band(tk_r, h, b), band(tq_r, h, b), 1, 1) + tbias[...]
            powers = jnp.exp2((scores - jnp.max(scores, axis=0, keepdims=True)) * POWER)
            tw[h, b] = powers * (1.0 / jnp.sum(powers, axis=0, keepdims=True))

    def time_group(g, carry):
        for n in range(GH):
            time_forward(g * GH + n)
        return carry

    lax.fori_loop(0, GROUPS, time_group, 0)

    def forward_space(g, carry):
        forward(group_cols(g), put_so(g), 3, g)
        return carry

    lax.fori_loop(0, GROUPS, forward_space, 0)

    await_bytes(b_b, a2a_ss.at[0])
    def apply_group(g, carry):
        await_bytes(so_r.at[:, group_cols(g)], so_rs.at[g])
        for n in range(GH):
            h = g * GH + n
            for b in range(2):
                out = mm(tw[h, b].astype(B16), band(so_r, h, b), 0, 0)
                for f in range(FRAMES):
                    t_f[g, f * PIX + b * BAND:f * PIX + (b + 1) * BAND, n * HD:(n + 1) * HD] = (
                        out[f * BAND:(f + 1) * BAND]
                    )
        return carry

    lax.fori_loop(0, GROUPS, apply_group, 0)
    for k in range(YS):
        block = [
            t_f[g, :, k * OUT_ROWS + part * SUB:k * OUT_ROWS + (part + 1) * SUB]
            for part in range(2)
            for g in range(GROUPS)
        ]
        b_b[:, k * BLOCK:(k + 1) * BLOCK] = jnp.concatenate(block, axis=1).astype(B16)

    spread(b_b, whole, put_out, 7, 0)
    forward(whole, put_oc, 2, 0)

    await_bytes(oc_r, a2a_rs.at[2])
    await_bytes(c_b, a2a_ss.at[2])
    await_bytes(a_b, a2a_ss.at[3])
    await_bytes(d_b, a2a_ss.at[1])

    def time_backward(h):
        for b in range(2):
            weights = tw[h, b]
            cot = band(oc_r, h, b)
            put_band(c_b, h, b, mm(weights.astype(B16), cot, 1, 0).astype(B16))
            prob = mm(band(so_r, h, b), cot, 1, 1)
            centre = jnp.sum(weights * prob, axis=0, keepdims=True)
            grad = (weights * (prob - centre)).astype(B16)
            put_band(a_b, h, b, (mm(grad, band(tk_r, h, b), 0, 0) * SCALE).astype(B16))
            put_band(d_b, h, b, (mm(grad, band(tq_r, h, b), 1, 0) * SCALE).astype(B16))

    def time_back_group(g, carry):
        for n in range(GH):
            time_backward(g * GH + n)
        spread(c_b, group_cols(g), put_sc(g), 4, g)

        @pl.when(g == 0)
        def _():
            forward(whole, put_out, 7, 0)

        return carry

    def forward_cot(g, carry):
        forward(group_cols(g), put_sc(g), 4, g)
        return carry

    lax.fori_loop(0, GROUPS, time_back_group, 0)
    spread(a_b, whole, put_tqg, 5, 0)
    lax.fori_loop(0, 2, forward_cot, 0)

    await_bytes(b_b, a2a_ss.at[7])

    def space_backward(h):
        hs = rows(h * HD, HD)
        weights = pw[h]
        cot = sc_r[:, hs]
        key = k_s[:, hs]
        prob = mm(v_s[:, hs], cot, 1, 1)
        centre = jnp.sum(weights * prob, axis=0, keepdims=True)
        grad = (weights * (prob - centre)).astype(B16)
        b_b[:, hs] = (mm(grad, key, 0, 0) * SCALE).astype(B16)
        dk = mm(grad, q_s[:, hs], 1, 0) * SCALE
        dv = mm(weights.astype(B16), cot, 1, 0)
        dk_f[:, hs] = dk[:ROWS]
        dv_f[:, hs] = dv[:ROWS]
        dk_x[:, hs] = dk[ROWS:].astype(B16)
        dv_x[:, hs] = dv[ROWS:].astype(B16)

    def backward_group(g):
        cols = group_cols(g)
        await_bytes(sc_r.at[:, cols], sc_rs.at[g])
        for n in range(GH):
            space_backward(g * GH + n)
        send(dk_x.at[:, cols], dk_r.at[:, cols], x_ss, x_rs.at[0, g], other)
        send(dv_x.at[:, cols], dv_r.at[:, cols], x_ss, x_rs.at[1, g], other)

    await_bytes(t_r, t_rs)
    tt[...] = t_r[...].T
    await_bytes(u_half(y_m, 1), y_rs.at[3])
    await_bytes(u_half(y_p, 0), y_rs.at[2])
    y_f = (y + 2) % YS
    await_bytes(u_half(y_f, 0), y_rs.at[4])
    await_bytes(u_half(y_f, 1), y_rs.at[5])

    z = zh * 2 + zl

    def chip(k):
        zd = (z + k) % 4
        return zd // 2, zd % 2

    def weight_part(k):
        zd = (z + k) % 4
        part = mm(tt[...], u_s[:, rows(zd * 2 * COLS, 2 * COLS)], 1, 0)
        wgf[k, 0] = part[:, :COLS]
        wgf[k, 1] = part[:, COLS:]

    def pair_sum(k, along_z):
        await_bytes(crecv.at[k], c_rs.at[k])
        rsend[k] = (wgf[k, core] + crecv[k].astype(F32)).astype(B16)
        for step in range(1, 4):
            xd = (x + step) % 4
            send(rsend.at[k, rows(xd * SUB, SUB)], ra.at[x, k], r_ss.at[0], r_rs.at[0], dev(xd, y, zh, zl, core))
        if along_z:
            zhd, zld = chip(k)
            send(rsend.at[k, pl.ds(SIDE, SIDE)], rb.at[z], r_ss.at[1], r_rs.at[1], dev(x, y, zhd, zld, core))

    def weight_step(n, carry):
        k = (n + 1) % 4
        weight_part(k)
        csend[k] = wgf[k, 1 - core].astype(B16)
        send(csend.at[k], crecv.at[k], c_ss, c_rs.at[k], other)

        @pl.when(n > 0)
        def _():
            pair_sum(n, True)

        return carry

    lax.fori_loop(0, 4, weight_step, 0)
    pair_sum(0, False)
    spread(d_b, whole, put_tkg, 6, 0)
    lax.fori_loop(2, GROUPS, forward_cot, 0)

    def first_stage():
        for k in range(4):
            ra[x, k] = rsend[k, rows(x * SUB, SUB)]
        rb[z] = rsend[0, SIDE:]
        await_bytes(ra.at[pl.ds(0, 3)], r_rs.at[0])
        for k in range(4):
            total = ra[0, k].astype(F32)
            for n in range(1, 4):
                total = total + ra[n, k].astype(F32)
            sa[k] = total.astype(B16)
            if k > 0:
                zhd, zld = chip(k)
                send(sa.at[k], ra2.at[z], r_ss.at[2], r_rs.at[2], dev(x, y, zhd, zld, core))
        ra2[z] = sa[0]
        await_bytes(rb.at[pl.ds(0, 3)], r_rs.at[1])
        total = rb[0].astype(F32)
        for n in range(1, 4):
            total = total + rb[n].astype(F32)
        sb[...] = total.astype(B16)
        for step in range(1, 4):
            xd = (x + step) % 4
            send(sb.at[rows(xd * SUB, SUB)], rb2.at[x], r_ss.at[3], r_rs.at[3], dev(xd, y, zh, zl, core))
        rb2[x] = sb[rows(x * SUB, SUB)]

    out_cols = rows((z * 2 + core) * COLS, COLS)
    zh_own, core_own = y // 2, y % 2

    def second_stage():
        for part, (held, n) in enumerate(((ra2, 2), (rb2, 3))):
            await_bytes(held.at[pl.ds(0, 3)], r_rs.at[n])
            total = held[0].astype(F32)
            for k in range(1, 4):
                total = total + held[k].astype(F32)
            red[part * SUB:(part + 1) * SUB] = total.astype(B16)
        for k in range(8):
            yd, zld = (y + k // 2) % YS, (zl + k) % 2
            mine = (yd == y) & (zh_own == zh) & (zld == zl) & (core_own == core)

            @pl.when(mine)
            def _():
                local(red, g_r.at[:, out_cols], g_rs)

            @pl.when(jnp.logical_not(mine))
            def _():
                send(red, g_r.at[:, out_cols], g_ss.at[k], g_rs, dev(x, yd, zh_own, zld, core_own))

    def backward_step(g, carry):
        backward_group(g)

        @pl.when(g == 0)
        def _():
            first_stage()

        @pl.when(g == 1)
        def _():
            second_stage()
            forward(whole, put_tqg, 5, 0)
            forward(whole, put_tkg, 6, 0)

        return carry

    lax.fori_loop(0, GROUPS, backward_step, 0)

    local(b_b, sqg_o.at[0], out_s.at[0])
    for g in range(GROUPS):
        cols = group_cols(g)
        await_bytes(dk_r.at[:, cols], x_rs.at[0, g])
        await_bytes(dv_r.at[:, cols], x_rs.at[1, g])
    await_bytes(dk_x, x_ss)
    await_bytes(dv_x, x_ss)
    dk_x[...] = (dk_f[...] + dk_r[...].astype(F32)).astype(B16)
    local(dk_x, skg_o.at[0], out_s.at[1])
    dv_x[...] = (dv_f[...] + dv_r[...].astype(F32)).astype(B16)
    local(dv_x, svg_o.at[0], out_s.at[2])

    await_bytes(tqg_r, a2a_rs.at[5])
    local(tqg_r, tqg_o.at[0], out_s.at[3])
    await_bytes(tkg_r, a2a_rs.at[6])
    local(tkg_r, tkg_o.at[0], out_s.at[4])

    await_bytes(k_s.at[own_k], kv_ss.at[0])
    await_bytes(v_s.at[own_k], kv_ss.at[1])
    for i, part in enumerate((0, 1, 0, 1, 0, 1)):
        await_bytes(u_half(0, part), y_ss.at[i])
    await_bytes(c_b, a2a_ss.at[4])
    await_bytes(a_b, a2a_ss.at[5])
    await_bytes(d_b, a2a_ss.at[6])
    for unit in range(8):
        await_bytes(hop.at[unit], hop_ss.at[unit])
    await_bytes(csend, c_ss)
    for n, held in enumerate((ra, rb, ra2, rb2)):
        await_bytes(held.at[pl.ds(0, 3)], r_ss.at[n])
    for k in range(8):
        yd, zld = (y + k // 2) % YS, (zl + k) % 2
        mine = (yd == y) & (zh_own == zh) & (zld == zl) & (core_own == core)

        @pl.when(jnp.logical_not(mine))
        def _():
            await_bytes(red, g_ss.at[k])

    await_bytes(g_r, g_rs)
    local(g_r, wg_o, out_s.at[5])
    await_bytes(tqg_r, out_s.at[3])
    await_bytes(tkg_r, out_s.at[4])
    await_bytes(g_r, out_s.at[5])
    await_bytes(b_b, out_s.at[0])
    await_bytes(dk_x, out_s.at[1])
    await_bytes(dv_x, out_s.at[2])


def store(a, b, c, d, e, wg, a_o, b_o, c_o, d_o, e_o, wg_o, held, low, wide, loads, stores):
    ins = [
        pltpu.make_async_copy(src, dst, loads.at[i])
        for i, (src, dst) in enumerate(
            [(wg, low)] + [(r, held.at[pl.ds(k, 1)]) for k, r in enumerate((a, b, c, d, e))]
        )
    ]
    outs = [pltpu.make_async_copy(wide, wg_o, stores.at[0])] + [
        pltpu.make_async_copy(held.at[pl.ds(k, 1)], r, stores.at[k + 1])
        for k, r in enumerate((a_o, b_o, c_o, d_o, e_o))
    ]
    for copy in ins:
        copy.start()
    for k, copy in enumerate(ins):
        copy.wait()
        if k == 0:
            wide[...] = low[...].astype(F32)
        outs[k].start()
    for copy in outs:
        copy.wait()


def local(qs, ks, vs, qt, kt, up, w, mask):
    hbm = pl.BlockSpec(memory_space=pl.ANY)
    vm = pltpu.VMEM
    dma = pltpu.SemaphoreType.DMA
    unit = jax.ShapeDtypeStruct((1, ROWS, HH), B16)
    own = vm((ROWS, HH), B16)
    outs = pl.pallas_call(
        kernel,
        out_shape=(unit,) * 5 + (jax.ShapeDtypeStruct((OUT_ROWS, D), B16),),
        in_specs=[hbm] * 7 + [pl.BlockSpec(memory_space=pltpu.VMEM)],
        out_specs=(hbm,) * 6,
        scratch_shapes=[
            own, vm((P_SIZE, HH), B16), vm((P_SIZE, HH), B16), vm((HH, D), B16),
            vm((YS * ROWS, D), B16), own, own, own, own, own, vm((YS * ROWS, BLOCK), B16),
            own, own, own, own,
            vm((HEADS, P_SIZE, ROWS), F32), vm((HEADS, 2, GROUP, GROUP), F32),
            vm((P_SIZE, ROWS), F32), vm((GROUP, GROUP), F32),
            vm((BLOCK, YS * ROWS), B16), vm((4, 2, BLOCK, COLS), F32),
            vm((4, BLOCK, COLS), B16), vm((4, BLOCK, COLS), B16),
            vm((4, BLOCK, COLS), B16), vm((4, 4, SUB, COLS), B16), vm((4, SIDE, COLS), B16),
            vm((4, SUB, COLS), B16), vm((4, SUB, COLS), B16), vm((4, SUB, COLS), B16),
            vm((SIDE, COLS), B16), vm((OUT_ROWS, COLS), B16),
            vm((ROWS, HH), F32), vm((ROWS, HH), F32), own, own, own, own,
            vm((8, 2 * PIX, HH), B16), vm((GROUPS, ROWS, GC), F32),
            own, own, vm((OUT_ROWS, D), B16),
            dma((6 + WCH,)), dma((2,)), dma((2,)), dma((6,)), dma((6,)), dma((8,)), dma((7,)),
            dma((GROUPS,)), dma((GROUPS,)), dma, dma((8,)), dma((8, GROUPS)), dma, dma((4,)), dma((4,)), dma((4,)),
            dma((8,)), dma, dma, dma((2, GROUPS)), dma((6,)),
        ],
        compiler_params=pltpu.CompilerParams(
            has_side_effects=True, vmem_limit_bytes=62 * 1024 * 1024
        ),
        cost_estimate=pl.CostEstimate(
            flops=8 * 10**9, bytes_accessed=20 * 10**6, transcendentals=3 * 10**6
        ),
    )(qs, ks, vs, qt, kt, up, w, mask)
    return pl.pallas_call(
        store,
        out_shape=(unit,) * 5 + (jax.ShapeDtypeStruct((OUT_ROWS, D), F32),),
        in_specs=[hbm] * 6,
        out_specs=(hbm,) * 6,
        scratch_shapes=[
            vm((5, ROWS, HH), B16), vm((OUT_ROWS, D), B16), vm((OUT_ROWS, D), F32), dma((6,)), dma((6,)),
        ],
        compiler_params=pltpu.CompilerParams(vmem_limit_bytes=62 * 1024 * 1024),
    )(*outs)


def solution(mesh):
    tokens = P("dp", "seq", None)
    return jax.shard_map(
        local,
        mesh=mesh,
        in_specs=(tokens,) * 6 + (P(), P()),
        out_specs=(tokens,) * 5 + (P("seq", None),),
        check_vma=False,
    )
```

```python
import math

import jax
import jax.numpy as jnp
from jax import lax
from jax.experimental import pallas as pl
from jax.experimental.pallas import tpu as pltpu
from jax.sharding import PartitionSpec as P

HEADS = 12
HD = 128
HH = HEADS * HD
D = 3072
ROWS = 256
P_SIZE = 512
TILE = 32
NT = 16
FRAMES = 8
PIX = ROWS // FRAMES
HALF = PIX // 2
YS = 4
BLOCK = HH // YS
COLS = D // 8
OUT_ROWS = 96
SUB = OUT_ROWS // 2
SIDE = BLOCK // 2
GROUPS = 4
GH = HEADS // GROUPS
GC = GH * HD
WCH = 6
WROWS = HH // WCH
SCALE = 1.0 / math.sqrt(HD)
POWER = SCALE / math.log(2.0)
NEG = -1e30
BAND = PIX // 2
GROUP = ROWS // 2
MESH = pl.DeviceIdType.MESH
F32 = jnp.float32
B16 = jnp.bfloat16


def mm(a, b, ca, cb):
    return lax.dot_general(a, b, (((ca,), (cb,)), ((), ())), preferred_element_type=F32)


def kernel(
    qs, ks, vs, qt, kt, up, w, mask,
    sqg_o, skg_o, svg_o, tqg_o, tkg_o, wg_o,
    q_s, k_s, v_s, w_s, u_s, tq_r, tk_r, so_r, oc_r, sc_r, t_r,
    a_b, b_b, c_b, d_b, pw, tw, bias, tbias, tt, wgf, csend, crecv, rsend, ra, rb, ra2, rb2, sa, sb, red,
    dk_f, dv_f, dk_x, dv_x, dk_r, dv_r, hop, t_f, tqg_r, tkg_r, g_r,
    ld, kv_ss, kv_rs, y_ss, y_rs, a2a_ss, a2a_rs, so_rs, sc_rs, t_rs, hop_ss, hop_rs,
    c_ss, c_rs, r_ss, r_rs, g_ss, g_rs, x_ss, x_rs, out_s,
):
    dp = lax.axis_index("dp")
    seq = lax.axis_index("seq")
    y, zl = dp // 2, dp % 2
    x, zh, core = seq // 4, (seq // 2) % 2, seq % 2
    frame = x * 2 + zh

    def dev(x_, y_, zh_, zl_, c_):
        return {"dp": y_ * 2 + zl_, "seq": x_ * 4 + zh_ * 2 + c_}

    def send(src, dst, ss, rs, to):
        pltpu.make_async_remote_copy(
            src_ref=src, dst_ref=dst, send_sem=ss, recv_sem=rs, device_id=to, device_id_type=MESH
        ).start()

    def await_bytes(ref, sem):
        pltpu.make_async_copy(ref, ref, sem).wait()

    def local(src, dst, sem):
        pltpu.make_async_copy(src, dst, sem).start()

    def rows(start, size):
        return pl.ds(pl.multiple_of(start, size), size)

    def spread(src, cols, put, unit, part):
        for zd in range(2):
            for side in range(2):
                far = ((x + 2) % 4 * 2 + zd) * PIX + side * HALF
                send(
                    src.at[rows(far, HALF), cols],
                    hop.at[unit, rows(side * PIX + zh * HALF, HALF), cols],
                    a2a_ss.at[unit], hop_rs.at[unit, part],
                    dev((x + 1 + 2 * side) % 4, y, zd, 1 - zl, core),
                )
        for step in (1, 3, 0):
            xd = (x + step) % 4
            for zd in range(2):
                put(
                    src, rows((xd * 2 + zd) * PIX, PIX), frame * PIX, PIX, a2a_ss.at[unit],
                    xd, zd, 1 - zl,
                )

    def forward(cols, put, unit, part):
        await_bytes(hop.at[unit, :, cols], hop_rs.at[unit, part])
        for side in range(2):
            came = (x + 3 + 2 * side) % 4
            for zs in range(2):
                put(
                    hop.at[unit], pl.ds(side * PIX + zs * HALF, HALF),
                    (came * 2 + zs) * PIX + side * HALF, HALF, hop_ss.at[unit],
                    (x + 1 + 2 * side) % 4, zh, zl,
                )

    def putter(dst, cols, rs):
        def put(src, src_rows, start, size, ss, xd, zd, zld):
            send(
                src.at[src_rows, cols], dst.at[rows(start, size), cols], ss, rs,
                dev(xd, y, zd, zld, core),
            )

        return put

    whole = pl.ds(0, HH)

    def group_cols(g):
        return rows(g * GC, GC)

    put_tq = putter(tq_r, whole, a2a_rs.at[0])
    put_tk = putter(tk_r, whole, a2a_rs.at[1])
    put_oc = putter(oc_r, whole, a2a_rs.at[2])

    def put_so(g):
        return putter(so_r, group_cols(g), so_rs.at[g])

    def put_sc(g):
        return putter(sc_r, group_cols(g), sc_rs.at[g])

    put_tqg = putter(tqg_r, whole, a2a_rs.at[5])
    put_tkg = putter(tkg_r, whole, a2a_rs.at[6])

    def put_out(src, src_rows, start, size, ss, xd, zd, zld):
        for k in range(YS):
            yd = (y + k) % YS
            send(
                src.at[src_rows, rows(yd * BLOCK, BLOCK)], t_r.at[rows(y * ROWS + start, size)],
                ss, t_rs, dev(xd, yd, zd, zld, core),
            )

    other = dev(x, y, zh, zl, 1 - core)
    y_up = dev(x, (y + 1) % YS, zh, zl, core)
    y_dn = dev(x, (y + 3) % YS, zh, zl, core)

    cut = 96
    own_k, far_k = pl.ds(0, ROWS), pl.ds(ROWS, ROWS)
    own_u = pl.ds(pl.multiple_of(y * ROWS, ROWS), ROWS)

    def u_half(owner, part):
        start, size = (0, cut) if part == 0 else (cut, ROWS - cut)
        return u_s.at[pl.ds(pl.multiple_of(owner * ROWS + start, PIX), size)]

    loads = (
        (ks.at[0], k_s.at[own_k]), (vs.at[0], v_s.at[own_k]), (qt.at[0], b_b), (kt.at[0], d_b),
        (up.at[0], u_s.at[own_u]), (qs.at[0], q_s),
    )
    for i, (src, dst) in enumerate(loads):
        local(src, dst, ld.at[i])
    for i in range(WCH):
        local(w.at[pl.ds(i * WROWS, WROWS)], w_s.at[pl.ds(i * WROWS, WROWS)], ld.at[6 + i])

    await_bytes(k_s.at[own_k], ld.at[0])
    send(k_s.at[own_k], k_s.at[far_k], kv_ss.at[0], kv_rs.at[0], other)
    await_bytes(v_s.at[own_k], ld.at[1])
    send(v_s.at[own_k], v_s.at[far_k], kv_ss.at[1], kv_rs.at[1], other)
    await_bytes(b_b, ld.at[2])
    spread(b_b, whole, put_tq, 0, 0)
    await_bytes(u_s.at[own_u], ld.at[4])
    send(u_half(y, 0), u_half(y, 0), y_ss.at[0], y_rs.at[0], y_up)
    send(u_half(y, 1), u_half(y, 1), y_ss.at[1], y_rs.at[1], y_dn)
    await_bytes(d_b, ld.at[3])
    spread(d_b, whole, put_tk, 1, 0)
    send(u_half(y, 0), u_half(y, 0), y_ss.at[2], y_rs.at[2], y_dn)
    send(u_half(y, 1), u_half(y, 1), y_ss.at[3], y_rs.at[3], y_up)

    key_row = lax.broadcasted_iota(jnp.int32, (P_SIZE, NT), 0)
    key_tile = jnp.where(
        key_row < ROWS, core * (NT // 2) + key_row // TILE,
        (1 - core) * (NT // 2) + (key_row - ROWS) // TILE,
    )
    key_hot = (key_tile == lax.broadcasted_iota(jnp.int32, (P_SIZE, NT), 1)).astype(F32)
    query_tile = core * (NT // 2) + lax.broadcasted_iota(jnp.int32, (ROWS, NT), 0) // TILE
    query_hot = (query_tile == lax.broadcasted_iota(jnp.int32, (ROWS, NT), 1)).astype(F32)
    rows_mask = mm(query_hot, mask[...].astype(F32), 1, 0)
    bias[...] = jnp.where(mm(key_hot, rows_mask, 1, 1) > 0.5, 0.0, NEG)
    same = (
        lax.broadcasted_iota(jnp.int32, (GROUP, GROUP), 0) % BAND
        == lax.broadcasted_iota(jnp.int32, (GROUP, GROUP), 1) % BAND
    )
    tbias[...] = jnp.where(same, 0.0, NEG)

    def cot_chunk(i, carry):
        part = rows(i * WROWS, WROWS)
        await_bytes(w_s.at[part], ld.at[6 + i])
        c_b[:, part] = mm(w_s[part, :], u_s[own_u, :], 1, 1).T.astype(B16)
        return carry

    lax.fori_loop(0, WCH, cot_chunk, 0)

    await_bytes(q_s, ld.at[5])
    await_bytes(k_s.at[far_k], kv_rs.at[0])
    await_bytes(v_s.at[far_k], kv_rs.at[1])

    def space_forward(h):
        hs = rows(h * HD, HD)
        scores = mm(k_s[:, hs], q_s[:, hs], 1, 1) + bias[...]
        powers = jnp.exp2((scores - jnp.max(scores, axis=0, keepdims=True)) * POWER)
        weights = powers * (1.0 / jnp.sum(powers, axis=0, keepdims=True))
        pw[h] = weights
        a_b[:, hs] = mm(weights.astype(B16), v_s[:, hs], 0, 0).astype(B16)

    def space_group(g, carry):
        for n in range(GH):
            space_forward(g * GH + n)
        spread(a_b, group_cols(g), put_so(g), 3, g)
        return carry

    lax.fori_loop(0, GROUPS, space_group, 0)
    forward(whole, put_tq, 0, 0)
    forward(whole, put_tk, 1, 0)
    spread(c_b, whole, put_oc, 2, 0)

    y_m, y_p = (y + 3) % YS, (y + 1) % YS
    await_bytes(u_half(y_m, 0), y_rs.at[0])
    send(u_half(y_m, 0), u_half(y_m, 0), y_ss.at[4], y_rs.at[4], y_up)
    await_bytes(u_half(y_p, 1), y_rs.at[1])
    send(u_half(y_p, 1), u_half(y_p, 1), y_ss.at[5], y_rs.at[5], y_dn)

    await_bytes(tq_r, a2a_rs.at[0])
    await_bytes(tk_r, a2a_rs.at[1])

    def band(ref, h, b):
        hs = rows(h * HD, HD)
        return jnp.concatenate(
            [ref[f * PIX + b * BAND:f * PIX + (b + 1) * BAND, hs] for f in range(FRAMES)], axis=0
        )

    def put_band(ref, h, b, value):
        hs = rows(h * HD, HD)
        for f in range(FRAMES):
            ref[f * PIX + b * BAND:f * PIX + (b + 1) * BAND, hs] = value[f * BAND:(f + 1) * BAND]

    def time_forward(h):
        for b in range(2):
            scores = mm(band(tk_r, h, b), band(tq_r, h, b), 1, 1) + tbias[...]
            powers = jnp.exp2((scores - jnp.max(scores, axis=0, keepdims=True)) * POWER)
            tw[h, b] = powers * (1.0 / jnp.sum(powers, axis=0, keepdims=True))

    def time_group(g, carry):
        for n in range(GH):
            time_forward(g * GH + n)
        return carry

    lax.fori_loop(0, GROUPS, time_group, 0)

    def forward_space(g, carry):
        forward(group_cols(g), put_so(g), 3, g)
        return carry

    lax.fori_loop(0, GROUPS, forward_space, 0)

    await_bytes(b_b, a2a_ss.at[0])
    def apply_group(g, carry):
        await_bytes(so_r.at[:, group_cols(g)], so_rs.at[g])
        for n in range(GH):
            h = g * GH + n
            for b in range(2):
                out = mm(tw[h, b].astype(B16), band(so_r, h, b), 0, 0)
                for f in range(FRAMES):
                    t_f[g, f * PIX + b * BAND:f * PIX + (b + 1) * BAND, n * HD:(n + 1) * HD] = (
                        out[f * BAND:(f + 1) * BAND]
                    )
        return carry

    lax.fori_loop(0, GROUPS, apply_group, 0)
    for k in range(YS):
        block = [
            t_f[g, :, k * OUT_ROWS + part * SUB:k * OUT_ROWS + (part + 1) * SUB]
            for part in range(2)
            for g in range(GROUPS)
        ]
        b_b[:, k * BLOCK:(k + 1) * BLOCK] = jnp.concatenate(block, axis=1).astype(B16)

    spread(b_b, whole, put_out, 7, 0)
    forward(whole, put_oc, 2, 0)

    await_bytes(oc_r, a2a_rs.at[2])
    await_bytes(c_b, a2a_ss.at[2])
    await_bytes(a_b, a2a_ss.at[3])
    await_bytes(d_b, a2a_ss.at[1])

    def time_backward(h):
        for b in range(2):
            weights = tw[h, b]
            cot = band(oc_r, h, b)
            put_band(c_b, h, b, mm(weights.astype(B16), cot, 1, 0).astype(B16))
            prob = mm(band(so_r, h, b), cot, 1, 1)
            centre = jnp.sum(weights * prob, axis=0, keepdims=True)
            grad = (weights * (prob - centre)).astype(B16)
            put_band(a_b, h, b, (mm(grad, band(tk_r, h, b), 0, 0) * SCALE).astype(B16))
            put_band(d_b, h, b, (mm(grad, band(tq_r, h, b), 1, 0) * SCALE).astype(B16))

    def time_back_group(g, carry):
        for n in range(GH):
            time_backward(g * GH + n)
        spread(c_b, group_cols(g), put_sc(g), 4, g)

        @pl.when(g == 0)
        def _():
            forward(whole, put_out, 7, 0)

        return carry

    def forward_cot(g, carry):
        forward(group_cols(g), put_sc(g), 4, g)
        return carry

    lax.fori_loop(0, GROUPS, time_back_group, 0)
    spread(a_b, whole, put_tqg, 5, 0)
    lax.fori_loop(0, 2, forward_cot, 0)

    await_bytes(b_b, a2a_ss.at[7])

    def space_backward(h):
        hs = rows(h * HD, HD)
        weights = pw[h]
        cot = sc_r[:, hs]
        key = k_s[:, hs]
        prob = mm(v_s[:, hs], cot, 1, 1)
        centre = jnp.sum(weights * prob, axis=0, keepdims=True)
        grad = (weights * (prob - centre)).astype(B16)
        b_b[:, hs] = (mm(grad, key, 0, 0) * SCALE).astype(B16)
        dk = mm(grad, q_s[:, hs], 1, 0) * SCALE
        dv = mm(weights.astype(B16), cot, 1, 0)
        dk_f[:, hs] = dk[:ROWS]
        dv_f[:, hs] = dv[:ROWS]
        dk_x[:, hs] = dk[ROWS:].astype(B16)
        dv_x[:, hs] = dv[ROWS:].astype(B16)

    def backward_group(g):
        cols = group_cols(g)
        await_bytes(sc_r.at[:, cols], sc_rs.at[g])
        for n in range(GH):
            space_backward(g * GH + n)
        send(dk_x.at[:, cols], dk_r.at[:, cols], x_ss, x_rs.at[0, g], other)
        send(dv_x.at[:, cols], dv_r.at[:, cols], x_ss, x_rs.at[1, g], other)

    await_bytes(t_r, t_rs)
    tt[...] = t_r[...].T
    await_bytes(u_half(y_m, 1), y_rs.at[3])
    await_bytes(u_half(y_p, 0), y_rs.at[2])
    y_f = (y + 2) % YS
    await_bytes(u_half(y_f, 0), y_rs.at[4])
    await_bytes(u_half(y_f, 1), y_rs.at[5])

    z = zh * 2 + zl

    def chip(k):
        zd = (z + k) % 4
        return zd // 2, zd % 2

    def weight_part(k):
        zd = (z + k) % 4
        part = mm(tt[...], u_s[:, rows(zd * 2 * COLS, 2 * COLS)], 1, 0)
        wgf[k, 0] = part[:, :COLS]
        wgf[k, 1] = part[:, COLS:]

    def pair_sum(k, along_z):
        await_bytes(crecv.at[k], c_rs.at[k])
        rsend[k] = (wgf[k, core] + crecv[k].astype(F32)).astype(B16)
        for step in range(1, 4):
            xd = (x + step) % 4
            send(rsend.at[k, rows(xd * SUB, SUB)], ra.at[x, k], r_ss.at[0], r_rs.at[0], dev(xd, y, zh, zl, core))
        if along_z:
            zhd, zld = chip(k)
            send(rsend.at[k, pl.ds(SIDE, SIDE)], rb.at[z], r_ss.at[1], r_rs.at[1], dev(x, y, zhd, zld, core))

    def weight_step(n, carry):
        k = (n + 1) % 4
        weight_part(k)
        csend[k] = wgf[k, 1 - core].astype(B16)
        send(csend.at[k], crecv.at[k], c_ss, c_rs.at[k], other)

        @pl.when(n > 0)
        def _():
            pair_sum(n, True)

        return carry

    lax.fori_loop(0, 4, weight_step, 0)
    pair_sum(0, False)
    spread(d_b, whole, put_tkg, 6, 0)
    lax.fori_loop(2, GROUPS, forward_cot, 0)

    def first_stage():
        for k in range(4):
            ra[x, k] = rsend[k, rows(x * SUB, SUB)]
        rb[z] = rsend[0, SIDE:]
        await_bytes(ra.at[pl.ds(0, 3)], r_rs.at[0])
        for k in range(4):
            total = ra[0, k].astype(F32)
            for n in range(1, 4):
                total = total + ra[n, k].astype(F32)
            sa[k] = total.astype(B16)
            if k > 0:
                zhd, zld = chip(k)
                send(sa.at[k], ra2.at[z], r_ss.at[2], r_rs.at[2], dev(x, y, zhd, zld, core))
        ra2[z] = sa[0]
        await_bytes(rb.at[pl.ds(0, 3)], r_rs.at[1])
        total = rb[0].astype(F32)
        for n in range(1, 4):
            total = total + rb[n].astype(F32)
        sb[...] = total.astype(B16)
        for step in range(1, 4):
            xd = (x + step) % 4
            send(sb.at[rows(xd * SUB, SUB)], rb2.at[x], r_ss.at[3], r_rs.at[3], dev(xd, y, zh, zl, core))
        rb2[x] = sb[rows(x * SUB, SUB)]

    out_cols = rows((z * 2 + core) * COLS, COLS)
    zh_own, core_own = y // 2, y % 2

    def second_stage():
        for part, (held, n) in enumerate(((ra2, 2), (rb2, 3))):
            await_bytes(held.at[pl.ds(0, 3)], r_rs.at[n])
            total = held[0].astype(F32)
            for k in range(1, 4):
                total = total + held[k].astype(F32)
            red[part * SUB:(part + 1) * SUB] = total.astype(B16)
        for k in range(8):
            yd, zld = (y + k // 2) % YS, (zl + k) % 2
            mine = (yd == y) & (zh_own == zh) & (zld == zl) & (core_own == core)

            @pl.when(mine)
            def _():
                local(red, g_r.at[:, out_cols], g_rs)

            @pl.when(jnp.logical_not(mine))
            def _():
                send(red, g_r.at[:, out_cols], g_ss.at[k], g_rs, dev(x, yd, zh_own, zld, core_own))

    def backward_step(g, carry):
        backward_group(g)

        @pl.when(g == 0)
        def _():
            first_stage()

        @pl.when(g == 1)
        def _():
            second_stage()
            forward(whole, put_tqg, 5, 0)
            forward(whole, put_tkg, 6, 0)

        return carry

    lax.fori_loop(0, GROUPS, backward_step, 0)

    local(b_b, sqg_o.at[0], out_s.at[0])
    for g in range(GROUPS):
        cols = group_cols(g)
        await_bytes(dk_r.at[:, cols], x_rs.at[0, g])
        await_bytes(dv_r.at[:, cols], x_rs.at[1, g])
    await_bytes(dk_x, x_ss)
    await_bytes(dv_x, x_ss)
    dk_x[...] = (dk_f[...] + dk_r[...].astype(F32)).astype(B16)
    local(dk_x, skg_o.at[0], out_s.at[1])
    dv_x[...] = (dv_f[...] + dv_r[...].astype(F32)).astype(B16)
    local(dv_x, svg_o.at[0], out_s.at[2])

    await_bytes(tqg_r, a2a_rs.at[5])
    local(tqg_r, tqg_o.at[0], out_s.at[3])
    await_bytes(tkg_r, a2a_rs.at[6])
    local(tkg_r, tkg_o.at[0], out_s.at[4])

    await_bytes(k_s.at[own_k], kv_ss.at[0])
    await_bytes(v_s.at[own_k], kv_ss.at[1])
    for i, part in enumerate((0, 1, 0, 1, 0, 1)):
        await_bytes(u_half(0, part), y_ss.at[i])
    await_bytes(c_b, a2a_ss.at[4])
    await_bytes(a_b, a2a_ss.at[5])
    await_bytes(d_b, a2a_ss.at[6])
    for unit in range(8):
        await_bytes(hop.at[unit], hop_ss.at[unit])
    await_bytes(csend, c_ss)
    for n, held in enumerate((ra, rb, ra2, rb2)):
        await_bytes(held.at[pl.ds(0, 3)], r_ss.at[n])
    for k in range(8):
        yd, zld = (y + k // 2) % YS, (zl + k) % 2
        mine = (yd == y) & (zh_own == zh) & (zld == zl) & (core_own == core)

        @pl.when(jnp.logical_not(mine))
        def _():
            await_bytes(red, g_ss.at[k])

    await_bytes(g_r, g_rs)
    local(g_r, wg_o, out_s.at[5])
    await_bytes(tqg_r, out_s.at[3])
    await_bytes(tkg_r, out_s.at[4])
    await_bytes(g_r, out_s.at[5])
    await_bytes(b_b, out_s.at[0])
    await_bytes(dk_x, out_s.at[1])
    await_bytes(dv_x, out_s.at[2])


def store(a, b, c, d, e, wg, a_o, b_o, c_o, d_o, e_o, wg_o, held, low, wide, loads, stores):
    ins = [
        pltpu.make_async_copy(src, dst, loads.at[i])
        for i, (src, dst) in enumerate(
            [(wg, low)] + [(r, held.at[pl.ds(k, 1)]) for k, r in enumerate((a, b, c, d, e))]
        )
    ]
    outs = [pltpu.make_async_copy(wide, wg_o, stores.at[0])] + [
        pltpu.make_async_copy(held.at[pl.ds(k, 1)], r, stores.at[k + 1])
        for k, r in enumerate((a_o, b_o, c_o, d_o, e_o))
    ]
    for copy in ins:
        copy.start()
    for k, copy in enumerate(ins):
        copy.wait()
        if k == 0:
            wide[...] = low[...].astype(F32)
        outs[k].start()
    for copy in outs:
        copy.wait()


def local(qs, ks, vs, qt, kt, up, w, mask):
    hbm = pl.BlockSpec(memory_space=pl.ANY)
    vm = pltpu.VMEM
    dma = pltpu.SemaphoreType.DMA
    unit = jax.ShapeDtypeStruct((1, ROWS, HH), B16)
    own = vm((ROWS, HH), B16)
    outs = pl.pallas_call(
        kernel,
        out_shape=(unit,) * 5 + (jax.ShapeDtypeStruct((OUT_ROWS, D), B16),),
        in_specs=[hbm] * 7 + [pl.BlockSpec(memory_space=pltpu.VMEM)],
        out_specs=(hbm,) * 6,
        scratch_shapes=[
            own, vm((P_SIZE, HH), B16), vm((P_SIZE, HH), B16), vm((HH, D), B16),
            vm((YS * ROWS, D), B16), own, own, own, own, own, vm((YS * ROWS, BLOCK), B16),
            own, own, own, own,
            vm((HEADS, P_SIZE, ROWS), F32), vm((HEADS, 2, GROUP, GROUP), F32),
            vm((P_SIZE, ROWS), F32), vm((GROUP, GROUP), F32),
            vm((BLOCK, YS * ROWS), B16), vm((4, 2, BLOCK, COLS), F32),
            vm((4, BLOCK, COLS), B16), vm((4, BLOCK, COLS), B16),
            vm((4, BLOCK, COLS), B16), vm((4, 4, SUB, COLS), B16), vm((4, SIDE, COLS), B16),
            vm((4, SUB, COLS), B16), vm((4, SUB, COLS), B16), vm((4, SUB, COLS), B16),
            vm((SIDE, COLS), B16), vm((OUT_ROWS, COLS), B16),
            vm((ROWS, HH), F32), vm((ROWS, HH), F32), own, own, own, own,
            vm((8, 2 * PIX, HH), B16), vm((GROUPS, ROWS, GC), F32),
            own, own, vm((OUT_ROWS, D), B16),
            dma((6 + WCH,)), dma((2,)), dma((2,)), dma((6,)), dma((6,)), dma((8,)), dma((7,)),
            dma((GROUPS,)), dma((GROUPS,)), dma, dma((8,)), dma((8, GROUPS)), dma, dma((4,)), dma((4,)), dma((4,)),
            dma((8,)), dma, dma, dma((2, GROUPS)), dma((6,)),
        ],
        compiler_params=pltpu.CompilerParams(
            has_side_effects=True, vmem_limit_bytes=62 * 1024 * 1024
        ),
        cost_estimate=pl.CostEstimate(
            flops=8 * 10**9, bytes_accessed=20 * 10**6, transcendentals=3 * 10**6
        ),
    )(qs, ks, vs, qt, kt, up, w, mask)
    return pl.pallas_call(
        store,
        out_shape=(unit,) * 5 + (jax.ShapeDtypeStruct((OUT_ROWS, D), F32),),
        in_specs=[hbm] * 6,
        out_specs=(hbm,) * 6,
        scratch_shapes=[
            vm((5, ROWS, HH), B16), vm((OUT_ROWS, D), B16), vm((OUT_ROWS, D), F32), dma((6,)), dma((6,)),
        ],
        compiler_params=pltpu.CompilerParams(vmem_limit_bytes=62 * 1024 * 1024),
    )(*outs)


def solution(mesh):
    tokens = P("dp", "seq", None)
    return jax.shard_map(
        local,
        mesh=mesh,
        in_specs=(tokens,) * 6 + (P(), P()),
        out_specs=(tokens,) * 5 + (P("seq", None),),
        check_vma=False,
    )
```

```python
import math

import jax
import jax.numpy as jnp
from jax import lax
from jax.experimental import pallas as pl
from jax.experimental.pallas import tpu as pltpu
from jax.sharding import PartitionSpec as P

HEADS = 12
HD = 128
HH = HEADS * HD
D = 3072
ROWS = 256
P_SIZE = 512
TILE = 32
NT = 16
FRAMES = 8
PIX = ROWS // FRAMES
HALF = PIX // 2
YS = 4
BLOCK = HH // YS
COLS = D // 8
OUT_ROWS = 96
SUB = OUT_ROWS // 2
SIDE = BLOCK // 2
GROUPS = 4
GH = HEADS // GROUPS
GC = GH * HD
WCH = 6
WROWS = HH // WCH
SCALE = 1.0 / math.sqrt(HD)
POWER = SCALE / math.log(2.0)
NEG = -1e30
BAND = PIX // 2
GROUP = ROWS // 2
MESH = pl.DeviceIdType.MESH
F32 = jnp.float32
B16 = jnp.bfloat16


def mm(a, b, ca, cb):
    return lax.dot_general(a, b, (((ca,), (cb,)), ((), ())), preferred_element_type=F32)


def kernel(
    qs, ks, vs, qt, kt, up, w, mask,
    sqg_o, skg_o, svg_o, tqg_o, tkg_o, wg_o,
    q_s, k_s, v_s, w_s, u_s, tq_r, tk_r, so_r, oc_r, sc_r, t_r,
    a_b, b_b, c_b, d_b, pw, tw, bias, tbias, tt, wgf, csend, crecv, rsend, ra, rb, ra2, rb2, sa, sb, red,
    dk_f, dv_f, dk_x, dv_x, dk_r, dv_r, hop, t_f, tqg_r, tkg_r, g_r,
    ld, kv_ss, kv_rs, y_ss, y_rs, a2a_ss, a2a_rs, so_rs, sc_rs, t_rs, hop_ss, hop_rs,
    c_ss, c_rs, r_ss, r_rs, g_ss, g_rs, x_ss, x_rs, out_s,
):
    dp = lax.axis_index("dp")
    seq = lax.axis_index("seq")
    y, zl = dp // 2, dp % 2
    x, zh, core = seq // 4, (seq // 2) % 2, seq % 2
    frame = x * 2 + zh

    def dev(x_, y_, zh_, zl_, c_):
        return {"dp": y_ * 2 + zl_, "seq": x_ * 4 + zh_ * 2 + c_}

    def send(src, dst, ss, rs, to):
        pltpu.make_async_remote_copy(
            src_ref=src, dst_ref=dst, send_sem=ss, recv_sem=rs, device_id=to, device_id_type=MESH
        ).start()

    def await_bytes(ref, sem):
        pltpu.make_async_copy(ref, ref, sem).wait()

    def local(src, dst, sem):
        pltpu.make_async_copy(src, dst, sem).start()

    def rows(start, size):
        return pl.ds(pl.multiple_of(start, size), size)

    def spread(src, cols, put, unit, part):
        for zd in range(2):
            for side in range(2):
                far = ((x + 2) % 4 * 2 + zd) * PIX + side * HALF
                send(
                    src.at[rows(far, HALF), cols],
                    hop.at[unit, rows(side * PIX + zh * HALF, HALF), cols],
                    a2a_ss.at[unit], hop_rs.at[unit, part],
                    dev((x + 1 + 2 * side) % 4, y, zd, 1 - zl, core),
                )
        for step in (1, 3, 0):
            xd = (x + step) % 4
            for zd in range(2):
                put(
                    src, rows((xd * 2 + zd) * PIX, PIX), frame * PIX, PIX, a2a_ss.at[unit],
                    xd, zd, 1 - zl,
                )

    def forward(cols, put, unit, part):
        await_bytes(hop.at[unit, :, cols], hop_rs.at[unit, part])
        for side in range(2):
            came = (x + 3 + 2 * side) % 4
            for zs in range(2):
                put(
                    hop.at[unit], pl.ds(side * PIX + zs * HALF, HALF),
                    (came * 2 + zs) * PIX + side * HALF, HALF, hop_ss.at[unit],
                    (x + 1 + 2 * side) % 4, zh, zl,
                )

    def putter(dst, cols, rs):
        def put(src, src_rows, start, size, ss, xd, zd, zld):
            send(
                src.at[src_rows, cols], dst.at[rows(start, size), cols], ss, rs,
                dev(xd, y, zd, zld, core),
            )

        return put

    whole = pl.ds(0, HH)

    def group_cols(g):
        return rows(g * GC, GC)

    put_tq = putter(tq_r, whole, a2a_rs.at[0])
    put_tk = putter(tk_r, whole, a2a_rs.at[1])
    put_oc = putter(oc_r, whole, a2a_rs.at[2])

    def put_so(g):
        return putter(so_r, group_cols(g), so_rs.at[g])

    def put_sc(g):
        return putter(sc_r, group_cols(g), sc_rs.at[g])

    put_tqg = putter(tqg_r, whole, a2a_rs.at[5])
    put_tkg = putter(tkg_r, whole, a2a_rs.at[6])

    def put_out(src, src_rows, start, size, ss, xd, zd, zld):
        for k in range(YS):
            yd = (y + k) % YS
            send(
                src.at[src_rows, rows(yd * BLOCK, BLOCK)], t_r.at[rows(y * ROWS + start, size)],
                ss, t_rs, dev(xd, yd, zd, zld, core),
            )

    other = dev(x, y, zh, zl, 1 - core)
    y_up = dev(x, (y + 1) % YS, zh, zl, core)
    y_dn = dev(x, (y + 3) % YS, zh, zl, core)

    half = ROWS // 2
    own_k, far_k = pl.ds(0, ROWS), pl.ds(ROWS, ROWS)
    own_u = pl.ds(pl.multiple_of(y * ROWS, ROWS), ROWS)

    def u_half(owner, part):
        return u_s.at[pl.ds(pl.multiple_of(owner * ROWS + part * half, half), half)]

    loads = (
        (ks.at[0], k_s.at[own_k]), (vs.at[0], v_s.at[own_k]), (qt.at[0], b_b), (kt.at[0], d_b),
        (up.at[0], u_s.at[own_u]), (qs.at[0], q_s),
    )
    for i, (src, dst) in enumerate(loads):
        local(src, dst, ld.at[i])
    for i in range(WCH):
        local(w.at[pl.ds(i * WROWS, WROWS)], w_s.at[pl.ds(i * WROWS, WROWS)], ld.at[6 + i])

    await_bytes(k_s.at[own_k], ld.at[0])
    send(k_s.at[own_k], k_s.at[far_k], kv_ss.at[0], kv_rs.at[0], other)
    await_bytes(v_s.at[own_k], ld.at[1])
    send(v_s.at[own_k], v_s.at[far_k], kv_ss.at[1], kv_rs.at[1], other)
    await_bytes(b_b, ld.at[2])
    spread(b_b, whole, put_tq, 0, 0)
    await_bytes(u_s.at[own_u], ld.at[4])
    send(u_half(y, 0), u_half(y, 0), y_ss.at[0], y_rs.at[0], y_up)
    send(u_half(y, 1), u_half(y, 1), y_ss.at[1], y_rs.at[1], y_dn)
    await_bytes(d_b, ld.at[3])
    spread(d_b, whole, put_tk, 1, 0)
    send(u_half(y, 0), u_half(y, 0), y_ss.at[2], y_rs.at[2], y_dn)
    send(u_half(y, 1), u_half(y, 1), y_ss.at[3], y_rs.at[3], y_up)

    key_row = lax.broadcasted_iota(jnp.int32, (P_SIZE, NT), 0)
    key_tile = jnp.where(
        key_row < ROWS, core * (NT // 2) + key_row // TILE,
        (1 - core) * (NT // 2) + (key_row - ROWS) // TILE,
    )
    key_hot = (key_tile == lax.broadcasted_iota(jnp.int32, (P_SIZE, NT), 1)).astype(F32)
    query_tile = core * (NT // 2) + lax.broadcasted_iota(jnp.int32, (ROWS, NT), 0) // TILE
    query_hot = (query_tile == lax.broadcasted_iota(jnp.int32, (ROWS, NT), 1)).astype(F32)
    rows_mask = mm(query_hot, mask[...].astype(F32), 1, 0)
    bias[...] = jnp.where(mm(key_hot, rows_mask, 1, 1) > 0.5, 0.0, NEG)
    same = (
        lax.broadcasted_iota(jnp.int32, (GROUP, GROUP), 0) % BAND
        == lax.broadcasted_iota(jnp.int32, (GROUP, GROUP), 1) % BAND
    )
    tbias[...] = jnp.where(same, 0.0, NEG)

    def cot_chunk(i, carry):
        part = rows(i * WROWS, WROWS)
        await_bytes(w_s.at[part], ld.at[6 + i])
        c_b[:, part] = mm(w_s[part, :], u_s[own_u, :], 1, 1).T.astype(B16)
        return carry

    lax.fori_loop(0, WCH, cot_chunk, 0)

    await_bytes(q_s, ld.at[5])
    await_bytes(k_s.at[far_k], kv_rs.at[0])
    await_bytes(v_s.at[far_k], kv_rs.at[1])

    def space_forward(h):
        hs = rows(h * HD, HD)
        scores = mm(k_s[:, hs], q_s[:, hs], 1, 1) + bias[...]
        powers = jnp.exp2((scores - jnp.max(scores, axis=0, keepdims=True)) * POWER)
        weights = powers * (1.0 / jnp.sum(powers, axis=0, keepdims=True))
        pw[h] = weights
        a_b[:, hs] = mm(weights.astype(B16), v_s[:, hs], 0, 0).astype(B16)

    def space_group(g, carry):
        for n in range(GH):
            space_forward(g * GH + n)
        spread(a_b, group_cols(g), put_so(g), 3, g)
        return carry

    lax.fori_loop(0, GROUPS, space_group, 0)
    forward(whole, put_tq, 0, 0)
    forward(whole, put_tk, 1, 0)
    spread(c_b, whole, put_oc, 2, 0)

    await_bytes(tq_r, a2a_rs.at[0])
    await_bytes(tk_r, a2a_rs.at[1])

    def band(ref, h, b):
        hs = rows(h * HD, HD)
        return jnp.concatenate(
            [ref[f * PIX + b * BAND:f * PIX + (b + 1) * BAND, hs] for f in range(FRAMES)], axis=0
        )

    def put_band(ref, h, b, value):
        hs = rows(h * HD, HD)
        for f in range(FRAMES):
            ref[f * PIX + b * BAND:f * PIX + (b + 1) * BAND, hs] = value[f * BAND:(f + 1) * BAND]

    def time_forward(h):
        for b in range(2):
            scores = mm(band(tk_r, h, b), band(tq_r, h, b), 1, 1) + tbias[...]
            powers = jnp.exp2((scores - jnp.max(scores, axis=0, keepdims=True)) * POWER)
            tw[h, b] = powers * (1.0 / jnp.sum(powers, axis=0, keepdims=True))

    def time_group(g, carry):
        for n in range(GH):
            time_forward(g * GH + n)
        return carry

    lax.fori_loop(0, GROUPS, time_group, 0)

    def forward_space(g, carry):
        forward(group_cols(g), put_so(g), 3, g)
        return carry

    lax.fori_loop(0, GROUPS, forward_space, 0)

    y_m, y_p = (y + 3) % YS, (y + 1) % YS
    await_bytes(u_half(y_m, 0), y_rs.at[0])
    send(u_half(y_m, 0), u_half(y_m, 0), y_ss.at[4], y_rs.at[4], y_up)
    await_bytes(u_half(y_p, 1), y_rs.at[1])
    send(u_half(y_p, 1), u_half(y_p, 1), y_ss.at[5], y_rs.at[5], y_dn)

    await_bytes(b_b, a2a_ss.at[0])
    def apply_group(g, carry):
        await_bytes(so_r.at[:, group_cols(g)], so_rs.at[g])
        for n in range(GH):
            h = g * GH + n
            for b in range(2):
                out = mm(tw[h, b].astype(B16), band(so_r, h, b), 0, 0)
                for f in range(FRAMES):
                    t_f[g, f * PIX + b * BAND:f * PIX + (b + 1) * BAND, n * HD:(n + 1) * HD] = (
                        out[f * BAND:(f + 1) * BAND]
                    )
        return carry

    lax.fori_loop(0, GROUPS, apply_group, 0)
    for k in range(YS):
        block = [
            t_f[g, :, k * OUT_ROWS + part * SUB:k * OUT_ROWS + (part + 1) * SUB]
            for part in range(2)
            for g in range(GROUPS)
        ]
        b_b[:, k * BLOCK:(k + 1) * BLOCK] = jnp.concatenate(block, axis=1).astype(B16)

    spread(b_b, whole, put_out, 7, 0)
    forward(whole, put_oc, 2, 0)

    await_bytes(oc_r, a2a_rs.at[2])
    await_bytes(c_b, a2a_ss.at[2])
    await_bytes(a_b, a2a_ss.at[3])
    await_bytes(d_b, a2a_ss.at[1])

    def time_backward(h):
        for b in range(2):
            weights = tw[h, b]
            cot = band(oc_r, h, b)
            put_band(c_b, h, b, mm(weights.astype(B16), cot, 1, 0).astype(B16))
            prob = mm(band(so_r, h, b), cot, 1, 1)
            centre = jnp.sum(weights * prob, axis=0, keepdims=True)
            grad = (weights * (prob - centre)).astype(B16)
            put_band(a_b, h, b, (mm(grad, band(tk_r, h, b), 0, 0) * SCALE).astype(B16))
            put_band(d_b, h, b, (mm(grad, band(tq_r, h, b), 1, 0) * SCALE).astype(B16))

    def time_back_group(g, carry):
        for n in range(GH):
            time_backward(g * GH + n)
        spread(c_b, group_cols(g), put_sc(g), 4, g)

        @pl.when(g == 0)
        def _():
            forward(whole, put_out, 7, 0)

        @pl.when(g > 0)
        def _():
            forward(group_cols(g - 1), put_sc(g - 1), 4, g - 1)

        return carry

    lax.fori_loop(0, GROUPS, time_back_group, 0)
    spread(a_b, whole, put_tqg, 5, 0)

    await_bytes(b_b, a2a_ss.at[7])

    def space_backward(h):
        hs = rows(h * HD, HD)
        weights = pw[h]
        cot = sc_r[:, hs]
        key = k_s[:, hs]
        prob = mm(v_s[:, hs], cot, 1, 1)
        centre = jnp.sum(weights * prob, axis=0, keepdims=True)
        grad = (weights * (prob - centre)).astype(B16)
        b_b[:, hs] = (mm(grad, key, 0, 0) * SCALE).astype(B16)
        dk = mm(grad, q_s[:, hs], 1, 0) * SCALE
        dv = mm(weights.astype(B16), cot, 1, 0)
        dk_f[:, hs] = dk[:ROWS]
        dv_f[:, hs] = dv[:ROWS]
        dk_x[:, hs] = dk[ROWS:].astype(B16)
        dv_x[:, hs] = dv[ROWS:].astype(B16)

    def backward_group(g):
        cols = group_cols(g)
        await_bytes(sc_r.at[:, cols], sc_rs.at[g])
        for n in range(GH):
            space_backward(g * GH + n)
        send(dk_x.at[:, cols], dk_r.at[:, cols], x_ss, x_rs.at[0, g], other)
        send(dv_x.at[:, cols], dv_r.at[:, cols], x_ss, x_rs.at[1, g], other)

    def backward_step(g, carry):
        backward_group(g)
        return carry

    forward(group_cols(GROUPS - 1), put_sc(GROUPS - 1), 4, GROUPS - 1)
    lax.fori_loop(0, 2, backward_step, 0)
    spread(d_b, whole, put_tkg, 6, 0)

    await_bytes(t_r, t_rs)
    tt[...] = t_r[...].T
    await_bytes(u_half(y_m, 1), y_rs.at[3])
    await_bytes(u_half(y_p, 0), y_rs.at[2])
    y_f = (y + 2) % YS
    await_bytes(u_half(y_f, 0), y_rs.at[4])
    await_bytes(u_half(y_f, 1), y_rs.at[5])

    z = zh * 2 + zl

    def chip(k):
        zd = (z + k) % 4
        return zd // 2, zd % 2

    def weight_part(k):
        zd = (z + k) % 4
        part = mm(tt[...], u_s[:, rows(zd * 2 * COLS, 2 * COLS)], 1, 0)
        wgf[k, 0] = part[:, :COLS]
        wgf[k, 1] = part[:, COLS:]

    def pair_sum(k, along_z):
        await_bytes(crecv.at[k], c_rs.at[k])
        rsend[k] = (wgf[k, core] + crecv[k].astype(F32)).astype(B16)
        for step in range(1, 4):
            xd = (x + step) % 4
            send(rsend.at[k, rows(xd * SUB, SUB)], ra.at[x, k], r_ss.at[0], r_rs.at[0], dev(xd, y, zh, zl, core))
        if along_z:
            zhd, zld = chip(k)
            send(rsend.at[k, pl.ds(SIDE, SIDE)], rb.at[z], r_ss.at[1], r_rs.at[1], dev(x, y, zhd, zld, core))

    def weight_step(n, carry):
        k = (n + 1) % 4
        weight_part(k)
        csend[k] = wgf[k, 1 - core].astype(B16)
        send(csend.at[k], crecv.at[k], c_ss, c_rs.at[k], other)

        @pl.when(n > 0)
        def _():
            pair_sum(n, True)

        return carry

    lax.fori_loop(0, 4, weight_step, 0)
    pair_sum(0, False)

    def first_stage():
        for k in range(4):
            ra[x, k] = rsend[k, rows(x * SUB, SUB)]
        rb[z] = rsend[0, SIDE:]
        await_bytes(ra.at[pl.ds(0, 3)], r_rs.at[0])
        for k in range(4):
            total = ra[0, k].astype(F32)
            for n in range(1, 4):
                total = total + ra[n, k].astype(F32)
            sa[k] = total.astype(B16)
            if k > 0:
                zhd, zld = chip(k)
                send(sa.at[k], ra2.at[z], r_ss.at[2], r_rs.at[2], dev(x, y, zhd, zld, core))
        ra2[z] = sa[0]
        await_bytes(rb.at[pl.ds(0, 3)], r_rs.at[1])
        total = rb[0].astype(F32)
        for n in range(1, 4):
            total = total + rb[n].astype(F32)
        sb[...] = total.astype(B16)
        for step in range(1, 4):
            xd = (x + step) % 4
            send(sb.at[rows(xd * SUB, SUB)], rb2.at[x], r_ss.at[3], r_rs.at[3], dev(xd, y, zh, zl, core))
        rb2[x] = sb[rows(x * SUB, SUB)]

    out_cols = rows((z * 2 + core) * COLS, COLS)
    zh_own, core_own = y // 2, y % 2

    def second_stage():
        for part, (held, n) in enumerate(((ra2, 2), (rb2, 3))):
            await_bytes(held.at[pl.ds(0, 3)], r_rs.at[n])
            total = held[0].astype(F32)
            for k in range(1, 4):
                total = total + held[k].astype(F32)
            red[part * SUB:(part + 1) * SUB] = total.astype(B16)
        for k in range(8):
            yd, zld = (y + k // 2) % YS, (zl + k) % 2
            mine = (yd == y) & (zh_own == zh) & (zld == zl) & (core_own == core)

            @pl.when(mine)
            def _():
                local(red, g_r.at[:, out_cols], g_rs)

            @pl.when(jnp.logical_not(mine))
            def _():
                send(red, g_r.at[:, out_cols], g_ss.at[k], g_rs, dev(x, yd, zh_own, zld, core_own))

    first_stage()
    second_stage()
    forward(whole, put_tqg, 5, 0)
    forward(whole, put_tkg, 6, 0)
    lax.fori_loop(2, GROUPS, backward_step, 0)

    local(b_b, sqg_o.at[0], out_s.at[0])
    for g in range(GROUPS):
        cols = group_cols(g)
        await_bytes(dk_r.at[:, cols], x_rs.at[0, g])
        await_bytes(dv_r.at[:, cols], x_rs.at[1, g])
    await_bytes(dk_x, x_ss)
    await_bytes(dv_x, x_ss)
    dk_x[...] = (dk_f[...] + dk_r[...].astype(F32)).astype(B16)
    local(dk_x, skg_o.at[0], out_s.at[1])
    dv_x[...] = (dv_f[...] + dv_r[...].astype(F32)).astype(B16)
    local(dv_x, svg_o.at[0], out_s.at[2])

    await_bytes(tqg_r, a2a_rs.at[5])
    local(tqg_r, tqg_o.at[0], out_s.at[3])
    await_bytes(tkg_r, a2a_rs.at[6])
    local(tkg_r, tkg_o.at[0], out_s.at[4])

    await_bytes(k_s.at[own_k], kv_ss.at[0])
    await_bytes(v_s.at[own_k], kv_ss.at[1])
    for i in range(6):
        await_bytes(u_half(0, 0), y_ss.at[i])
    await_bytes(c_b, a2a_ss.at[4])
    await_bytes(a_b, a2a_ss.at[5])
    await_bytes(d_b, a2a_ss.at[6])
    for unit in range(8):
        await_bytes(hop.at[unit], hop_ss.at[unit])
    await_bytes(csend, c_ss)
    for n, held in enumerate((ra, rb, ra2, rb2)):
        await_bytes(held.at[pl.ds(0, 3)], r_ss.at[n])
    for k in range(8):
        yd, zld = (y + k // 2) % YS, (zl + k) % 2
        mine = (yd == y) & (zh_own == zh) & (zld == zl) & (core_own == core)

        @pl.when(jnp.logical_not(mine))
        def _():
            await_bytes(red, g_ss.at[k])

    await_bytes(g_r, g_rs)
    local(g_r, wg_o, out_s.at[5])
    await_bytes(tqg_r, out_s.at[3])
    await_bytes(tkg_r, out_s.at[4])
    await_bytes(g_r, out_s.at[5])
    await_bytes(b_b, out_s.at[0])
    await_bytes(dk_x, out_s.at[1])
    await_bytes(dv_x, out_s.at[2])


def store(a, b, c, d, e, wg, a_o, b_o, c_o, d_o, e_o, wg_o, held, low, wide, loads, stores):
    ins = [
        pltpu.make_async_copy(src, dst, loads.at[i])
        for i, (src, dst) in enumerate(
            [(wg, low)] + [(r, held.at[pl.ds(k, 1)]) for k, r in enumerate((a, b, c, d, e))]
        )
    ]
    outs = [pltpu.make_async_copy(wide, wg_o, stores.at[0])] + [
        pltpu.make_async_copy(held.at[pl.ds(k, 1)], r, stores.at[k + 1])
        for k, r in enumerate((a_o, b_o, c_o, d_o, e_o))
    ]
    for copy in ins:
        copy.start()
    for k, copy in enumerate(ins):
        copy.wait()
        if k == 0:
            wide[...] = low[...].astype(F32)
        outs[k].start()
    for copy in outs:
        copy.wait()


def local(qs, ks, vs, qt, kt, up, w, mask):
    hbm = pl.BlockSpec(memory_space=pl.ANY)
    vm = pltpu.VMEM
    dma = pltpu.SemaphoreType.DMA
    unit = jax.ShapeDtypeStruct((1, ROWS, HH), B16)
    own = vm((ROWS, HH), B16)
    outs = pl.pallas_call(
        kernel,
        out_shape=(unit,) * 5 + (jax.ShapeDtypeStruct((OUT_ROWS, D), B16),),
        in_specs=[hbm] * 7 + [pl.BlockSpec(memory_space=pltpu.VMEM)],
        out_specs=(hbm,) * 6,
        scratch_shapes=[
            own, vm((P_SIZE, HH), B16), vm((P_SIZE, HH), B16), vm((HH, D), B16),
            vm((YS * ROWS, D), B16), own, own, own, own, own, vm((YS * ROWS, BLOCK), B16),
            own, own, own, own,
            vm((HEADS, P_SIZE, ROWS), F32), vm((HEADS, 2, GROUP, GROUP), F32),
            vm((P_SIZE, ROWS), F32), vm((GROUP, GROUP), F32),
            vm((BLOCK, YS * ROWS), B16), vm((4, 2, BLOCK, COLS), F32),
            vm((4, BLOCK, COLS), B16), vm((4, BLOCK, COLS), B16),
            vm((4, BLOCK, COLS), B16), vm((4, 4, SUB, COLS), B16), vm((4, SIDE, COLS), B16),
            vm((4, SUB, COLS), B16), vm((4, SUB, COLS), B16), vm((4, SUB, COLS), B16),
            vm((SIDE, COLS), B16), vm((OUT_ROWS, COLS), B16),
            vm((ROWS, HH), F32), vm((ROWS, HH), F32), own, own, own, own,
            vm((8, 2 * PIX, HH), B16), vm((GROUPS, ROWS, GC), F32),
            own, own, vm((OUT_ROWS, D), B16),
            dma((6 + WCH,)), dma((2,)), dma((2,)), dma((6,)), dma((6,)), dma((8,)), dma((7,)),
            dma((GROUPS,)), dma((GROUPS,)), dma, dma((8,)), dma((8, GROUPS)), dma, dma((4,)), dma((4,)), dma((4,)),
            dma((8,)), dma, dma, dma((2, GROUPS)), dma((6,)),
        ],
        compiler_params=pltpu.CompilerParams(
            has_side_effects=True, vmem_limit_bytes=62 * 1024 * 1024
        ),
        cost_estimate=pl.CostEstimate(
            flops=8 * 10**9, bytes_accessed=20 * 10**6, transcendentals=3 * 10**6
        ),
    )(qs, ks, vs, qt, kt, up, w, mask)
    return pl.pallas_call(
        store,
        out_shape=(unit,) * 5 + (jax.ShapeDtypeStruct((OUT_ROWS, D), F32),),
        in_specs=[hbm] * 6,
        out_specs=(hbm,) * 6,
        scratch_shapes=[
            vm((5, ROWS, HH), B16), vm((OUT_ROWS, D), B16), vm((OUT_ROWS, D), F32), dma((6,)), dma((6,)),
        ],
        compiler_params=pltpu.CompilerParams(vmem_limit_bytes=62 * 1024 * 1024),
    )(*outs)


def solution(mesh):
    tokens = P("dp", "seq", None)
    return jax.shard_map(
        local,
        mesh=mesh,
        in_specs=(tokens,) * 6 + (P(), P()),
        out_specs=(tokens,) * 5 + (P("seq", None),),
        check_vma=False,
    )
```

```python
import math

import jax
import jax.numpy as jnp
from jax import lax
from jax.experimental import pallas as pl
from jax.experimental.pallas import tpu as pltpu
from jax.sharding import PartitionSpec as P

HEADS = 12
HD = 128
HH = HEADS * HD
D = 3072
ROWS = 256
P_SIZE = 512
TILE = 32
NT = 16
FRAMES = 8
PIX = ROWS // FRAMES
HALF = PIX // 2
YS = 4
BLOCK = HH // YS
COLS = D // 8
OUT_ROWS = 96
SUB = OUT_ROWS // 2
SIDE = BLOCK // 2
GROUPS = 4
GH = HEADS // GROUPS
GC = GH * HD
WCH = 6
WROWS = HH // WCH
SCALE = 1.0 / math.sqrt(HD)
POWER = SCALE / math.log(2.0)
NEG = -1e30
BAND = PIX // 2
GROUP = ROWS // 2
MESH = pl.DeviceIdType.MESH
F32 = jnp.float32
B16 = jnp.bfloat16


def mm(a, b, ca, cb):
    return lax.dot_general(a, b, (((ca,), (cb,)), ((), ())), preferred_element_type=F32)


def kernel(
    qs, ks, vs, qt, kt, up, w, mask,
    sqg_o, skg_o, svg_o, tqg_o, tkg_o, wg_o,
    q_s, k_s, v_s, w_s, u_s, tq_r, tk_r, so_r, oc_r, sc_r, t_r,
    a_b, b_b, c_b, d_b, pw, tw, bias, tbias, tt, wgf, csend, crecv, rsend, ra, rb, ra2, rb2, sa, sb, red,
    dk_f, dv_f, dk_x, dv_x, dk_r, dv_r, hop, t_f, tqg_r, tkg_r, g_r,
    ld, kv_ss, kv_rs, y_ss, y_rs, a2a_ss, a2a_rs, so_rs, sc_rs, t_rs, hop_ss, hop_rs,
    c_ss, c_rs, r_ss, r_rs, g_ss, g_rs, x_ss, x_rs, out_s,
):
    dp = lax.axis_index("dp")
    seq = lax.axis_index("seq")
    y, zl = dp // 2, dp % 2
    x, zh, core = seq // 4, (seq // 2) % 2, seq % 2
    frame = x * 2 + zh

    def dev(x_, y_, zh_, zl_, c_):
        return {"dp": y_ * 2 + zl_, "seq": x_ * 4 + zh_ * 2 + c_}

    def send(src, dst, ss, rs, to):
        pltpu.make_async_remote_copy(
            src_ref=src, dst_ref=dst, send_sem=ss, recv_sem=rs, device_id=to, device_id_type=MESH
        ).start()

    def await_bytes(ref, sem):
        pltpu.make_async_copy(ref, ref, sem).wait()

    def local(src, dst, sem):
        pltpu.make_async_copy(src, dst, sem).start()

    def rows(start, size):
        return pl.ds(pl.multiple_of(start, size), size)

    def spread(src, cols, put, unit, part):
        for zd in range(2):
            for side in range(2):
                far = ((x + 2) % 4 * 2 + zd) * PIX + side * HALF
                send(
                    src.at[rows(far, HALF), cols],
                    hop.at[unit, rows(side * PIX + zh * HALF, HALF), cols],
                    a2a_ss.at[unit], hop_rs.at[unit, part],
                    dev((x + 1 + 2 * side) % 4, y, zd, 1 - zl, core),
                )
        for step, turn in ((1, 0), (3, 1), (0, 0), (1, 1), (3, 0), (0, 1)):
            xd, zd = (x + step) % 4, (zh + turn) % 2
            put(
                src, rows((xd * 2 + zd) * PIX, PIX), frame * PIX, PIX, a2a_ss.at[unit],
                xd, zd, 1 - zl,
            )

    def forward(cols, put, unit, part):
        await_bytes(hop.at[unit, :, cols], hop_rs.at[unit, part])
        for side in range(2):
            came = (x + 3 + 2 * side) % 4
            for zs in range(2):
                put(
                    hop.at[unit], pl.ds(side * PIX + zs * HALF, HALF),
                    (came * 2 + zs) * PIX + side * HALF, HALF, hop_ss.at[unit],
                    (x + 1 + 2 * side) % 4, zh, zl,
                )

    def putter(dst, cols, rs):
        def put(src, src_rows, start, size, ss, xd, zd, zld):
            send(
                src.at[src_rows, cols], dst.at[rows(start, size), cols], ss, rs,
                dev(xd, y, zd, zld, core),
            )

        return put

    whole = pl.ds(0, HH)

    def group_cols(g):
        return rows(g * GC, GC)

    put_tq = putter(tq_r, whole, a2a_rs.at[0])
    put_tk = putter(tk_r, whole, a2a_rs.at[1])
    put_oc = putter(oc_r, whole, a2a_rs.at[2])

    def put_so(g):
        return putter(so_r, group_cols(g), so_rs.at[g])

    def put_sc(g):
        return putter(sc_r, group_cols(g), sc_rs.at[g])

    put_tqg = putter(tqg_r, whole, a2a_rs.at[5])
    put_tkg = putter(tkg_r, whole, a2a_rs.at[6])

    def put_out(src, src_rows, start, size, ss, xd, zd, zld):
        for k in range(YS):
            yd = (y + k) % YS
            send(
                src.at[src_rows, rows(yd * BLOCK, BLOCK)], t_r.at[rows(y * ROWS + start, size)],
                ss, t_rs, dev(xd, yd, zd, zld, core),
            )

    other = dev(x, y, zh, zl, 1 - core)
    y_up = dev(x, (y + 1) % YS, zh, zl, core)
    y_dn = dev(x, (y + 3) % YS, zh, zl, core)

    half = ROWS // 2
    own_k, far_k = pl.ds(0, ROWS), pl.ds(ROWS, ROWS)
    own_u = pl.ds(pl.multiple_of(y * ROWS, ROWS), ROWS)

    def u_half(owner, part):
        return u_s.at[pl.ds(pl.multiple_of(owner * ROWS + part * half, half), half)]

    loads = (
        (ks.at[0], k_s.at[own_k]), (vs.at[0], v_s.at[own_k]), (qt.at[0], b_b), (kt.at[0], d_b),
        (up.at[0], u_s.at[own_u]), (qs.at[0], q_s),
    )
    for i, (src, dst) in enumerate(loads):
        local(src, dst, ld.at[i])
    for i in range(WCH):
        local(w.at[pl.ds(i * WROWS, WROWS)], w_s.at[pl.ds(i * WROWS, WROWS)], ld.at[6 + i])

    await_bytes(k_s.at[own_k], ld.at[0])
    send(k_s.at[own_k], k_s.at[far_k], kv_ss.at[0], kv_rs.at[0], other)
    await_bytes(v_s.at[own_k], ld.at[1])
    send(v_s.at[own_k], v_s.at[far_k], kv_ss.at[1], kv_rs.at[1], other)
    await_bytes(b_b, ld.at[2])
    spread(b_b, whole, put_tq, 0, 0)
    await_bytes(u_s.at[own_u], ld.at[4])
    send(u_half(y, 0), u_half(y, 0), y_ss.at[0], y_rs.at[0], y_up)
    send(u_half(y, 1), u_half(y, 1), y_ss.at[1], y_rs.at[1], y_dn)
    await_bytes(d_b, ld.at[3])
    spread(d_b, whole, put_tk, 1, 0)
    send(u_half(y, 0), u_half(y, 0), y_ss.at[2], y_rs.at[2], y_dn)
    send(u_half(y, 1), u_half(y, 1), y_ss.at[3], y_rs.at[3], y_up)

    key_row = lax.broadcasted_iota(jnp.int32, (P_SIZE, NT), 0)
    key_tile = jnp.where(
        key_row < ROWS, core * (NT // 2) + key_row // TILE,
        (1 - core) * (NT // 2) + (key_row - ROWS) // TILE,
    )
    key_hot = (key_tile == lax.broadcasted_iota(jnp.int32, (P_SIZE, NT), 1)).astype(F32)
    query_tile = core * (NT // 2) + lax.broadcasted_iota(jnp.int32, (ROWS, NT), 0) // TILE
    query_hot = (query_tile == lax.broadcasted_iota(jnp.int32, (ROWS, NT), 1)).astype(F32)
    rows_mask = mm(query_hot, mask[...].astype(F32), 1, 0)
    bias[...] = jnp.where(mm(key_hot, rows_mask, 1, 1) > 0.5, 0.0, NEG)
    same = (
        lax.broadcasted_iota(jnp.int32, (GROUP, GROUP), 0) % BAND
        == lax.broadcasted_iota(jnp.int32, (GROUP, GROUP), 1) % BAND
    )
    tbias[...] = jnp.where(same, 0.0, NEG)

    def cot_chunk(i, carry):
        part = rows(i * WROWS, WROWS)
        await_bytes(w_s.at[part], ld.at[6 + i])
        c_b[:, part] = mm(w_s[part, :], u_s[own_u, :], 1, 1).T.astype(B16)
        return carry

    lax.fori_loop(0, WCH, cot_chunk, 0)

    await_bytes(q_s, ld.at[5])
    await_bytes(k_s.at[far_k], kv_rs.at[0])
    await_bytes(v_s.at[far_k], kv_rs.at[1])

    def space_forward(h):
        hs = rows(h * HD, HD)
        scores = mm(k_s[:, hs], q_s[:, hs], 1, 1) + bias[...]
        powers = jnp.exp2((scores - jnp.max(scores, axis=0, keepdims=True)) * POWER)
        weights = powers * (1.0 / jnp.sum(powers, axis=0, keepdims=True))
        pw[h] = weights
        a_b[:, hs] = mm(weights.astype(B16), v_s[:, hs], 0, 0).astype(B16)

    def space_group(g, carry):
        for n in range(GH):
            space_forward(g * GH + n)
        spread(a_b, group_cols(g), put_so(g), 3, g)
        return carry

    lax.fori_loop(0, GROUPS, space_group, 0)
    forward(whole, put_tq, 0, 0)
    forward(whole, put_tk, 1, 0)
    spread(c_b, whole, put_oc, 2, 0)

    await_bytes(tq_r, a2a_rs.at[0])
    await_bytes(tk_r, a2a_rs.at[1])

    def band(ref, h, b):
        hs = rows(h * HD, HD)
        return jnp.concatenate(
            [ref[f * PIX + b * BAND:f * PIX + (b + 1) * BAND, hs] for f in range(FRAMES)], axis=0
        )

    def put_band(ref, h, b, value):
        hs = rows(h * HD, HD)
        for f in range(FRAMES):
            ref[f * PIX + b * BAND:f * PIX + (b + 1) * BAND, hs] = value[f * BAND:(f + 1) * BAND]

    def time_forward(h):
        for b in range(2):
            scores = mm(band(tk_r, h, b), band(tq_r, h, b), 1, 1) + tbias[...]
            powers = jnp.exp2((scores - jnp.max(scores, axis=0, keepdims=True)) * POWER)
            tw[h, b] = powers * (1.0 / jnp.sum(powers, axis=0, keepdims=True))

    def time_group(g, carry):
        for n in range(GH):
            time_forward(g * GH + n)
        return carry

    lax.fori_loop(0, GROUPS, time_group, 0)

    def forward_space(g, carry):
        forward(group_cols(g), put_so(g), 3, g)
        return carry

    lax.fori_loop(0, GROUPS, forward_space, 0)

    y_m, y_p = (y + 3) % YS, (y + 1) % YS
    await_bytes(u_half(y_m, 0), y_rs.at[0])
    send(u_half(y_m, 0), u_half(y_m, 0), y_ss.at[4], y_rs.at[4], y_up)
    await_bytes(u_half(y_p, 1), y_rs.at[1])
    send(u_half(y_p, 1), u_half(y_p, 1), y_ss.at[5], y_rs.at[5], y_dn)

    await_bytes(b_b, a2a_ss.at[0])
    def apply_group(g, carry):
        await_bytes(so_r.at[:, group_cols(g)], so_rs.at[g])
        for n in range(GH):
            h = g * GH + n
            for b in range(2):
                out = mm(tw[h, b].astype(B16), band(so_r, h, b), 0, 0)
                for f in range(FRAMES):
                    t_f[g, f * PIX + b * BAND:f * PIX + (b + 1) * BAND, n * HD:(n + 1) * HD] = (
                        out[f * BAND:(f + 1) * BAND]
                    )
        return carry

    lax.fori_loop(0, GROUPS, apply_group, 0)
    for k in range(YS):
        block = [
            t_f[g, :, k * OUT_ROWS + part * SUB:k * OUT_ROWS + (part + 1) * SUB]
            for part in range(2)
            for g in range(GROUPS)
        ]
        b_b[:, k * BLOCK:(k + 1) * BLOCK] = jnp.concatenate(block, axis=1).astype(B16)

    spread(b_b, whole, put_out, 7, 0)
    forward(whole, put_oc, 2, 0)

    await_bytes(oc_r, a2a_rs.at[2])
    await_bytes(c_b, a2a_ss.at[2])
    await_bytes(a_b, a2a_ss.at[3])
    await_bytes(d_b, a2a_ss.at[1])

    def time_backward(h):
        for b in range(2):
            weights = tw[h, b]
            cot = band(oc_r, h, b)
            put_band(c_b, h, b, mm(weights.astype(B16), cot, 1, 0).astype(B16))
            prob = mm(band(so_r, h, b), cot, 1, 1)
            centre = jnp.sum(weights * prob, axis=0, keepdims=True)
            grad = (weights * (prob - centre)).astype(B16)
            put_band(a_b, h, b, (mm(grad, band(tk_r, h, b), 0, 0) * SCALE).astype(B16))
            put_band(d_b, h, b, (mm(grad, band(tq_r, h, b), 1, 0) * SCALE).astype(B16))

    def time_back_group(g, carry):
        for n in range(GH):
            time_backward(g * GH + n)
        spread(c_b, group_cols(g), put_sc(g), 4, g)

        @pl.when(g == 0)
        def _():
            forward(whole, put_out, 7, 0)

        @pl.when(g > 0)
        def _():
            forward(group_cols(g - 1), put_sc(g - 1), 4, g - 1)

        return carry

    lax.fori_loop(0, GROUPS, time_back_group, 0)
    spread(a_b, whole, put_tqg, 5, 0)

    await_bytes(b_b, a2a_ss.at[7])

    def space_backward(h):
        hs = rows(h * HD, HD)
        weights = pw[h]
        cot = sc_r[:, hs]
        key = k_s[:, hs]
        prob = mm(v_s[:, hs], cot, 1, 1)
        centre = jnp.sum(weights * prob, axis=0, keepdims=True)
        grad = (weights * (prob - centre)).astype(B16)
        b_b[:, hs] = (mm(grad, key, 0, 0) * SCALE).astype(B16)
        dk = mm(grad, q_s[:, hs], 1, 0) * SCALE
        dv = mm(weights.astype(B16), cot, 1, 0)
        dk_f[:, hs] = dk[:ROWS]
        dv_f[:, hs] = dv[:ROWS]
        dk_x[:, hs] = dk[ROWS:].astype(B16)
        dv_x[:, hs] = dv[ROWS:].astype(B16)

    def backward_group(g):
        cols = group_cols(g)
        await_bytes(sc_r.at[:, cols], sc_rs.at[g])
        for n in range(GH):
            space_backward(g * GH + n)
        send(dk_x.at[:, cols], dk_r.at[:, cols], x_ss, x_rs.at[0, g], other)
        send(dv_x.at[:, cols], dv_r.at[:, cols], x_ss, x_rs.at[1, g], other)

    def backward_step(g, carry):
        backward_group(g)
        return carry

    forward(group_cols(GROUPS - 1), put_sc(GROUPS - 1), 4, GROUPS - 1)
    lax.fori_loop(0, 2, backward_step, 0)
    spread(d_b, whole, put_tkg, 6, 0)

    await_bytes(t_r, t_rs)
    tt[...] = t_r[...].T
    await_bytes(u_half(y_m, 1), y_rs.at[3])
    await_bytes(u_half(y_p, 0), y_rs.at[2])
    y_f = (y + 2) % YS
    await_bytes(u_half(y_f, 0), y_rs.at[4])
    await_bytes(u_half(y_f, 1), y_rs.at[5])

    z = zh * 2 + zl

    def chip(k):
        zd = (z + k) % 4
        return zd // 2, zd % 2

    def weight_part(k):
        zd = (z + k) % 4
        part = mm(tt[...], u_s[:, rows(zd * 2 * COLS, 2 * COLS)], 1, 0)
        wgf[k, 0] = part[:, :COLS]
        wgf[k, 1] = part[:, COLS:]

    def pair_sum(k, along_z):
        await_bytes(crecv.at[k], c_rs.at[k])
        rsend[k] = (wgf[k, core] + crecv[k].astype(F32)).astype(B16)
        for step in range(1, 4):
            xd = (x + step) % 4
            send(rsend.at[k, rows(xd * SUB, SUB)], ra.at[x, k], r_ss.at[0], r_rs.at[0], dev(xd, y, zh, zl, core))
        if along_z:
            zhd, zld = chip(k)
            send(rsend.at[k, pl.ds(SIDE, SIDE)], rb.at[z], r_ss.at[1], r_rs.at[1], dev(x, y, zhd, zld, core))

    def weight_step(n, carry):
        k = (n + 1) % 4
        weight_part(k)
        csend[k] = wgf[k, 1 - core].astype(B16)
        send(csend.at[k], crecv.at[k], c_ss, c_rs.at[k], other)

        @pl.when(n > 0)
        def _():
            pair_sum(n, True)

        return carry

    lax.fori_loop(0, 4, weight_step, 0)
    pair_sum(0, False)

    def first_stage():
        for k in range(4):
            ra[x, k] = rsend[k, rows(x * SUB, SUB)]
        rb[z] = rsend[0, SIDE:]
        await_bytes(ra.at[pl.ds(0, 3)], r_rs.at[0])
        for k in range(4):
            total = ra[0, k].astype(F32)
            for n in range(1, 4):
                total = total + ra[n, k].astype(F32)
            sa[k] = total.astype(B16)
            if k > 0:
                zhd, zld = chip(k)
                send(sa.at[k], ra2.at[z], r_ss.at[2], r_rs.at[2], dev(x, y, zhd, zld, core))
        ra2[z] = sa[0]
        await_bytes(rb.at[pl.ds(0, 3)], r_rs.at[1])
        total = rb[0].astype(F32)
        for n in range(1, 4):
            total = total + rb[n].astype(F32)
        sb[...] = total.astype(B16)
        for step in range(1, 4):
            xd = (x + step) % 4
            send(sb.at[rows(xd * SUB, SUB)], rb2.at[x], r_ss.at[3], r_rs.at[3], dev(xd, y, zh, zl, core))
        rb2[x] = sb[rows(x * SUB, SUB)]

    out_cols = rows((z * 2 + core) * COLS, COLS)
    zh_own, core_own = y // 2, y % 2

    def second_stage():
        for part, (held, n) in enumerate(((ra2, 2), (rb2, 3))):
            await_bytes(held.at[pl.ds(0, 3)], r_rs.at[n])
            total = held[0].astype(F32)
            for k in range(1, 4):
                total = total + held[k].astype(F32)
            red[part * SUB:(part + 1) * SUB] = total.astype(B16)
        for k in range(8):
            yd, zld = (y + k // 2) % YS, (zl + k) % 2
            mine = (yd == y) & (zh_own == zh) & (zld == zl) & (core_own == core)

            @pl.when(mine)
            def _():
                local(red, g_r.at[:, out_cols], g_rs)

            @pl.when(jnp.logical_not(mine))
            def _():
                send(red, g_r.at[:, out_cols], g_ss.at[k], g_rs, dev(x, yd, zh_own, zld, core_own))

    first_stage()
    second_stage()
    forward(whole, put_tqg, 5, 0)
    forward(whole, put_tkg, 6, 0)
    lax.fori_loop(2, GROUPS, backward_step, 0)

    local(b_b, sqg_o.at[0], out_s.at[0])
    for g in range(GROUPS):
        cols = group_cols(g)
        await_bytes(dk_r.at[:, cols], x_rs.at[0, g])
        await_bytes(dv_r.at[:, cols], x_rs.at[1, g])
    await_bytes(dk_x, x_ss)
    await_bytes(dv_x, x_ss)
    dk_x[...] = (dk_f[...] + dk_r[...].astype(F32)).astype(B16)
    local(dk_x, skg_o.at[0], out_s.at[1])
    dv_x[...] = (dv_f[...] + dv_r[...].astype(F32)).astype(B16)
    local(dv_x, svg_o.at[0], out_s.at[2])

    await_bytes(tqg_r, a2a_rs.at[5])
    local(tqg_r, tqg_o.at[0], out_s.at[3])
    await_bytes(tkg_r, a2a_rs.at[6])
    local(tkg_r, tkg_o.at[0], out_s.at[4])

    await_bytes(k_s.at[own_k], kv_ss.at[0])
    await_bytes(v_s.at[own_k], kv_ss.at[1])
    for i in range(6):
        await_bytes(u_half(0, 0), y_ss.at[i])
    await_bytes(c_b, a2a_ss.at[4])
    await_bytes(a_b, a2a_ss.at[5])
    await_bytes(d_b, a2a_ss.at[6])
    for unit in range(8):
        await_bytes(hop.at[unit], hop_ss.at[unit])
    await_bytes(csend, c_ss)
    for n, held in enumerate((ra, rb, ra2, rb2)):
        await_bytes(held.at[pl.ds(0, 3)], r_ss.at[n])
    for k in range(8):
        yd, zld = (y + k // 2) % YS, (zl + k) % 2
        mine = (yd == y) & (zh_own == zh) & (zld == zl) & (core_own == core)

        @pl.when(jnp.logical_not(mine))
        def _():
            await_bytes(red, g_ss.at[k])

    await_bytes(g_r, g_rs)
    local(g_r, wg_o, out_s.at[5])
    await_bytes(tqg_r, out_s.at[3])
    await_bytes(tkg_r, out_s.at[4])
    await_bytes(g_r, out_s.at[5])
    await_bytes(b_b, out_s.at[0])
    await_bytes(dk_x, out_s.at[1])
    await_bytes(dv_x, out_s.at[2])


def store(a, b, c, d, e, wg, a_o, b_o, c_o, d_o, e_o, wg_o, held, low, wide, loads, stores):
    ins = [
        pltpu.make_async_copy(src, dst, loads.at[i])
        for i, (src, dst) in enumerate(
            [(wg, low)] + [(r, held.at[pl.ds(k, 1)]) for k, r in enumerate((a, b, c, d, e))]
        )
    ]
    outs = [pltpu.make_async_copy(wide, wg_o, stores.at[0])] + [
        pltpu.make_async_copy(held.at[pl.ds(k, 1)], r, stores.at[k + 1])
        for k, r in enumerate((a_o, b_o, c_o, d_o, e_o))
    ]
    for copy in ins:
        copy.start()
    for k, copy in enumerate(ins):
        copy.wait()
        if k == 0:
            wide[...] = low[...].astype(F32)
        outs[k].start()
    for copy in outs:
        copy.wait()


def local(qs, ks, vs, qt, kt, up, w, mask):
    hbm = pl.BlockSpec(memory_space=pl.ANY)
    vm = pltpu.VMEM
    dma = pltpu.SemaphoreType.DMA
    unit = jax.ShapeDtypeStruct((1, ROWS, HH), B16)
    own = vm((ROWS, HH), B16)
    outs = pl.pallas_call(
        kernel,
        out_shape=(unit,) * 5 + (jax.ShapeDtypeStruct((OUT_ROWS, D), B16),),
        in_specs=[hbm] * 7 + [pl.BlockSpec(memory_space=pltpu.VMEM)],
        out_specs=(hbm,) * 6,
        scratch_shapes=[
            own, vm((P_SIZE, HH), B16), vm((P_SIZE, HH), B16), vm((HH, D), B16),
            vm((YS * ROWS, D), B16), own, own, own, own, own, vm((YS * ROWS, BLOCK), B16),
            own, own, own, own,
            vm((HEADS, P_SIZE, ROWS), F32), vm((HEADS, 2, GROUP, GROUP), F32),
            vm((P_SIZE, ROWS), F32), vm((GROUP, GROUP), F32),
            vm((BLOCK, YS * ROWS), B16), vm((4, 2, BLOCK, COLS), F32),
            vm((4, BLOCK, COLS), B16), vm((4, BLOCK, COLS), B16),
            vm((4, BLOCK, COLS), B16), vm((4, 4, SUB, COLS), B16), vm((4, SIDE, COLS), B16),
            vm((4, SUB, COLS), B16), vm((4, SUB, COLS), B16), vm((4, SUB, COLS), B16),
            vm((SIDE, COLS), B16), vm((OUT_ROWS, COLS), B16),
            vm((ROWS, HH), F32), vm((ROWS, HH), F32), own, own, own, own,
            vm((8, 2 * PIX, HH), B16), vm((GROUPS, ROWS, GC), F32),
            own, own, vm((OUT_ROWS, D), B16),
            dma((6 + WCH,)), dma((2,)), dma((2,)), dma((6,)), dma((6,)), dma((8,)), dma((7,)),
            dma((GROUPS,)), dma((GROUPS,)), dma, dma((8,)), dma((8, GROUPS)), dma, dma((4,)), dma((4,)), dma((4,)),
            dma((8,)), dma, dma, dma((2, GROUPS)), dma((6,)),
        ],
        compiler_params=pltpu.CompilerParams(
            has_side_effects=True, vmem_limit_bytes=62 * 1024 * 1024
        ),
        cost_estimate=pl.CostEstimate(
            flops=8 * 10**9, bytes_accessed=20 * 10**6, transcendentals=3 * 10**6
        ),
    )(qs, ks, vs, qt, kt, up, w, mask)
    return pl.pallas_call(
        store,
        out_shape=(unit,) * 5 + (jax.ShapeDtypeStruct((OUT_ROWS, D), F32),),
        in_specs=[hbm] * 6,
        out_specs=(hbm,) * 6,
        scratch_shapes=[
            vm((5, ROWS, HH), B16), vm((OUT_ROWS, D), B16), vm((OUT_ROWS, D), F32), dma((6,)), dma((6,)),
        ],
        compiler_params=pltpu.CompilerParams(vmem_limit_bytes=62 * 1024 * 1024),
    )(*outs)


def solution(mesh):
    tokens = P("dp", "seq", None)
    return jax.shard_map(
        local,
        mesh=mesh,
        in_specs=(tokens,) * 6 + (P(), P()),
        out_specs=(tokens,) * 5 + (P("seq", None),),
        check_vma=False,
    )
```
